32 devices in a mesh: batch: 8 (over z, y), wide: 4 (over x, core).
Axes of the slice: x: 2, y: 2, z: 4, core: 2. Of those that a mesh axis runs over, the one named last changes fastest.
Arguments:
- layer_in: bfloat16 [32768, 512], P(('batch', 'wide')), may hold values from -6 to 6
- dual_in: float32 [32768, 512], P(('batch', 'wide')), may hold values from -6 to 6
- long_count: int32 [32], P(('batch', 'wide')), may hold values from 0 to 1, as said below
- w_query: bfloat16 [512, 512], replicated, may hold values from -0.375 to 0.375
- w_key: bfloat16 [512, 512], replicated, may hold values from -0.375 to 0.375
- w_value: bfloat16 [512, 512], replicated, may hold values from -0.25 to 0.25
- w_output: bfloat16 [512, 512], replicated, may hold values from -0.75 to 0.75
- gain_one: float32 [512], replicated, may hold values from 0.5 to 1.5
- shift_one: float32 [512], replicated, may hold values from -3 to 3
- w_in: bfloat16 [512, 2048], P(None, 'wide'), may hold values from -0.25 to 0.25
- bias_in: bfloat16 [2048], P('wide'), may hold values from -3 to 3
- w_out: bfloat16 [2048, 512], P('wide'), may hold values from -0.1875 to 0.1875
- bias_out: float32 [512], replicated, may hold values from -3 to 3
- gain_two: float32 [512], replicated, may hold values from 0.5 to 1.5
- shift_two: float32 [512], replicated, may hold values from -3 to 3
- cot_main: float32 [32768, 512], P(('batch', 'wide')), may hold values from -6 to 6
- cot_dual: float32 [32768, 512], P(('batch', 'wide')), may hold values from -6 to 6
Outputs:
- layer_out: bfloat16 [32768, 512], P(('batch', 'wide'))
- dual_out: float32 [32768, 512], P(('batch', 'wide'))
- grad_layer_in: float32 [32768, 512], P(('batch', 'wide'))
- grad_w_query: float32 [512, 512], replicated
- grad_w_key: float32 [512, 512], replicated
- grad_w_value: float32 [512, 512], replicated
- grad_w_output: float32 [512, 512], replicated
- grad_gain_one: float32 [512], replicated
- grad_shift_one: float32 [512], replicated
- grad_w_in: float32 [512, 2048], P(None, 'wide')
- grad_bias_in: float32 [2048], P('wide')
- grad_w_out: float32 [2048, 512], P('wide')
- grad_bias_out: float32 [512], replicated
- grad_gain_two: float32 [512], replicated
- grad_shift_two: float32 [512], replicated
The draws below stay inside these ranges and needn't reach their ends.
Inputs may be any that keep to these rules, and one draw needn't show every extreme that they name: `long_count`: each entry counts the 1024-token sequences that open a device's 1024 tokens; the rest of those tokens are 256-token sequences.
All inputs are finite; a program needn't handle non-finite values.
Results may differ from the reference program's by a relative error of at most 0.017.
The reference program's roundings to bfloat16 on the way count: a program that leaves them out, or rounds other values in their place, can miss the bound.
Values may be sent and summed in bfloat16 or wider, within the bound.
A program may use at most 256 MiB of HBM per device.

```python
import jax
import jax.numpy as jnp
from jax import lax

D = 512
HEADS = 8
HEAD_DIM = 64
FF = 2048
TOK_DEV = 1024
LONG = 1024
SHORT = 256
TOKENS = 32768


def draw_long_count(key, part):
    top = TOK_DEV // LONG
    counts = jax.random.randint(key, (TOKENS // TOK_DEV,), 0, top + 1, dtype=jnp.int32)
    counts = counts.at[0].set(top).at[1].set(0)
    return counts.astype(jnp.int32)


def block_scale(stream_key, extent, split, smallest, high):
    factor_of = 1.0
    for dim, shards_of in split:
        heights = jax.random.uniform(jax.random.fold_in(jax.random.fold_in(stream_key, 6), dim), (shards_of,), jnp.float32, smallest / len(split), high / len(split))
        factor_of = factor_of * jnp.repeat(jnp.exp(heights), extent[dim] // shards_of).reshape((-1,) + (1,) * (len(extent) - 1 - dim))
    return factor_of


def bell_draw(rng, extent, scale, limit, cuts=(), held_as=jnp.bfloat16):
    array = scale * jax.random.normal(rng, extent, jnp.float32)
    if cuts:
        array = array * block_scale(rng, extent, cuts, -0.22, 0.18)
    return jnp.clip(array, -limit, limit).astype(held_as)


def setup_inputs(seed: int = 0) -> dict:
    key_of = jax.random.split(jax.random.key(seed), 18)
    return {
        "layer_in": bell_draw(key_of[0], (TOKENS, D), 1.0, 6.0, ((0, 32),)),
        "dual_in": bell_draw(key_of[1], (TOKENS, D), 1.0, 6.0, ((0, 32),), jnp.float32),
        "long_count": draw_long_count(jax.random.fold_in(key_of[17], 71), 0),
        "w_query": bell_draw(key_of[3], (D, D), (D // 2) ** -0.5, 0.375),
        "w_key": bell_draw(key_of[4], (D, D), (D // 2) ** -0.5, 0.375),
        "w_value": bell_draw(key_of[5], (D, D), D ** -0.5, 0.25),
        "w_output": bell_draw(key_of[6], (D, D), (D // 8) ** -0.5, 0.75),
        "gain_one": jnp.clip(1.0 + 0.1 * jax.random.normal(key_of[7], (D,), jnp.float32), 0.5, 1.5),
        "shift_one": bell_draw(key_of[8], (D,), 0.5, 3.0, (), jnp.float32),
        "w_in": bell_draw(key_of[9], (D, FF), D ** -0.5, 0.25, ((1, 4),)),
        "bias_in": bell_draw(key_of[10], (FF,), 0.5, 3.0, ((0, 4),)),
        "w_out": bell_draw(key_of[11], (FF, D), (FF // 2) ** -0.5, 0.1875, ((0, 4),)),
        "bias_out": bell_draw(key_of[12], (D,), 0.5, 3.0, (), jnp.float32),
        "gain_two": jnp.clip(1.0 + 0.1 * jax.random.normal(key_of[13], (D,), jnp.float32), 0.5, 1.5),
        "shift_two": bell_draw(key_of[14], (D,), 0.5, 3.0, (), jnp.float32),
        "cot_main": bell_draw(key_of[15], (TOKENS, D), 1.0, 6.0, ((0, 32),), jnp.float32),
        "cot_dual": bell_draw(key_of[16], (TOKENS, D), 1.0, 6.0, ((0, 32),), jnp.float32),
    }


@jax.custom_vjp
def low(v):
    return lax.optimization_barrier(v.astype(jnp.bfloat16)).astype(jnp.float32)

@jax.custom_vjp
def low_back(v):
    return v

def low_keep(v):
    return (low(v), None)

def low_pass(kept, grad):
    return (grad,)

def back_keep(v):
    return (v, None)

def back_low(kept, grad):
    return (low(grad),)
low.defvjp(low_keep, low_pass)
low_back.defvjp(back_keep, back_low)
EPSILON = 1e-05
MASKED = -1000000000.0

def matmul(left, right):
    return jnp.dot(left, right, precision=lax.Precision.HIGHEST)

def rounded(value):
    return low(low_back(value))

def smooth_unit(value):
    return 0.5 * value * (1.0 + jax.scipy.special.erf(value * 0.7071067811865476))

def layer_norm(hidden, gain, shift):
    centre = hidden - lax.optimization_barrier(jnp.mean(hidden, axis=-1, keepdims=True))
    spread = lax.optimization_barrier(jnp.mean(centre * centre, axis=-1, keepdims=True))
    return centre * lax.rsqrt(spread + EPSILON) * gain + shift

def visible_mask(count, windows):
    positions = jnp.arange(LONG, dtype=jnp.int32)
    is_long = jnp.arange(windows, dtype=jnp.int32) < count.astype(jnp.int32)
    segment = jnp.where(is_long[:, None], jnp.int32(0), positions[None, :] // SHORT)
    causal = positions[:, None] >= positions[None, :]
    same_seq = segment[:, :, None] == segment[:, None, :]
    return (causal[None] & same_seq)[:, None]

def block_forward(params, inputs, duals, count):
    w_query, w_key, w_value, w_output, gain_one, shift_one, w_in, bias_in, w_out, bias_out, gain_two, shift_two = params
    windows = TOK_DEV // LONG
    shape_four = (windows, LONG, HEADS, HEAD_DIM)
    factor = jnp.float32(HEAD_DIM) ** (-0.5)
    query = rounded(matmul(inputs, w_query)).reshape(shape_four)
    keyed = rounded(matmul(inputs, w_key)).reshape(shape_four)
    values = rounded(matmul(inputs, w_value)).reshape(shape_four)
    scores = jnp.einsum('wqhd,wkhd->whqk', query, keyed, precision=lax.Precision.HIGHEST) * factor
    scores = jnp.where(visible_mask(count, windows), low_back(scores), MASKED)
    probs = low(jax.nn.softmax(scores, axis=-1))
    mixed = jnp.einsum('whqk,wkhd->wqhd', probs, values, precision=lax.Precision.HIGHEST).reshape(TOK_DEV, D)
    attended = low_back(matmul(rounded(mixed), w_output))
    first = layer_norm(inputs + attended, gain_one, shift_one)
    first_low = low(first)
    pre = low_back(matmul(first_low, w_in) + bias_in)
    active_low = low(smooth_unit(pre))
    branch = low_back(matmul(active_low, w_out) + bias_out)
    return (layer_norm(first + branch, gain_two, shift_two), duals + attended + branch)

def reference(layer_in, dual_in, long_count, w_query, w_key, w_value, w_output, gain_one, shift_one, w_in, bias_in, w_out, bias_out, gain_two, shift_two, cot_main, cot_dual):
    params = tuple((value.astype(jnp.float32) for value in (w_query, w_key, w_value, w_output, gain_one, shift_one, w_in, bias_in, w_out, bias_out, gain_two, shift_two)))
    units = TOKENS // TOK_DEV
    inputs = layer_in.astype(jnp.float32).reshape(units, TOK_DEV, D)
    duals = dual_in.astype(jnp.float32).reshape(units, TOK_DEV, D)
    counts = long_count.astype(jnp.int32)

    def whole(params, inputs):

        def one_block(item):
            return block_forward(params, item[0], item[1], item[2])
        return lax.map(jax.checkpoint(one_block), (inputs, duals, counts))
    outputs, pull = jax.vjp(whole, params, inputs)
    cots = (cot_main.astype(jnp.float32).reshape(units, TOK_DEV, D), cot_dual.astype(jnp.float32).reshape(units, TOK_DEV, D))
    grads, grad_in = pull(cots)
    return (outputs[0].reshape(TOKENS, D).astype(jnp.bfloat16), outputs[1].reshape(TOKENS, D), grad_in.reshape(TOKENS, D), grads[0], grads[1], grads[2], grads[3], grads[4], grads[5], grads[6], grads[7], grads[8], grads[9], grads[10], grads[11])
```

```python
import functools

import jax
import jax.numpy as jnp
from jax import lax
from jax.experimental import pallas as pl
from jax.experimental.pallas import tpu as pltpu
from jax.sharding import PartitionSpec as P

HEADS = 8
HEAD_DIM = 64
LONG = 1024
SHORT = 256
EPSILON = 1e-05
MASKED = -1000000000.0
BLOCK = 256
GROUP = 4

bf16 = jnp.bfloat16
f32 = jnp.float32


def contract(left, right, a, b):
    return lax.dot_general(
        left, right, (((a,), (b,)), ((), ())), preferred_element_type=f32
    )


def dot_nn(left, right):
    return contract(left, right, 1, 0)


def dot_nt(left, right):
    return contract(left, right, 1, 1)


def dot_tn(left, right):
    return contract(left, right, 0, 0)


def dot_tt(left, right):
    return contract(left, right, 0, 1)


def rows_of(block):
    return slice(block * BLOCK, (block + 1) * BLOCK)


def head_of(head):
    return pl.ds(pl.multiple_of(head * HEAD_DIM, HEAD_DIM), HEAD_DIM)


def block_rows(block):
    return pl.ds(pl.multiple_of(block * BLOCK, BLOCK), BLOCK)


def each(count, step):
    lax.fori_loop(0, count, lambda at, _: (step(at), 0)[1], 0)


def row_mean(value):
    return jnp.mean(value, axis=-1, keepdims=True)


def col_sum(value):
    return jnp.sum(value, axis=0, keepdims=True)


class Net:
    def start(self):
        pass

    def weights(self, block):
        pass

    def ffn_grad(self, which, block):
        pass

    def attn_grad(self, chunk):
        pass

    def tick(self, place):
        pass

    def finish(self):
        pass


def layer(r, net, order):
    tokens, width = r.x.shape
    blocks = tokens // BLOCK
    hidden = len(order)

    def project(block):
        cols = rows_of(block)
        xb = r.x[cols]
        r.qt[:, cols] = (dot_tt(r.wq[...], xb) * HEAD_DIM**-0.5).astype(bf16)
        r.kt[:, cols] = dot_tt(r.wk[...], xb).astype(bf16)
        r.vt[:, cols] = dot_tt(r.wv[...], xb).astype(bf16)

    r.wait("x", "wq", "wk", "wv")
    for block in range(blocks):
        project(block)
        net.tick(("project", block))

    row_at = lax.broadcasted_iota(jnp.int32, (BLOCK, BLOCK), 0)
    col_at = lax.broadcasted_iota(jnp.int32, (BLOCK, BLOCK), 1)
    causal = row_at <= col_at
    away = jnp.where(r.count > 0, 0.0, 2e9).astype(f32)

    def soften(head, qb):
        hs = head_of(head)
        query = r.qt[hs, rows_of(qb)]
        parts = []
        peak_off = None
        for tb in range(qb + 1):
            scores = dot_tn(r.kt[hs, rows_of(tb)], query)
            if tb == qb:
                scores = jnp.where(causal, scores, MASKED)
            parts.append(scores)
            peak = jnp.max(scores, axis=0, keepdims=True)
            if tb < qb:
                peak_off = peak if peak_off is None else jnp.maximum(peak_off, peak)
        if peak_off is not None:
            peak = jnp.maximum(peak, peak_off - away)
        total = jnp.zeros((1, BLOCK), f32)
        for tb in range(qb + 1):
            expo = jnp.exp(parts[tb] - (peak if tb == qb else peak + away))
            total += jnp.sum(expo, axis=0, keepdims=True)
            r.p[qb][head, rows_of(tb)] = expo.astype(bf16)
        r.inv_total[pl.ds(head, 1), rows_of(qb)] = 1.0 / total

    def mix(head, qb):
        hs = head_of(head)
        mixed = dot_nn(r.vt[hs, : (qb + 1) * BLOCK], r.p[qb][head])
        mixed *= r.inv_total[pl.ds(head, 1), rows_of(qb)]
        r.mt[hs, rows_of(qb)] = mixed.astype(bf16)

    def attend(group):
        for at in range(GROUP + 1):
            head = group * GROUP + at
            for qb in range(blocks):
                if at < GROUP:
                    soften(head, qb)
                if at > 0:
                    mix(head - 1, qb)

    each(HEADS // GROUP, attend)

    r.wait("wo", "dual")
    gain_one, shift_one = r.vec[0:1], r.vec[1:2]
    def norm_block(block):
        rows = block_rows(block)
        attended = dot_tn(r.mt[:, rows], r.wo[...])
        r.dual[rows] += attended
        hidden_one = r.x[rows].astype(f32) + attended
        centre = hidden_one - row_mean(hidden_one)
        inverse = lax.rsqrt(row_mean(centre * centre) + EPSILON)
        normed = centre * inverse
        r.n1[rows] = normed
        r.i1[rows] = inverse
        r.fl[rows] = (normed * gain_one + shift_one).astype(bf16)

    each(blocks, norm_block)

    for step, j in enumerate(order):
        net.weights(step)

        def half_block(block, j=j):
            rows = block_rows(block)
            pre = dot_nn(r.fl[rows], r.wi[j]) + r.bi[j]
            phi = 0.5 + 0.5 * lax.erf(pre * 0.7071067811865476)
            bell = jnp.exp(-0.5 * pre * pre) * 0.3989422804014327
            r.act[j, rows] = (pre * phi).astype(bf16)
            r.slope[j, rows] = (phi + pre * bell).astype(bf16)

        each(blocks, half_block)

    r.wait("cm", "cd")
    gain_two, shift_two, bias_out = r.vec[3:4], r.vec[4:5], r.vec[2:3]
    r.gvec[...] = jnp.zeros_like(r.gvec)

    def second_block(block):
        rows = block_rows(block)
        branch = dot_nn(r.act[order[0], rows], r.wo2[order[0]])
        for j in order[1:]:
            branch += dot_nn(r.act[j, rows], r.wo2[j])
        branch += bias_out
        r.dual[rows] += branch
        hidden_two = r.n1[rows] * gain_one + shift_one + branch
        centre = hidden_two - row_mean(hidden_two)
        inverse = lax.rsqrt(row_mean(centre * centre) + EPSILON)
        normed = centre * inverse
        r.lo[rows] = (normed * gain_two + shift_two).astype(bf16)
        grad = r.cm[rows]
        r.gvec[3:4] += col_sum(grad * normed)
        r.gvec[4:5] += col_sum(grad)
        scaled = grad * gain_two
        g_sum = inverse * (
            scaled - row_mean(scaled) - normed * row_mean(scaled * normed)
        )
        r.cm[rows] = g_sum
        g_branch = (g_sum + r.cd[rows]).astype(bf16)
        r.gb[rows] = g_branch
        r.gvec[2:3] += col_sum(g_branch.astype(f32))

    each(blocks, second_block)
    r.put("lo")
    r.put("dual")

    for step, j in enumerate(order):
        r.gwo2[j] = dot_tn(r.act[j], r.gb[...]).astype(bf16)
        net.ffn_grad(0, step)
    for step, j in enumerate(order):
        r.gbi[j] = jnp.zeros_like(r.gbi[j])

        def pre_block(block, j=j):
            rows = block_rows(block)
            g_act = dot_nt(r.gb[rows], r.wo2[j])
            g_pre = (g_act * r.slope[j, rows].astype(f32)).astype(bf16)
            r.slope[j, rows] = g_pre
            r.gbi[j] += col_sum(g_pre.astype(f32))

        each(blocks, pre_block)
        r.gwi[j] = dot_tn(r.fl[...], r.slope[j]).astype(bf16)
        net.ffn_grad(1, step)

    def first_block(block):
        rows = block_rows(block)
        g_first = dot_nt(r.slope[order[0], rows], r.wi[order[0]])
        for j in order[1:]:
            g_first += dot_nt(r.slope[j, rows], r.wi[j])
        g_first += r.cm[rows]
        normed = r.n1[rows]
        r.gvec[0:1] += col_sum(g_first * normed)
        r.gvec[1:2] += col_sum(g_first)
        scaled = g_first * gain_one
        g_resid = r.i1[rows] * (
            scaled - row_mean(scaled) - normed * row_mean(scaled * normed)
        )
        r.cm[rows] = g_resid
        g_att = (g_resid + r.cd[rows]).astype(bf16)
        r.gatt[rows] = g_att
        g_mixed = dot_nt(r.wo[...], g_att)
        g_mixed = g_mixed.reshape(HEADS, HEAD_DIM, BLOCK) * r.inv_total[:, rows][:, None]
        g_mixed = g_mixed.reshape(width, BLOCK).astype(bf16)
        r.got[:, rows] = g_mixed
        centred = g_mixed.astype(f32) * r.mt[:, rows].astype(f32)
        r.centred[:, rows] = jnp.sum(centred.reshape(HEADS, HEAD_DIM, BLOCK), axis=1)

    each(blocks, first_block)
    r.gw_o[...] = dot_nn(r.mt[...], r.gatt[...]).astype(bf16)
    net.attn_grad(0)
    r.xt[...] = r.x[...].T

    def back_values(head, tb):
        hs = head_of(head)
        total = None
        for qb in range(tb, blocks):
            part = dot_nt(r.got[hs, rows_of(qb)], r.p[qb][head, rows_of(tb)])
            total = part if total is None else total + part
        r.dvt[hs, rows_of(tb)] = total.astype(bf16)

    def back_scores(head, qb, slot):
        hs = head_of(head)
        got = r.got[hs, rows_of(qb)]
        centred = r.centred[pl.ds(head, 1), rows_of(qb)]
        for tb in range(qb + 1):
            g_probs = dot_tn(r.vt[hs, rows_of(tb)], got)
            probs = r.p[qb][head, rows_of(tb)].astype(f32)
            slot[qb][rows_of(tb)] = (probs * (g_probs - centred)).astype(bf16)

    def back_query(head, qb, slot):
        hs = head_of(head)
        g_query = dot_nn(r.kt[hs, : (qb + 1) * BLOCK], slot[qb][...])
        r.dqt[hs, rows_of(qb)] = (g_query * HEAD_DIM**-0.5).astype(bf16)

    def back_keys(head, tb, slot):
        hs = head_of(head)
        total = None
        for qb in range(tb, blocks):
            part = dot_nt(r.qt[hs, rows_of(qb)], slot[qb][rows_of(tb)])
            total = part if total is None else total + part
        r.dkt[hs, rows_of(tb)] = total.astype(bf16)

    half = width // 2

    def value_heads(group):
        for at in range(GROUP):
            for tb in range(blocks):
                back_values(group * GROUP + at, tb)

    each(HEADS // GROUP, value_heads)
    r.gw_v[...] = dot_nt(r.xt[...], r.dvt[...]).astype(bf16)
    net.attn_grad(1)

    def score_heads(group):
        for at in range(GROUP + 1):
            head = group * GROUP + at
            for block in range(blocks):
                if at < GROUP:
                    back_scores(head, block, r.gs[at % 2])
                if at > 0:
                    back_query(head - 1, block, r.gs[(at - 1) % 2])
                    back_keys(head - 1, block, r.gs[(at - 1) % 2])
        rows = pl.ds(pl.multiple_of(group * half, half), half)
        r.gw_qk[group, :, :half] = dot_nt(r.xt[...], r.dqt[rows]).astype(bf16)
        r.gw_qk[group, :, half:] = dot_nt(r.xt[...], r.dkt[rows]).astype(bf16)

    each(HEADS // GROUP, score_heads)

    def input_block(block):
        rows = block_rows(block)
        grad = dot_tt(r.dqt[:, rows], r.wq[...])
        grad += dot_tt(r.dkt[:, rows], r.wk[...])
        grad += dot_tt(r.dvt[:, rows], r.wv[...])
        r.cm[rows] += grad

    each(blocks, input_block)
    r.put("cm")
    net.finish()
    r.drain()


class Refs:
    def __init__(self, names, refs):
        self.__dict__.update(zip(names, refs))
        self.pending = {}
        self.out = []

    def fetch(self, name, source, target, sem):
        copy = pltpu.make_async_copy(source, target, sem)
        copy.start()
        self.pending[name] = copy

    def wait(self, *names):
        for name in names:
            if name in self.pending:
                self.pending.pop(name).wait()

    def put(self, name):
        source, target, sem = self.outs[name]
        copy = pltpu.make_async_copy(source, target, sem)
        copy.start()
        self.out.append(copy)

    def drain(self):
        for copy in self.out:
            copy.wait()


FETCHED = ("x", "wq", "wk", "wv", "wo", "wi", "wo2", "dual", "cm", "cd")


def scratch_list(tokens, width, hidden, piece):
    vmem = pltpu.VMEM
    blocks = tokens // BLOCK
    names = {
        "x": vmem((tokens, width), bf16),
        "wq": vmem((width, width), bf16),
        "wk": vmem((width, width), bf16),
        "wv": vmem((width, width), bf16),
        "wo": vmem((width, width), bf16),
        "wi": vmem((hidden, width, piece), bf16),
        "wo2": vmem((hidden, piece, width), bf16),
        "dual": vmem((tokens, width), f32),
        "cm": vmem((tokens, width), f32),
        "cd": vmem((tokens, width), f32),
        "qt": vmem((width, tokens), bf16),
        "kt": vmem((width, tokens), bf16),
        "vt": vmem((width, tokens), bf16),
        "mt": vmem((width, tokens), bf16),
        "inv_total": vmem((HEADS, tokens), f32),
        "centred": vmem((HEADS, tokens), f32),
        "n1": vmem((tokens, width), f32),
        "i1": vmem((tokens, 1), f32),
        "fl": vmem((tokens, width), bf16),
        "act": vmem((hidden, tokens, piece), bf16),
        "slope": vmem((hidden, tokens, piece), bf16),
        "gb": vmem((tokens, width), bf16),
        "lo": vmem((tokens, width), bf16),
        "gatt": vmem((tokens, width), bf16),
        "got": vmem((width, tokens), bf16),
        "dqt": vmem((width, tokens), bf16),
        "dkt": vmem((width, tokens), bf16),
        "dvt": vmem((width, tokens), bf16),
        "xt": vmem((width, tokens), bf16),
    }
    for qb in range(blocks):
        names[f"p{qb}"] = vmem((HEADS, (qb + 1) * BLOCK, BLOCK), bf16)
        names[f"g{qb}"] = vmem(((qb + 1) * BLOCK, BLOCK), bf16)
        names[f"h{qb}"] = vmem(((qb + 1) * BLOCK, BLOCK), bf16)
    return names


def plain_kernel(names, blocks, order, *refs):
    r = Refs(names, refs)
    r.count = r.count_ref[0]
    sems = r.sems
    for at, name in enumerate(FETCHED):
        r.fetch(name, getattr(r, name + "_hbm"), getattr(r, name), sems.at[at])
    r.p = [getattr(r, f"p{qb}") for qb in range(blocks)]
    r.gs = [[getattr(r, f"{s}{qb}") for qb in range(blocks)] for s in "gh"]
    base = len(FETCHED)
    r.outs = {
        "lo": (r.lo, r.lo_hbm, sems.at[base]),
        "dual": (r.dual, r.dual_out, sems.at[base + 1]),
        "cm": (r.cm, r.gx_out, sems.at[base + 2]),
    }
    r.wait("wi", "wo2")
    layer(r, Net(), order)


def plain_layer(x, dual, count, wq, wk, wv, wo, vec, wi, bi, wo2, cm, cd):
    tokens, width = x.shape
    hidden, _, piece = wi.shape
    blocks = tokens // BLOCK
    anyspace = pl.BlockSpec(memory_space=pl.ANY)
    vm = pl.BlockSpec(memory_space=pltpu.VMEM)
    sm = pl.BlockSpec(memory_space=pltpu.SMEM)
    ins = {
        "x_hbm": (x, anyspace),
        "wq_hbm": (wq, anyspace),
        "wk_hbm": (wk, anyspace),
        "wv_hbm": (wv, anyspace),
        "wo_hbm": (wo, anyspace),
        "wi_hbm": (wi, anyspace),
        "wo2_hbm": (wo2, anyspace),
        "dual_hbm": (dual, anyspace),
        "cm_hbm": (cm, anyspace),
        "cd_hbm": (cd, anyspace),
        "count_ref": (count, sm),
        "vec": (vec, vm),
        "bi": (bi, vm),
    }
    shape = jax.ShapeDtypeStruct
    outs = {
        "lo_hbm": (shape((tokens, width), bf16), anyspace),
        "dual_out": (shape((tokens, width), f32), anyspace),
        "gx_out": (shape((tokens, width), f32), anyspace),
        "gw_o": (shape((width, width), bf16), vm),
        "gw_v": (shape((width, width), bf16), vm),
        "gw_qk": (shape((2, width, width), bf16), vm),
        "gwi": (shape((hidden, width, piece), bf16), vm),
        "gwo2": (shape((hidden, piece, width), bf16), vm),
        "gvec": (shape((8, width), f32), vm),
        "gbi": (shape((hidden, 1, piece), f32), vm),
    }
    scratch = scratch_list(tokens, width, hidden, piece)
    scratch["sems"] = pltpu.SemaphoreType.DMA((len(FETCHED) + 3,))
    names = list(ins) + list(outs) + list(scratch)
    return pl.pallas_call(
        functools.partial(plain_kernel, names, blocks, tuple(range(hidden))),
        out_shape=[o[0] for o in outs.values()],
        in_specs=[i[1] for i in ins.values()],
        out_specs=[o[1] for o in outs.values()],
        scratch_shapes=list(scratch.values()),
        compiler_params=pltpu.CompilerParams(vmem_limit_bytes=63 << 20),
        cost_estimate=pl.CostEstimate(flops=25 * 10**9, bytes_accessed=30 << 20, transcendentals=12 << 20),
    )(*[i[0] for i in ins.values()])


def unpack(summed_qk, half):
    gq = jnp.concatenate([summed_qk[0][:, :half], summed_qk[1][:, :half]], axis=1)
    gk = jnp.concatenate([summed_qk[0][:, half:], summed_qk[1][:, half:]], axis=1)
    return gq, gk


def plain_body(layer_in, dual_in, long_count, w_query, w_key, w_value, w_output, gain_one, shift_one,
               w_in, bias_in, w_out, bias_out, gain_two, shift_two, cot_main, cot_dual):
    width = layer_in.shape[1]
    piece = width
    w_in_all = lax.all_gather(w_in, "wide", axis=1, tiled=True)
    bias_all = lax.all_gather(bias_in, "wide", axis=0, tiled=True)
    w_out_all = lax.all_gather(w_out, "wide", axis=0, tiled=True)
    hidden = w_in_all.shape[1] // piece
    wi = w_in_all.reshape(width, hidden, piece).transpose(1, 0, 2)
    wo2 = w_out_all.reshape(hidden, piece, width)
    bi = bias_all.astype(f32).reshape(hidden, 1, piece)
    zero = jnp.zeros_like(gain_one)
    vec = jnp.stack([gain_one, shift_one, bias_out, gain_two, shift_two, zero, zero, zero])
    lo, dual, gx, gw_o, gw_v, gw_qk, gwi, gwo2, gvec, gbi = plain_layer(
        layer_in, dual_in, long_count, w_query, w_key, w_value, w_output, vec, wi, bi, wo2, cot_main, cot_dual)
    gwi = gwi.transpose(1, 0, 2).reshape(w_in_all.shape)
    gwo2 = gwo2.reshape(w_out_all.shape)
    gwi = lax.psum(lax.psum_scatter(gwi, "wide", scatter_dimension=1, tiled=True), "batch").astype(f32)
    gwo2 = lax.psum(lax.psum_scatter(gwo2, "wide", scatter_dimension=0, tiled=True), "batch").astype(f32)
    gbi = lax.psum(lax.psum_scatter(gbi.reshape(-1), "wide", scatter_dimension=0, tiled=True), "batch")
    gw_o, gw_v, gw_qk, gvec = lax.psum((gw_o, gw_v, gw_qk, gvec), ("batch", "wide"))
    gq, gk = unpack(gw_qk.astype(f32), width // 2)
    return (lo, dual, gx, gq, gk, gw_v.astype(f32), gw_o.astype(f32), gvec[0], gvec[1], gwi, gbi, gwo2, gvec[2], gvec[3], gvec[4])


def solution(mesh):
    tokens = P(("batch", "wide"), None)
    return jax.shard_map(
        plain_body,
        mesh=mesh,
        in_specs=(tokens, tokens, P(("batch", "wide")), P(), P(), P(), P(), P(), P(), P(None, "wide"), P("wide"),
                  P("wide", None), P(), P(), P(), tokens, tokens),
        out_specs=(tokens, tokens, tokens, P(), P(), P(), P(), P(), P(), P(None, "wide"), P("wide"),
                   P("wide", None), P(), P(), P()),
        check_vma=False,
    )
```

```python
import functools

import jax
import jax.numpy as jnp
from jax import lax
from jax.experimental import pallas as pl
from jax.experimental.pallas import tpu as pltpu
from jax.sharding import PartitionSpec as P

HEADS = 8
HEAD_DIM = 64
EPSILON = 1e-05
MASKED = -1000000000.0
BLOCK = 256
HALF = 512
PARTS = 4
PRE_UNROLL = 1
HALF_UNROLL = NORM_UNROLL = SECOND_UNROLL = FIRST_UNROLL = INPUT_UNROLL = 2
Y_FIRST = (True, True, True, False, False, False)

bf16 = jnp.bfloat16
f32 = jnp.float32


def contract(left, right, a, b):
    return lax.dot_general(
        left, right, (((a,), (b,)), ((), ())), preferred_element_type=f32
    )


def dot_nn(left, right):
    return contract(left, right, 1, 0)


def dot_nt(left, right):
    return contract(left, right, 1, 1)


def dot_tn(left, right):
    return contract(left, right, 0, 0)


def dot_tt(left, right):
    return contract(left, right, 0, 1)


def span_of(at, size):
    if isinstance(at, int):
        return slice(at * size, (at + 1) * size)
    return pl.ds(pl.multiple_of(at * size, size), size)


def rows_of(block):
    return span_of(block, BLOCK)


def head_of(head):
    return span_of(head, HEAD_DIM)


def split(block):
    return block // 2, span_of(block % 2, BLOCK)


def each(count, step, unroll=1):
    def several(at, _):
        for k in range(unroll):
            step(at * unroll + k)
        return 0

    lax.fori_loop(0, count // unroll, several, 0)


def row_mean(value):
    return jnp.mean(value, axis=-1, keepdims=True)


def col_sum(value):
    return jnp.sum(value, axis=0, keepdims=True)


def joined(value):
    return value.reshape(value.shape[0] * value.shape[1], value.shape[2])


def layer(r, net):
    tokens, width = r.x.shape
    blocks = tokens // BLOCK
    hidden = r.wi.shape[0]
    slots = tuple(range(hidden))

    r.wait("x", "wq", "wk", "wv")
    for block in range(blocks):
        cols = rows_of(block)
        xb = r.x[cols]
        r.qt[:, cols] = (dot_tt(r.wq[...], xb) * HEAD_DIM**-0.5).astype(bf16)
        r.kt[:, cols] = dot_tt(r.wk[...], xb).astype(bf16)
        r.vt[:, cols] = dot_tt(r.wv[...], xb).astype(bf16)
    net.tick(At.PROJECT)

    row_at = lax.broadcasted_iota(jnp.int32, (BLOCK, BLOCK), 0)
    col_at = lax.broadcasted_iota(jnp.int32, (BLOCK, BLOCK), 1)
    causal = row_at <= col_at
    away = jnp.where(r.count > 0, 0.0, 2e9).astype(f32)

    def soften(head, qb):
        hs = head_of(head)
        query = r.qt[hs, rows_of(qb)]
        parts = []
        peak_off = None
        for tb in range(qb + 1):
            scores = dot_tn(r.kt[hs, rows_of(tb)], query)
            if tb == qb:
                scores = jnp.where(causal, scores, MASKED)
            parts.append(scores)
            peak = jnp.max(scores, axis=0, keepdims=True)
            if tb < qb:
                peak_off = peak if peak_off is None else jnp.maximum(peak_off, peak)
        if peak_off is not None:
            peak = jnp.maximum(peak, peak_off - away)
        total = jnp.zeros((1, BLOCK), f32)
        for tb in range(qb + 1):
            expo = jnp.exp(parts[tb] - (peak if tb == qb else peak + away))
            total += jnp.sum(expo, axis=0, keepdims=True)
            r.p[qb][head, rows_of(tb)] = expo.astype(bf16)
        r.inv_total[pl.ds(head, 1), rows_of(qb)] = 1.0 / total

    def mix(head, qb):
        hs = head_of(head)
        mixed = dot_nn(r.vt[hs, : (qb + 1) * BLOCK], r.p[qb][head])
        mixed *= r.inv_total[pl.ds(head, 1), rows_of(qb)]
        r.mt[hs, rows_of(qb)] = mixed.astype(bf16)

    for head in range(HEADS + 1):
        for qb in range(blocks):
            if head < HEADS:
                soften(head, qb)
            if head > 0:
                mix(head - 1, qb)
        net.tick(At.ATTEND, head)

    r.wait("wo", "dual")
    gain_one, shift_one = r.gain_one[...][None], r.shift_one[...][None]

    def norm_block(block):
        rows = rows_of(block)
        attended = dot_tn(r.mt[:, rows], r.wo[...])
        r.dual[rows] += attended
        hidden_one = r.x[rows].astype(f32) + attended
        centre = hidden_one - row_mean(hidden_one)
        inverse = lax.rsqrt(row_mean(centre * centre) + EPSILON)
        normed = centre * inverse
        r.n1[rows] = normed
        r.i1[rows] = inverse
        r.fl[rows] = (normed * gain_one + shift_one).astype(bf16)

    each(blocks, norm_block, NORM_UNROLL)

    def half_block(block, pair, place):
        first_low = r.fl[rows_of(block)]
        th, rows = split(block)
        for j in pair:
            pre = dot_nn(first_low, r.wi[j]) + r.bi[j, 0:1]
            phi = 0.5 + 0.5 * lax.erf(pre * 0.7071067811865476)
            bell = jnp.exp(-0.5 * pre * pre) * 0.3989422804014327
            r.act[j, th, rows] = (pre * phi).astype(bf16)
            r.slope[j, th, rows] = (phi + pre * bell).astype(bf16)
        net.loop_tick(place, block, blocks)

    net.tick(At.HIDDEN)
    each(blocks, lambda block: half_block(block, slots[:2], At.HALVES), HALF_UNROLL)
    net.tick(At.OTHERS)
    each(blocks, lambda block: half_block(block, slots[2:], At.HALVES2), HALF_UNROLL)

    r.wait("cm", "cd")
    net.tick(At.BRANCH)
    gain_two, shift_two = r.gain_two[...][None], r.shift_two[...][None]
    bias_out = r.bias_out[...][None]
    r.gvec[...] = jnp.zeros_like(r.gvec)

    def second_block(block):
        rows = rows_of(block)
        th, cut = split(block)
        branch = dot_nn(r.act[0, th, cut], r.wo2[0])
        for j in slots[1:]:
            branch += dot_nn(r.act[j, th, cut], r.wo2[j])
        branch += bias_out
        r.dual[rows] += branch
        hidden_two = r.n1[rows] * gain_one + shift_one + branch
        centre = hidden_two - row_mean(hidden_two)
        inverse = lax.rsqrt(row_mean(centre * centre) + EPSILON)
        normed = centre * inverse
        r.gwi[th, cut] = (normed * gain_two + shift_two).astype(bf16)
        grad = r.cm[rows]
        r.gvec[3:4] += col_sum(grad * normed)
        r.gvec[4:5] += col_sum(grad)
        scaled = grad * gain_two
        g_sum = inverse * (
            scaled - row_mean(scaled) - normed * row_mean(scaled * normed)
        )
        r.cm[rows] = g_sum
        g_branch = (g_sum + r.cd[rows]).astype(bf16)
        r.gb[rows] = g_branch
        r.gvec[2:3] += col_sum(g_branch.astype(f32))

    each(blocks, second_block, SECOND_UNROLL)
    r.put("lo", 0)
    r.put("lo", 1)
    r.put("dual", 0)

    for j in reversed(slots):
        r.gwo2[j] = dot_tn(joined(r.act[j]), r.gb[...]).astype(bf16)
        net.tick(At.OUT, j)
    r.gbi[...] = jnp.zeros_like(r.gbi)

    def pre_block(block):
        g_branch = r.gb[rows_of(block)]
        th, rows = split(block)
        for j in slots:
            g_act = dot_nt(g_branch, r.wo2[j])
            g_pre = (g_act * r.slope[j, th, rows].astype(f32)).astype(bf16)
            r.slope[j, th, rows] = g_pre
            r.gbi[j] += col_sum(g_pre.astype(f32))
        net.loop_tick(At.PRE, block, blocks)

    each(blocks, pre_block, PRE_UNROLL)
    r.finished("lo")
    for j in reversed(slots):
        r.gwi[j] = dot_tn(r.fl[...], joined(r.slope[j])).astype(bf16)
        net.tick(At.IN, j)

    def first_block(block):
        rows = rows_of(block)
        th, cut = split(block)
        g_first = dot_nt(r.slope[0, th, cut], r.wi[0])
        for j in slots[1:]:
            g_first += dot_nt(r.slope[j, th, cut], r.wi[j])
        g_first += r.cm[rows]
        normed = r.n1[rows]
        r.gvec[0:1] += col_sum(g_first * normed)
        r.gvec[1:2] += col_sum(g_first)
        scaled = g_first * gain_one
        g_resid = r.i1[rows] * (
            scaled - row_mean(scaled) - normed * row_mean(scaled * normed)
        )
        r.cm[rows] = g_resid
        g_att = (g_resid + r.cd[rows]).astype(bf16)
        r.gb[rows] = g_att
        g_mixed = dot_nt(r.wo[...], g_att)
        g_mixed = g_mixed.reshape(HEADS, HEAD_DIM, BLOCK) * r.inv_total[:, rows][:, None]
        g_mixed = g_mixed.reshape(width, BLOCK).astype(bf16)
        r.act[3, th, :, cut] = g_mixed
        centred = g_mixed.astype(f32) * r.mt[:, rows].astype(f32)
        r.centred[:, rows] = jnp.sum(centred.reshape(HEADS, HEAD_DIM, BLOCK), axis=1)
        net.loop_tick(At.FIRST, block, blocks)

    each(blocks, first_block, FIRST_UNROLL)
    r.gw[0] = dot_nn(r.mt[...], r.gb[...]).astype(bf16)
    net.tick(At.W_OUTPUT)
    for th in range(2):
        r.slope[0, th] = r.x[th * HALF : (th + 1) * HALF].T

    def columns(which, head, block):
        th, cut = split(block)
        return which, th, head_of(head), cut

    def back_values(head, tb):
        total = None
        for qb in range(tb, blocks):
            part = dot_nt(r.act[columns(3, head, qb)], r.p[qb][head, rows_of(tb)])
            total = part if total is None else total + part
        r.act[columns(2, head, tb)] = total.astype(bf16)

    def back_scores(head, qb, slot):
        got = r.act[columns(3, head, qb)]
        centred = r.centred[pl.ds(head, 1), rows_of(qb)]
        for tb in range(qb + 1):
            g_probs = dot_tn(r.vt[head_of(head), rows_of(tb)], got)
            probs = r.p[qb][head, rows_of(tb)].astype(f32)
            slot[qb][rows_of(tb)] = (probs * (g_probs - centred)).astype(bf16)

    def back_query(head, qb, slot):
        g_query = dot_nn(r.kt[head_of(head), : (qb + 1) * BLOCK], slot[qb][...])
        r.act[columns(0, head, qb)] = (g_query * HEAD_DIM**-0.5).astype(bf16)

    def back_keys(head, tb, slot):
        total = None
        for qb in range(tb, blocks):
            part = dot_nt(r.qt[head_of(head), rows_of(qb)], slot[qb][rows_of(tb)])
            total = part if total is None else total + part
        r.act[columns(1, head, tb)] = total.astype(bf16)

    def against_x(which, rows):
        total = dot_nt(r.slope[0, 0], r.act[which, 0, rows])
        return (total + dot_nt(r.slope[0, 1], r.act[which, 1, rows])).astype(bf16)

    for head in range(HEADS):
        for tb in range(blocks):
            back_values(head, tb)
        net.tick(At.VALUES, head)
    r.gw[1] = against_x(2, slice(0, width))
    net.tick(At.W_VALUE)
    size = HEADS // PARTS
    part_width = size * HEAD_DIM

    for head in range(HEADS + 1):
        for block in range(blocks):
            if head < HEADS:
                back_scores(head, block, r.gs[head % 2])
            if head > 0:
                back_query(head - 1, block, r.gs[(head - 1) % 2])
                back_keys(head - 1, block, r.gs[(head - 1) % 2])
        if head > 0 and head % size == 0:
            part = head // size - 1
            rows = span_of(part, part_width)
            r.gqk[part, :, :part_width] = against_x(0, rows)
            r.gqk[part, :, part_width:] = against_x(1, rows)
        net.tick(At.SCORES, head)

    def input_block(block):
        rows = rows_of(block)
        th, cut = split(block)
        grad = dot_tt(r.act[0, th, :, cut], r.wq[...])
        grad += dot_tt(r.act[1, th, :, cut], r.wk[...])
        grad += dot_tt(r.act[2, th, :, cut], r.wv[...])
        r.cm[rows] += grad
        net.loop_tick(At.INPUT, block, blocks)

    each(blocks, input_block, INPUT_UNROLL)
    r.put("cm", 0)
    net.tick(At.END)


class Refs:
    def __init__(self, names, refs):
        self.__dict__.update(zip(names, refs))
        self.pending = {}
        self.out = {}

    def fetch(self, name, source, target, sem):
        copy = pltpu.make_async_copy(source, target, sem)
        copy.start()
        self.pending[name] = copy

    def wait(self, *names):
        for name in names:
            self.pending.pop(name).wait()

    def put(self, name, at):
        source, target, sem = self.outs[name, at]
        copy = pltpu.make_async_copy(source, target, sem)
        copy.start()
        self.out[name, at] = copy

    def finished(self, name):
        for key in [key for key in self.out if key[0] == name]:
            self.out.pop(key).wait()

    def drain(self):
        for copy in self.out.values():
            copy.wait()


FETCHED = ("x", "wq", "wk", "wv", "wo", "dual", "cm", "cd")


def scratch_of(tokens, width, hidden):
    vmem = pltpu.VMEM
    wide = (hidden, tokens // HALF, HALF, HALF)
    names = dict(
        x=vmem((tokens, width), bf16),
        wq=vmem((width, width), bf16),
        wk=vmem((width, width), bf16),
        wv=vmem((width, width), bf16),
        wo=vmem((width, width), bf16),
        dual=vmem((tokens, width), f32),
        cm=vmem((tokens, width), f32),
        cd=vmem((tokens, width), f32),
        qt=vmem((width, tokens), bf16),
        kt=vmem((width, tokens), bf16),
        vt=vmem((width, tokens), bf16),
        mt=vmem((width, tokens), bf16),
        inv_total=vmem((HEADS, tokens), f32),
        centred=vmem((HEADS, tokens), f32),
        n1=vmem((tokens, width), f32),
        i1=vmem((tokens, 1), f32),
        fl=vmem((tokens, width), bf16),
        act=vmem(wide, bf16),
        slope=vmem(wide, bf16),
        gb=vmem((tokens, width), bf16),
    )
    for qb in range(tokens // BLOCK):
        names[f"p{qb}"] = vmem((HEADS, (qb + 1) * BLOCK, BLOCK), bf16)
        names[f"g{qb}"] = vmem(((qb + 1) * BLOCK, BLOCK), bf16)
        names[f"h{qb}"] = vmem(((qb + 1) * BLOCK, BLOCK), bf16)
    return names


def begin(r, tokens):
    blocks = tokens // BLOCK
    r.count = r.count_ref[0]
    r.p = [getattr(r, f"p{qb}") for qb in range(blocks)]
    r.gs = [[getattr(r, f"{s}{qb}") for qb in range(blocks)] for s in "gh"]
    for at, name in enumerate(FETCHED):
        r.fetch(name, getattr(r, name + "_hbm"), getattr(r, name), r.sems.at[at])
    base = len(FETCHED)
    r.outs = {
        ("lo", 0): (r.gwi.at[0], r.lo_out.at[0:HALF], r.sems.at[base]),
        ("lo", 1): (r.gwi.at[1], r.lo_out.at[HALF : 2 * HALF], r.sems.at[base + 1]),
        ("dual", 0): (r.dual, r.dual_out, r.sems.at[base + 2]),
        ("cm", 0): (r.cm, r.gx_out, r.sems.at[base + 3]),
    }
    return base + 4


class Quiet:
    def tick(self, *place):
        pass

    def loop_tick(self, place, at, count):
        pass


class At:
    (PROJECT, ATTEND, HIDDEN, HALVES, OTHERS, HALVES2, BRANCH, OUT, PRE, IN, FIRST, W_OUTPUT,
     VALUES, W_VALUE, SCORES, INPUT, END) = range(17)


class Kind:
    (W_X, W_Y, W_CORE, W_PASS, W_TURN, W_BIAS, F_AWAY, F_NEAR, F_X, F_Y, F_Y_OWN, F_NEXT, F_FAR,
     G_FAR, G_Y, G_NEXT, A_CORE, A_ONE, A_TWO, A_NEXT, A_FAR, B_FAR, B_NEXT, B_TWO, B_ONE, B_CORE,
     V_STEP) = range(27)


class Net:
    def __init__(self, r, plan):
        self.r = r
        self.plan = plan
        b, w = lax.axis_index("batch"), lax.axis_index("wide")
        z, y, x, c = b // 2, b % 2, w // 2, w % 2
        self.y, self.x, self.c, self.w = y, x, c, w
        self.core = (b, x * 2 + 1 - c)
        self.ex = (b, (1 - x) * 2 + c)
        self.diagonal = (b, (1 - x) * 2 + 1 - c)
        self.why = (z * 2 + 1 - y, w)
        self.odd, self.high = z % 2, z // 2
        self.next = ((z + 1 - 2 * self.odd) * 2 + y, w)
        self.far = (((z + 2) % 4) * 2 + y, w)
        self.table = {}
        self.used = set()
        self.parts = []
        self.describe()

    def copy(self, name, to, source, target):
        self.table[name] = (len(self.table), to, source, target)

    def build(self, name):
        index, to, source, target = self.table[name]
        return pltpu.make_async_remote_copy(
            src_ref=source(),
            dst_ref=target(),
            send_sem=self.r.send_sem.at[index],
            recv_sem=self.r.recv_sem.at[index],
            device_id=to,
            device_id_type=pl.DeviceIdType.MESH,
        )

    def start(self, *names):
        for name in names:
            self.used.add(name)
            self.build(name).start()

    def got(self, *names):
        for name in names:
            self.build(name).wait_recv()

    def tick(self, *place):
        for event, *args in self.plan.get(place, ()):
            event(self, *args)

    def loop_tick(self, place, at, count):
        for k in range(count):
            if self.plan.get((place, k)):
                self.guard(at, k, place)

    def guard(self, at, k, place):
        if isinstance(at, int):
            if at == k:
                self.tick(place, k)
        else:
            pl.when(at == k)(functools.partial(self.tick, place, k))

    def span(self, start, size):
        return pl.ds(pl.multiple_of(start, size), size)

    def describe(self):
        r, copy, span = self.r, self.copy, self.span
        y, x, c, odd, high = self.y, self.x, self.c, self.odd, self.high
        own = (r.wi_hbm, r.wo2_hbm)
        held = (r.wi, r.wo2)
        for m in range(2):
            copy((Kind.W_CORE, m), self.core, lambda m=m: own[m], lambda m=m: held[m].at[1])
            for q in range(2):
                mine = lambda q=q: span(y * 256 + q * 128, 128)
                other = lambda q=q: span((1 - y) * 256 + q * 128, 128)
                copy((Kind.W_X, m, q), self.ex, lambda m=m, f=mine: own[m].at[f()], lambda m=m, f=mine: held[m].at[2, f()])
                copy((Kind.W_Y, m, q), self.why, lambda m=m, f=mine: held[m].at[2, f()], lambda m=m, f=mine: held[m].at[2, f()])
                copy((Kind.W_PASS, m, q), self.core, lambda m=m, f=mine: held[m].at[2, f()], lambda m=m, f=mine: held[m].at[3, f()])
                copy((Kind.W_TURN, m, q), self.core, lambda m=m, f=other: held[m].at[2, f()], lambda m=m, f=other: held[m].at[3, f()])
        for slot, to in ((1, self.core), (2, self.ex), (3, self.diagonal)):
            copy((Kind.W_BIAS, slot), to, lambda: r.bi.at[0], lambda slot=slot: r.bi.at[slot])

        grads = (r.gwo2, r.gwi)
        for m in range(2):
            copy((Kind.F_AWAY, m), self.core, lambda m=m: grads[m].at[3], lambda m=m: r.rca.at[m])
            copy((Kind.F_NEAR, m), self.core, lambda m=m: grads[m].at[1], lambda m=m: r.rcd.at[m])
            for h in range(2):
                kept = lambda h=h: span(h * 256 + y * 128, 128)
                away = lambda h=h: span(h * 256 + (1 - y) * 128, 128)
                if h == 0:
                    copy((Kind.F_X, m, h), self.ex, lambda m=m: grads[m].at[2, 0:256], lambda m=m: r.rx.at[m, 0:256])
                else:
                    copy((Kind.F_X, m, h), self.ex, lambda m=m, f=kept: grads[m].at[2, f()], lambda m=m: r.rx.at[m, 256:384])
                    copy((Kind.F_Y_OWN, m, h), self.why, lambda m=m, f=away: grads[m].at[0, f()], lambda m=m: r.ry.at[m, 2])
                slot = 0 if h == 0 else 2
                copy((Kind.F_Y, m, h), self.why, lambda m=m, s=slot, f=away: grads[m].at[s, f()], lambda m=m, h=h: r.ry.at[m, h])
                u = m * 2 + h
                near = lambda h=h: span(h * 256 + y * 128 + odd * 64, 64)
                near_y = lambda h=h: span(h * 256 + (1 - y) * 128 + odd * 64, 64)
                gone = lambda h=h: span(h * 256 + y * 128 + (1 - odd) * 64, 64)
                piece = lambda h=h: span(h * 256 + y * 128 + odd * 64 + high * 32, 32)
                gone2 = lambda h=h: span(h * 256 + y * 128 + odd * 64 + (1 - high) * 32, 32)
                copy((Kind.F_NEXT, m, h), self.next, lambda m=m, f=gone: grads[m].at[0, f()], lambda u=u: r.rn.at[u])
                copy((Kind.F_FAR, m, h), self.far, lambda m=m, f=gone2: grads[m].at[0, f()], lambda u=u: r.rf.at[u])
                for kind, to, rows in ((Kind.G_FAR, self.far, piece), (Kind.G_Y, self.why, near)):
                    copy((kind, m, h), to, lambda m=m, f=rows: r.fout.at[m, f()], lambda m=m, f=rows: r.fout.at[m, f()])
                for k, rows in enumerate((near, near_y)):
                    copy((Kind.G_NEXT, m, h, k), self.next, lambda m=m, f=rows: r.fout.at[m, f()], lambda m=m, f=rows: r.fout.at[m, f()])

        for n in range(2 + PARTS):
            refs = (r.gw, r.ac, r.a1, r.a2, r.a3, r.a4, r.aout)
            at = n
            if n >= 2:
                refs = (r.gqk, r.qc, r.q1, r.q2, r.q3, r.q4, r.qout)
                at = n - 2
            grad, *received, out = [ref.at[at] for ref in refs]
            first, second = ((self.ex, x), (self.why, y))
            if Y_FIRST[n]:
                first, second = second, first
            levels = ((self.core, c), first, second, (self.next, odd), (self.far, high))
            kinds = (Kind.A_CORE, Kind.A_ONE, Kind.A_TWO, Kind.A_NEXT, Kind.A_FAR)
            back = (Kind.B_CORE, Kind.B_ONE, Kind.B_TWO, Kind.B_NEXT, Kind.B_FAR)
            size = grad.shape[0]
            base = lambda: 0
            keeps = []
            for level, (to, bit) in enumerate(levels):
                size //= 2
                keep = lambda f=base, p=bit, s=size: span(f() + p * s, s)
                give = lambda f=base, p=bit, s=size: span(f() + (1 - p) * s, s)
                base = lambda f=base, p=bit, s=size: f() + p * s
                keeps.append(keep)
                copy((kinds[level], n), to, lambda g=grad, f=give: g.at[f()], lambda t=received[level]: t)
                copy((back[level], n), to, lambda o=out, f=keep: o.at[f()], lambda o=out, f=keep: o.at[f()])
            self.parts.append((grad, received, out, keeps))

        for at, to in enumerate((self.core, self.ex, self.why, self.next, self.far)):
            copy((Kind.V_STEP, at), to, lambda at=at: r.vs.at[at], lambda at=at: r.vr.at[at])

    def enter(self):
        barrier = pltpu.get_barrier_semaphore()
        peers = [self.core, self.ex, self.diagonal, self.why, self.next, self.far]
        for peer in peers:
            pl.semaphore_signal(barrier, inc=1, device_id=peer, device_id_type=pl.DeviceIdType.MESH)
        pl.semaphore_wait(barrier, len(peers))
        for slot in (1, 2, 3):
            self.start((Kind.W_BIAS, slot))
        for m in range(2):
            self.start((Kind.W_X, m, 0), (Kind.W_X, m, 1))
        self.start((Kind.W_CORE, 0), (Kind.W_CORE, 1))

    def pass_x(self, m, q):
        self.got((Kind.W_X, m, q))
        self.start((Kind.W_Y, m, q), (Kind.W_PASS, m, q))

    def pass_y(self, m, q):
        self.got((Kind.W_Y, m, q))
        self.start((Kind.W_TURN, m, q))

    def arrived_near(self, m):
        if m == 0:
            self.got((Kind.W_BIAS, 1), (Kind.W_BIAS, 2), (Kind.W_BIAS, 3))
        self.got((Kind.W_CORE, m))

    def arrived_far(self, m):
        for q in range(2):
            self.got((Kind.W_PASS, m, q), (Kind.W_TURN, m, q))

    def grad(self, m):
        return (self.r.gwo2, self.r.gwi)[m]

    def f_core(self, m, slot):
        self.start((Kind.F_AWAY if slot == 3 else Kind.F_NEAR, m))

    def f_x(self, m):
        r, grad = self.r, self.grad(m)
        self.got((Kind.F_AWAY, m))
        grad[2] = (grad[2].astype(f32) + r.rca[m].astype(f32)).astype(bf16)
        self.start((Kind.F_X, m, 0), (Kind.F_Y, m, 1))

    def f_near(self, m):
        r, grad = self.r, self.grad(m)
        self.got((Kind.F_NEAR, m))
        grad[0] = (grad[0].astype(f32) + r.rcd[m].astype(f32)).astype(bf16)
        self.start((Kind.F_Y_OWN, m, 1))

    def f_own(self, m, h):
        r, grad = self.r, self.grad(m)
        y = self.y
        if h == 0:
            self.got((Kind.F_X, m, 0))
            total = grad[0, 0:256].astype(f32) + r.rx[m, 0:256].astype(f32)
            grad[0, 0:256] = total.astype(bf16)
            self.start((Kind.F_Y, m, 0))
        else:
            self.got((Kind.F_Y, m, 1))
            s = self.span(256 + y * 128, 128)
            grad[2, s] = (grad[2, s].astype(f32) + r.ry[m, 1].astype(f32)).astype(bf16)
            self.start((Kind.F_X, m, 1))

    def f_y(self, m, h):
        r, grad = self.r, self.grad(m)
        s = self.span(h * 256 + self.y * 128, 128)
        if h == 0:
            self.got((Kind.F_Y, m, 0))
            total = grad[0, s].astype(f32) + r.ry[m, 0].astype(f32)
        else:
            self.got((Kind.F_Y_OWN, m, 1), (Kind.F_X, m, 1))
            total = grad[0, s].astype(f32) + r.ry[m, 2].astype(f32) + r.rx[m, 256:384].astype(f32)
        grad[0, s] = total.astype(bf16)
        self.start((Kind.F_NEXT, m, h))

    def f_z(self, m, h):
        r, grad = self.r, self.grad(m)
        self.got((Kind.F_NEXT, m, h))
        s = self.span(h * 256 + self.y * 128 + self.odd * 64, 64)
        grad[0, s] = (grad[0, s].astype(f32) + r.rn[m * 2 + h].astype(f32)).astype(bf16)
        self.start((Kind.F_FAR, m, h))

    def f_zz(self, m, h):
        r, grad = self.r, self.grad(m)
        self.got((Kind.F_FAR, m, h))
        s = self.span(h * 256 + self.y * 128 + self.odd * 64 + self.high * 32, 32)
        r.fout[m, s] = (grad[0, s].astype(f32) + r.rf[m * 2 + h].astype(f32)).astype(bf16)
        self.start((Kind.G_FAR, m, h))

    def f_g(self, m, h):
        self.got((Kind.G_FAR, m, h))
        self.start((Kind.G_Y, m, h), (Kind.G_NEXT, m, h, 0))

    def f_gg(self, m, h):
        self.got((Kind.G_Y, m, h))
        self.start((Kind.G_NEXT, m, h, 1))

    def f_end(self, m, h):
        self.got((Kind.G_NEXT, m, h, 0), (Kind.G_NEXT, m, h, 1))
        self.r.put("f", m * 2 + h)

    def a_core(self, n):
        self.start((Kind.A_CORE, n))

    def a_sum(self, n, level, target=None):
        grad, received, _, keeps = self.parts[n]
        s = keeps[level]()
        total = grad[s].astype(f32) + received[level][...].astype(f32)
        (grad if target is None else target)[s] = total.astype(bf16)

    def a_1(self, n):
        self.got((Kind.A_CORE, n))
        self.a_sum(n, 0)
        self.start((Kind.A_ONE, n))

    def a_2(self, n):
        self.got((Kind.A_ONE, n))
        self.a_sum(n, 1)
        self.start((Kind.A_TWO, n))

    def a_z(self, n):
        self.got((Kind.A_TWO, n))
        self.a_sum(n, 2)
        self.start((Kind.A_NEXT, n))

    def a_zz(self, n):
        self.got((Kind.A_NEXT, n))
        self.a_sum(n, 3)
        self.start((Kind.A_FAR, n))

    def a_g(self, n):
        self.got((Kind.A_FAR, n))
        self.a_sum(n, 4, self.parts[n][2])
        self.start((Kind.B_FAR, n))

    def a_gg(self, n):
        self.got((Kind.B_FAR, n))
        self.start((Kind.B_NEXT, n))

    def a_3(self, n):
        self.got((Kind.B_NEXT, n))
        self.start((Kind.B_TWO, n))

    def a_4(self, n):
        self.got((Kind.B_TWO, n))
        self.start((Kind.B_ONE, n))

    def a_5(self, n):
        self.got((Kind.B_ONE, n))
        self.start((Kind.B_CORE, n))

    def a_end(self, n):
        self.got((Kind.B_CORE, n))
        self.r.put("a", n)

    def v_core(self):
        r = self.r
        x, c = self.x, self.c
        r.vs[0, 0:8] = r.gvec[...]
        r.vs[0, pl.ds(8 + x * 2 + c, 1)] = r.gbi[0]
        r.vs[0, pl.ds(8 + x * 2 + 1 - c, 1)] = r.gbi[1]
        r.vs[0, pl.ds(8 + (1 - x) * 2 + c, 1)] = r.gbi[2]
        r.vs[0, pl.ds(8 + (1 - x) * 2 + 1 - c, 1)] = r.gbi[3]
        self.start((Kind.V_STEP, 0))

    def v_next(self, at):
        r = self.r
        self.got((Kind.V_STEP, at))
        r.vs[at + 1] = r.vs[at] + r.vr[at]
        if at < 4:
            self.start((Kind.V_STEP, at + 1))
        else:
            r.vs[5, 12:13] = r.vs[5, pl.ds(8 + self.w, 1)]
            r.put("v", 0)

    def leave(self):
        for name in self.table:
            if name in self.used:
                self.build(name).wait_send()


def plain_kernel(names, *refs):
    r = Refs(names, refs)
    begin(r, r.x.shape[0])
    layer(r, Quiet())
    r.drain()


ANY = pl.BlockSpec(memory_space=pl.ANY)
IN_VMEM = pl.BlockSpec(memory_space=pltpu.VMEM)
IN_SMEM = pl.BlockSpec(memory_space=pltpu.SMEM)
COST = pl.CostEstimate(
    flops=25 * 10**9, bytes_accessed=30 << 20, transcendentals=12 << 20
)


def plain_layer(operands, count, vectors, wi, bi, wo2):
    tokens, width = operands["x_hbm"].shape
    hidden = wi.shape[0]
    shape = jax.ShapeDtypeStruct
    ins = {name: (value, ANY) for name, value in operands.items()}
    ins.update(count_ref=(count, IN_SMEM))
    ins.update({name: (value, IN_VMEM) for name, value in vectors.items()})
    ins.update(wi=(wi, IN_VMEM), bi=(bi, IN_VMEM), wo2=(wo2, IN_VMEM))
    outs = dict(
        lo_out=(shape((tokens, width), bf16), ANY),
        dual_out=(shape((tokens, width), f32), ANY),
        gx_out=(shape((tokens, width), f32), ANY),
        gw=(shape((2, width, width), bf16), IN_VMEM),
        gqk=(shape((PARTS, width, 2 * width // PARTS), bf16), IN_VMEM),
        gwi=(shape((hidden, width, HALF), bf16), IN_VMEM),
        gwo2=(shape((hidden, HALF, width), bf16), IN_VMEM),
        gvec=(shape((8, width), f32), IN_VMEM),
        gbi=(shape((hidden, 1, HALF), f32), IN_VMEM),
    )
    scratch = scratch_of(tokens, width, hidden)
    scratch["sems"] = pltpu.SemaphoreType.DMA((len(FETCHED) + 4,))
    names = list(ins) + list(outs) + list(scratch)
    return pl.pallas_call(
        functools.partial(plain_kernel, names),
        out_shape=[o[0] for o in outs.values()],
        in_specs=[i[1] for i in ins.values()],
        out_specs=[o[1] for o in outs.values()],
        scratch_shapes=list(scratch.values()),
        compiler_params=pltpu.CompilerParams(vmem_limit_bytes=62 << 20),
        cost_estimate=COST,
    )(*[i[0] for i in ins.values()])


def sort_out(layer_in, dual_in, long_count, w_query, w_key, w_value, w_output, gain_one, shift_one,
             w_in, bias_in, w_out, bias_out, gain_two, shift_two, cot_main, cot_dual):
    operands = dict(
        x_hbm=layer_in, wq_hbm=w_query, wk_hbm=w_key, wv_hbm=w_value, wo_hbm=w_output,
        dual_hbm=dual_in, cm_hbm=cot_main, cd_hbm=cot_dual,
    )
    vectors = dict(
        gain_one=gain_one, shift_one=shift_one, gain_two=gain_two, shift_two=shift_two, bias_out=bias_out
    )
    return operands, long_count, vectors, w_in, bias_in, w_out


def plain_body(*args):
    operands, count, vectors, w_in, bias_in, w_out = sort_out(*args)
    width = w_in.shape[0]
    w_in_all = lax.all_gather(w_in, "wide", axis=1, tiled=True)
    bias_all = lax.all_gather(bias_in, "wide", axis=0, tiled=True)
    w_out_all = lax.all_gather(w_out, "wide", axis=0, tiled=True)
    hidden = w_in_all.shape[1] // HALF
    wi = w_in_all.reshape(width, hidden, HALF).transpose(1, 0, 2)
    wo2 = w_out_all.reshape(hidden, HALF, width)
    bi = bias_all.astype(f32).reshape(hidden, 1, HALF)
    lo, dual, gx, gw, gqk, gwi, gwo2, gvec, gbi = plain_layer(operands, count, vectors, wi, bi, wo2)
    gwi = gwi.transpose(1, 0, 2).reshape(w_in_all.shape)
    gwo2 = gwo2.reshape(w_out_all.shape)
    gwi = lax.psum(lax.psum_scatter(gwi, "wide", scatter_dimension=1, tiled=True), "batch")
    gwo2 = lax.psum(lax.psum_scatter(gwo2, "wide", scatter_dimension=0, tiled=True), "batch")
    gbi = lax.psum_scatter(gbi.reshape(-1), "wide", scatter_dimension=0, tiled=True)
    gbi = lax.psum(gbi, "batch")
    gw, gqk, gvec = lax.psum((gw, gqk, gvec), ("batch", "wide"))
    gw, gqk = gw.astype(f32), gqk.astype(f32)
    part = width // PARTS
    gq = jnp.concatenate(list(gqk[:, :, :part]), axis=1)
    gk = jnp.concatenate(list(gqk[:, :, part:]), axis=1)
    return (lo, dual, gx, gq, gk, gw[1], gw[0], gvec[0], gvec[1], gwi.astype(f32), gbi,
            gwo2.astype(f32), gvec[2], gvec[3], gvec[4])


def steps():
    n = Net
    plan = {}
    plan[(At.ATTEND, 0)] = (
        (n.pass_x, 0, 0),
    )
    plan[(At.ATTEND, 5)] = (
        (n.pass_x, 0, 1),
    )
    plan[(At.ATTEND, 8)] = (
        (n.pass_y, 0, 0),
    )
    plan[(At.HIDDEN,)] = (
        (n.pass_x, 1, 0),
        (n.arrived_near, 0),
    )
    plan[(At.HALVES, 3)] = (
        (n.pass_y, 0, 1),
        (n.pass_x, 1, 1),
    )
    plan[(At.OTHERS,)] = (
        (n.pass_y, 1, 0),
        (n.arrived_far, 0),
    )
    plan[(At.BRANCH,)] = (
        (n.pass_y, 1, 1),
        (n.arrived_near, 1),
        (n.arrived_far, 1),
    )
    plan[(At.OUT, 3)] = (
        (n.f_core, 0, 3),
    )
    plan[(At.OUT, 1)] = (
        (n.f_core, 0, 1),
    )
    plan[(At.PRE, 1)] = (
        (n.f_x, 0),
        (n.f_near, 0),
    )
    plan[(At.IN, 3)] = (
        (n.f_core, 1, 3),
    )
    plan[(At.IN, 1)] = (
        (n.f_core, 1, 1),
    )
    plan[(At.FIRST, 1)] = (
        (n.f_x, 1),
        (n.f_own, 0, 1),
        (n.f_near, 1),
        (n.f_own, 0, 0),
    )
    plan[(At.W_OUTPUT,)] = (
        (n.a_core, 0),
        (n.v_core,),
    )
    plan[(At.VALUES, 1)] = (
        (n.f_own, 1, 1),
    )
    plan[(At.VALUES, 4)] = (
        (n.v_next, 0),
        (n.a_1, 0),
    )
    plan[(At.W_VALUE,)] = (
        (n.a_core, 1),
        (n.f_own, 1, 0),
    )
    plan[(At.SCORES, 1)] = (
        (n.a_1, 1),
        (n.f_y, 0, 0),
        (n.f_y, 0, 1),
    )
    plan[(At.SCORES, 2)] = (
        (n.a_core, 2),
    )
    plan[(At.SCORES, 3)] = (
        (n.a_2, 0),
        (n.f_y, 1, 1),
        (n.v_next, 1),
        (n.a_1, 2),
    )
    plan[(At.SCORES, 4)] = (
        (n.a_core, 3),
        (n.f_z, 0, 0),
    )
    plan[(At.SCORES, 5)] = (
        (n.f_z, 0, 1),
        (n.f_y, 1, 0),
        (n.a_z, 0),
        (n.a_1, 3),
        (n.f_z, 1, 1),
    )
    plan[(At.SCORES, 6)] = (
        (n.a_core, 4),
        (n.a_2, 1),
    )
    plan[(At.SCORES, 7)] = (
        (n.f_zz, 0, 0),
        (n.v_next, 2),
    )
    plan[(At.SCORES, 8)] = (
        (n.a_core, 5),
        (n.a_1, 4),
        (n.a_2, 3),
        (n.a_2, 2),
        (n.a_zz, 0),
        (n.f_zz, 0, 1),
        (n.a_z, 1),
        (n.f_z, 1, 0),
    )
    plan[(At.INPUT, 1)] = (
        (n.f_zz, 1, 1),
        (n.v_next, 3),
        (n.a_1, 5),
    )
    plan[(At.INPUT, 3)] = (
        (n.a_2, 4),
        (n.a_z, 3),
        (n.a_g, 0),
        (n.a_z, 2),
        (n.a_zz, 1),
        (n.f_g, 0, 0),
    )
    plan[(At.END,)] = (
        (n.f_g, 0, 1),
        (n.a_2, 5),
        (n.a_z, 4),
        (n.a_zz, 3),
        (n.f_zz, 1, 0),
        (n.a_zz, 2),
        (n.f_gg, 0, 0),
        (n.f_g, 1, 1),
        (n.f_gg, 0, 1),
        (n.v_next, 4),
        (n.a_z, 5),
        (n.a_gg, 0),
        (n.a_zz, 4),
        (n.a_g, 1),
        (n.a_g, 3),
        (n.f_gg, 1, 1),
        (n.f_g, 1, 0),
        (n.a_g, 2),
        (n.f_end, 0, 0),
        (n.a_g, 4),
        (n.a_gg, 1),
        (n.a_gg, 3),
        (n.f_gg, 1, 0),
        (n.a_gg, 2),
        (n.f_end, 0, 1),
        (n.a_zz, 5),
        (n.a_gg, 4),
        (n.a_3, 0),
        (n.f_end, 1, 1),
        (n.a_g, 5),
        (n.a_4, 0),
        (n.a_3, 1),
        (n.a_3, 3),
        (n.a_gg, 5),
        (n.f_end, 1, 0),
        (n.a_3, 2),
        (n.a_3, 4),
        (n.a_3, 5),
        (n.a_4, 1),
        (n.a_5, 0),
        (n.a_4, 3),
        (n.a_4, 2),
        (n.a_4, 4),
        (n.a_end, 0),
        (n.a_4, 5),
        (n.a_5, 3),
        (n.a_5, 1),
        (n.a_5, 4),
        (n.a_end, 3),
        (n.a_5, 2),
        (n.a_5, 5),
        (n.a_end, 1),
        (n.a_end, 4),
        (n.a_end, 2),
        (n.a_end, 5),
    )
    return plan


COPIES = 144


def tuned_kernel(names, *refs):
    r = Refs(names, refs)
    base = begin(r, r.x.shape[0])
    sems = r.sems
    for u in range(4):
        m, cut = u // 2, slice(u % 2 * 256, u % 2 * 256 + 256)
        r.outs["f", u] = (r.fout.at[m, cut], r.f_out.at[m, cut], sems.at[base + u])
    for n in range(2 + PARTS):
        pair = (r.aout.at[n], r.a_out.at[n]) if n < 2 else (r.qout.at[n - 2], r.q_out.at[n - 2])
        r.outs["a", n] = (*pair, sems.at[base + 4 + n])
    r.outs["v", 0] = (r.vs.at[5], r.v_out, sems.at[base + 6 + PARTS])
    r.fetch("wi", r.wi_hbm, r.wi.at[0], sems.at[base + 7 + PARTS])
    r.fetch("wo2", r.wo2_hbm, r.wo2.at[0], sems.at[base + 8 + PARTS])
    r.bi[0] = jnp.broadcast_to(r.bias_in[...].astype(f32)[None], r.bi.shape[1:])
    net = Net(r, steps())
    net.enter()
    r.wait("wi", "wo2")
    layer(r, net)
    net.leave()
    r.drain()


def tuned_layer(operands, count, vectors, w_in, bias_in, w_out):
    tokens, width = operands["x_hbm"].shape
    hidden = 4
    part = 2 * width // PARTS
    shape = jax.ShapeDtypeStruct
    vmem = pltpu.VMEM
    ins = {name: (value, ANY) for name, value in operands.items()}
    ins.update(count_ref=(count, IN_SMEM))
    ins.update({name: (value, IN_VMEM) for name, value in vectors.items()})
    ins.update(wi_hbm=(w_in, ANY), wo2_hbm=(w_out, ANY), bias_in=(bias_in, IN_VMEM))
    outs = dict(
        lo_out=shape((tokens, width), bf16),
        dual_out=shape((tokens, width), f32),
        gx_out=shape((tokens, width), f32),
        f_out=shape((2, HALF, width), bf16),
        a_out=shape((2, width, width), bf16),
        q_out=shape((PARTS, width, part), bf16),
        v_out=shape((16, width), f32),
    )
    scratch = scratch_of(tokens, width, hidden)
    scratch.update(
        wi=vmem((hidden, width, HALF), bf16),
        wo2=vmem((hidden, HALF, width), bf16),
        bi=vmem((hidden, 8, HALF), f32),
        gw=vmem((2, width, width), bf16),
        gqk=vmem((PARTS, width, part), bf16),
        gwi=vmem((hidden, width, HALF), bf16),
        gwo2=vmem((hidden, HALF, width), bf16),
        gvec=vmem((8, width), f32),
        gbi=vmem((hidden, 1, HALF), f32),
        rca=vmem((2, HALF, width), bf16),
        rcd=vmem((2, HALF, width), bf16),
        rx=vmem((2, 384, width), bf16),
        ry=vmem((2, 3, 128, width), bf16),
        rn=vmem((4, 64, width), bf16),
        rf=vmem((4, 32, width), bf16),
        fout=vmem((2, HALF, width), bf16),
        ac=vmem((2, 256, width), bf16),
        a1=vmem((2, 128, width), bf16),
        a2=vmem((2, 64, width), bf16),
        a3=vmem((2, 32, width), bf16),
        a4=vmem((2, 16, width), bf16),
        aout=vmem((2, width, width), bf16),
        qc=vmem((PARTS, 256, part), bf16),
        q1=vmem((PARTS, 128, part), bf16),
        q2=vmem((PARTS, 64, part), bf16),
        q3=vmem((PARTS, 32, part), bf16),
        q4=vmem((PARTS, 16, part), bf16),
        qout=vmem((PARTS, width, part), bf16),
        vs=vmem((6, 16, width), f32),
        vr=vmem((5, 16, width), f32),
        sems=pltpu.SemaphoreType.DMA((len(FETCHED) + 4 + 9 + PARTS,)),
        send_sem=pltpu.SemaphoreType.DMA((COPIES,)),
        recv_sem=pltpu.SemaphoreType.DMA((COPIES,)),
    )
    names = list(ins) + list(outs) + list(scratch)
    return pl.pallas_call(
        functools.partial(tuned_kernel, names),
        out_shape=list(outs.values()),
        in_specs=[i[1] for i in ins.values()],
        out_specs=[ANY] * len(outs),
        scratch_shapes=list(scratch.values()),
        compiler_params=pltpu.CompilerParams(
            vmem_limit_bytes=int(63.5 * 2**20), collective_id=0, has_side_effects=True
        ),
        cost_estimate=COST,
    )(*[i[0] for i in ins.values()])


def widen_kernel(lo, dual, gx, f, a, q, v, lo_out, dual_out, gx_out, gq, gk, gv, go, gwi, gwo,
                 gg1, gs1, gbi, gbo, gg2, gs2, f_low, a_low, q_low, lo_held, dual_held, gx_held, wide, sems):
    loads = ((f, f_low), (a, a_low), (q, q_low), (dual, dual_held), (gx, gx_held), (lo, lo_held))
    copies = []
    for at, (source, target) in enumerate(loads):
        copies.append(pltpu.make_async_copy(source, target, sems.at[at]))
        copies[at].start()
    for at, out in enumerate((gg1, gs1, gbo, gg2, gs2)):
        out[...] = v[at]
    gbi[...] = v[12]
    outs = []

    def send(source, target):
        copy = pltpu.make_async_copy(source, target, sems.at[6 + len(outs)])
        copy.start()
        outs.append(copy)

    copies[0].wait()
    wide[0] = f_low[0].astype(f32)
    send(wide.at[0], gwo)
    wide[1] = f_low[1].astype(f32)
    send(wide.at[1], gwi)
    copies[1].wait()
    wide[2] = a_low[0].astype(f32)
    send(wide.at[2], go)
    wide[3] = a_low[1].astype(f32)
    send(wide.at[3], gv)
    copies[2].wait()
    part = q.shape[2] // 2
    for at, target in ((4, gq), (5, gk)):
        for p in range(PARTS):
            wide[at, :, p * part : (p + 1) * part] = q_low[p, :, (at - 4) * part : (at - 3) * part].astype(f32)
        send(wide.at[at], target)
    for at, source, target in ((3, dual_held, dual_out), (4, gx_held, gx_out), (5, lo_held, lo_out)):
        copies[at].wait()
        send(source, target)
    for copy in outs:
        copy.wait()


def widen(lo, dual, gx, f, a, q, v):
    width = f.shape[2]
    shape = jax.ShapeDtypeStruct
    matrix = (shape((width, width), f32), ANY)
    vector = (shape((width,), f32), IN_VMEM)
    outs = [(shape(t.shape, t.dtype), ANY) for t in (lo, dual, gx)] + [matrix] * 6 + [vector] * 6
    return pl.pallas_call(
        widen_kernel,
        out_shape=[o[0] for o in outs],
        in_specs=[ANY] * 6 + [IN_VMEM],
        out_specs=[o[1] for o in outs],
        scratch_shapes=[
            pltpu.VMEM(f.shape, bf16),
            pltpu.VMEM(a.shape, bf16),
            pltpu.VMEM(q.shape, bf16),
            *[pltpu.VMEM(t.shape, t.dtype) for t in (lo, dual, gx)],
            pltpu.VMEM((6, width, width), f32),
            pltpu.SemaphoreType.DMA((15,)),
        ],
        compiler_params=pltpu.CompilerParams(vmem_limit_bytes=int(63.5 * 2**20)),
        cost_estimate=pl.CostEstimate(flops=0, bytes_accessed=19 << 20, transcendentals=0),
    )(lo, dual, gx, f, a, q, v)


def tuned_body(*args):
    (lo, dual, gx, gq, gk, gv, go, gwi, gwo, gg1, gs1, gbi, gbo, gg2, gs2) = widen(*tuned_layer(*sort_out(*args)))
    return lo, dual, gx, gq, gk, gv, go, gg1, gs1, gwi, gbi, gwo, gbo, gg2, gs2


def solution(mesh):
    tokens = P(("batch", "wide"), None)
    fits = mesh.shape["batch"] == 8 and mesh.shape["wide"] == 4
    return jax.shard_map(
        tuned_body if fits else plain_body,
        mesh=mesh,
        in_specs=(tokens, tokens, P(("batch", "wide")), P(), P(), P(), P(), P(), P(), P(None, "wide"), P("wide"),
                  P("wide", None), P(), P(), P(), tokens, tokens),
        out_specs=(tokens, tokens, tokens, P(), P(), P(), P(), P(), P(), P(None, "wide"), P("wide"),
                   P("wide", None), P(), P(), P()),
        check_vma=False,
    )
```

```python
import functools

import jax
import jax.numpy as jnp
from jax import lax
from jax.experimental import pallas as pl
from jax.experimental.pallas import tpu as pltpu
from jax.sharding import PartitionSpec as P

HEADS = 8
HEAD_DIM = 64
EPSILON = 1e-05
MASKED = -1000000000.0
BLOCK = 256
HALF = 512
PARTS = 4
PRE_UNROLL = 1
HALF_UNROLL = NORM_UNROLL = SECOND_UNROLL = FIRST_UNROLL = INPUT_UNROLL = 2
CORE, X, Y, NEXT, FAR, ZED, WIDE, BATCH = range(8)
UNITS = (
    (0, 0, 256, (Y, X, ZED)),
    (0, 256, 256, (X, NEXT, FAR, Y)),
    (1, 0, 256, (NEXT, Y, X, FAR)),
    (1, 256, 256, (FAR, X, Y, NEXT)),
)
CHUNKS = (
    (CORE, X, Y, ZED),
    (CORE, X, Y, ZED),
    (CORE, ZED, X, Y),
    (CORE, Y, ZED, X),
    (CORE, Y, X, ZED),
    (WIDE, Y, ZED),
)

bf16 = jnp.bfloat16
f32 = jnp.float32


def contract(left, right, a, b):
    return lax.dot_general(
        left, right, (((a,), (b,)), ((), ())), preferred_element_type=f32
    )


def dot_nn(left, right):
    return contract(left, right, 1, 0)


def dot_nt(left, right):
    return contract(left, right, 1, 1)


def dot_tn(left, right):
    return contract(left, right, 0, 0)


def dot_tt(left, right):
    return contract(left, right, 0, 1)


def span_of(at, size):
    if isinstance(at, int):
        return slice(at * size, (at + 1) * size)
    return pl.ds(pl.multiple_of(at * size, size), size)


def rows_of(block):
    return span_of(block, BLOCK)


def head_of(head):
    return span_of(head, HEAD_DIM)


def split(block):
    return block // 2, span_of(block % 2, BLOCK)


def each(count, step, unroll=1):
    def several(at, _):
        for k in range(unroll):
            step(at * unroll + k)
        return 0

    lax.fori_loop(0, count // unroll, several, 0)


def row_mean(value):
    return jnp.mean(value, axis=-1, keepdims=True)


def col_sum(value):
    return jnp.sum(value, axis=0, keepdims=True)


def joined(value):
    return value.reshape(value.shape[0] * value.shape[1], value.shape[2])


def layer(r, net):
    tokens, width = r.x.shape
    blocks = tokens // BLOCK
    hidden = r.wi.shape[0]
    slots = tuple(range(hidden))

    r.wait("x", "wq", "wk", "wv")
    for block in range(blocks):
        cols = rows_of(block)
        xb = r.x[cols]
        r.qt[:, cols] = (dot_tt(r.wq[...], xb) * HEAD_DIM**-0.5).astype(bf16)
        r.kt[:, cols] = dot_tt(r.wk[...], xb).astype(bf16)
        r.vt[:, cols] = dot_tt(r.wv[...], xb).astype(bf16)
    net.tick(At.PROJECT)

    row_at = lax.broadcasted_iota(jnp.int32, (BLOCK, BLOCK), 0)
    col_at = lax.broadcasted_iota(jnp.int32, (BLOCK, BLOCK), 1)
    causal = row_at <= col_at
    away = jnp.where(r.count > 0, 0.0, 2e9).astype(f32)

    def soften(head, qb):
        hs = head_of(head)
        query = r.qt[hs, rows_of(qb)]
        parts = []
        peak_off = None
        for tb in range(qb + 1):
            scores = dot_tn(r.kt[hs, rows_of(tb)], query)
            if tb == qb:
                scores = jnp.where(causal, scores, MASKED)
            parts.append(scores)
            peak = jnp.max(scores, axis=0, keepdims=True)
            if tb < qb:
                peak_off = peak if peak_off is None else jnp.maximum(peak_off, peak)
        if peak_off is not None:
            peak = jnp.maximum(peak, peak_off - away)
        total = jnp.zeros((1, BLOCK), f32)
        for tb in range(qb + 1):
            expo = jnp.exp(parts[tb] - (peak if tb == qb else peak + away))
            total += jnp.sum(expo, axis=0, keepdims=True)
            r.p[qb][head, rows_of(tb)] = expo.astype(bf16)
        r.inv_total[pl.ds(head, 1), rows_of(qb)] = 1.0 / total

    def mix(head, qb):
        hs = head_of(head)
        mixed = dot_nn(r.vt[hs, : (qb + 1) * BLOCK], r.p[qb][head])
        mixed *= r.inv_total[pl.ds(head, 1), rows_of(qb)]
        r.mt[hs, rows_of(qb)] = mixed.astype(bf16)

    for head in range(HEADS + 1):
        for qb in range(blocks):
            if head < HEADS:
                soften(head, qb)
            if head > 0:
                mix(head - 1, qb)
        net.tick(At.ATTEND, head)

    r.wait("wo", "dual")
    gain_one, shift_one = r.gain_one[...][None], r.shift_one[...][None]

    def norm_block(block):
        rows = rows_of(block)
        attended = dot_tn(r.mt[:, rows], r.wo[...])
        r.dual[rows] += attended
        hidden_one = r.x[rows].astype(f32) + attended
        centre = hidden_one - row_mean(hidden_one)
        inverse = lax.rsqrt(row_mean(centre * centre) + EPSILON)
        normed = centre * inverse
        r.n1[rows] = normed
        r.i1[rows] = inverse
        r.fl[rows] = (normed * gain_one + shift_one).astype(bf16)

    each(blocks, norm_block, NORM_UNROLL)

    def half_block(block, pair, place):
        first_low = r.fl[rows_of(block)]
        th, rows = split(block)
        for j in pair:
            pre = dot_nn(first_low, r.wi[j]) + r.bi[j, 0:1]
            phi = 0.5 + 0.5 * lax.erf(pre * 0.7071067811865476)
            bell = jnp.exp(-0.5 * pre * pre) * 0.3989422804014327
            r.act[j, th, rows] = (pre * phi).astype(bf16)
            r.slope[j, th, rows] = (phi + pre * bell).astype(bf16)
        net.loop_tick(place, block, blocks)

    net.tick(At.HIDDEN)
    each(blocks, lambda block: half_block(block, slots[:2], At.HALVES), HALF_UNROLL)
    net.tick(At.OTHERS)
    each(blocks, lambda block: half_block(block, slots[2:], At.HALVES2), HALF_UNROLL)

    r.wait("cm", "cd")
    net.tick(At.BRANCH)
    gain_two, shift_two = r.gain_two[...][None], r.shift_two[...][None]
    bias_out = r.bias_out[...][None]
    r.gvec[...] = jnp.zeros_like(r.gvec)

    def second_block(block):
        rows = rows_of(block)
        th, cut = split(block)
        branch = dot_nn(r.act[0, th, cut], r.wo2[0])
        for j in slots[1:]:
            branch += dot_nn(r.act[j, th, cut], r.wo2[j])
        branch += bias_out
        r.dual[rows] += branch
        hidden_two = r.n1[rows] * gain_one + shift_one + branch
        centre = hidden_two - row_mean(hidden_two)
        inverse = lax.rsqrt(row_mean(centre * centre) + EPSILON)
        normed = centre * inverse
        r.gwi[th, cut] = (normed * gain_two + shift_two).astype(bf16)
        grad = r.cm[rows]
        r.gvec[3:4] += col_sum(grad * normed)
        r.gvec[4:5] += col_sum(grad)
        scaled = grad * gain_two
        g_sum = inverse * (
            scaled - row_mean(scaled) - normed * row_mean(scaled * normed)
        )
        r.cm[rows] = g_sum
        g_branch = (g_sum + r.cd[rows]).astype(bf16)
        r.gb[rows] = g_branch
        r.gvec[2:3] += col_sum(g_branch.astype(f32))

    each(blocks, second_block, SECOND_UNROLL)
    r.put("lo", 0)
    r.put("lo", 1)
    r.put("dual", 0)

    for j in reversed(slots):
        r.gwo2[j] = dot_tn(joined(r.act[j]), r.gb[...]).astype(bf16)
        net.tick(At.OUT, j)
    r.gbi[...] = jnp.zeros_like(r.gbi)

    def pre_block(block):
        g_branch = r.gb[rows_of(block)]
        th, rows = split(block)
        for j in slots:
            g_act = dot_nt(g_branch, r.wo2[j])
            g_pre = (g_act * r.slope[j, th, rows].astype(f32)).astype(bf16)
            r.slope[j, th, rows] = g_pre
            r.gbi[j] += col_sum(g_pre.astype(f32))
        net.loop_tick(At.PRE, block, blocks)

    each(blocks, pre_block, PRE_UNROLL)
    r.finished("lo")
    for j in reversed(slots):
        r.gwi[j] = dot_tn(r.fl[...], joined(r.slope[j])).astype(bf16)
        net.tick(At.IN, j)

    def first_block(block):
        rows = rows_of(block)
        th, cut = split(block)
        g_first = dot_nt(r.slope[0, th, cut], r.wi[0])
        for j in slots[1:]:
            g_first += dot_nt(r.slope[j, th, cut], r.wi[j])
        g_first += r.cm[rows]
        normed = r.n1[rows]
        r.gvec[0:1] += col_sum(g_first * normed)
        r.gvec[1:2] += col_sum(g_first)
        scaled = g_first * gain_one
        g_resid = r.i1[rows] * (
            scaled - row_mean(scaled) - normed * row_mean(scaled * normed)
        )
        r.cm[rows] = g_resid
        g_att = (g_resid + r.cd[rows]).astype(bf16)
        r.gb[rows] = g_att
        g_mixed = dot_nt(r.wo[...], g_att)
        g_mixed = g_mixed.reshape(HEADS, HEAD_DIM, BLOCK) * r.inv_total[:, rows][:, None]
        g_mixed = g_mixed.reshape(width, BLOCK).astype(bf16)
        r.act[3, th, :, cut] = g_mixed
        centred = g_mixed.astype(f32) * r.mt[:, rows].astype(f32)
        r.centred[:, rows] = jnp.sum(centred.reshape(HEADS, HEAD_DIM, BLOCK), axis=1)
        net.loop_tick(At.FIRST, block, blocks)

    each(blocks, first_block, FIRST_UNROLL)
    r.gw[0] = dot_nn(r.mt[...], r.gb[...]).astype(bf16)
    net.tick(At.W_OUTPUT)
    for th in range(2):
        r.slope[0, th] = r.x[th * HALF : (th + 1) * HALF].T

    def columns(which, head, block):
        th, cut = split(block)
        return which, th, head_of(head), cut

    def back_values(head, tb):
        total = None
        for qb in range(tb, blocks):
            part = dot_nt(r.act[columns(3, head, qb)], r.p[qb][head, rows_of(tb)])
            total = part if total is None else total + part
        r.act[columns(2, head, tb)] = total.astype(bf16)

    def back_scores(head, qb, slot):
        got = r.act[columns(3, head, qb)]
        centred = r.centred[pl.ds(head, 1), rows_of(qb)]
        for tb in range(qb + 1):
            g_probs = dot_tn(r.vt[head_of(head), rows_of(tb)], got)
            probs = r.p[qb][head, rows_of(tb)].astype(f32)
            slot[qb][rows_of(tb)] = (probs * (g_probs - centred)).astype(bf16)

    def back_query(head, qb, slot):
        g_query = dot_nn(r.kt[head_of(head), : (qb + 1) * BLOCK], slot[qb][...])
        r.act[columns(0, head, qb)] = (g_query * HEAD_DIM**-0.5).astype(bf16)

    def back_keys(head, tb, slot):
        total = None
        for qb in range(tb, blocks):
            part = dot_nt(r.qt[head_of(head), rows_of(qb)], slot[qb][rows_of(tb)])
            total = part if total is None else total + part
        r.act[columns(1, head, tb)] = total.astype(bf16)

    def against_x(which, rows):
        total = dot_nt(r.slope[0, 0], r.act[which, 0, rows])
        return (total + dot_nt(r.slope[0, 1], r.act[which, 1, rows])).astype(bf16)

    for head in range(HEADS):
        for tb in range(blocks):
            back_values(head, tb)
        net.tick(At.VALUES, head)
    r.gw[1] = against_x(2, slice(0, width))
    net.tick(At.W_VALUE)
    size = HEADS // PARTS
    part_width = size * HEAD_DIM

    for head in range(HEADS + 1):
        for block in range(blocks):
            if head < HEADS:
                back_scores(head, block, r.gs[head % 2])
            if head > 0:
                back_query(head - 1, block, r.gs[(head - 1) % 2])
                back_keys(head - 1, block, r.gs[(head - 1) % 2])
        if head > 0 and head % size == 0:
            part = head // size - 1
            rows = span_of(part, part_width)
            r.gqk[part, :, :part_width] = against_x(0, rows)
            r.gqk[part, :, part_width:] = against_x(1, rows)
        net.tick(At.SCORES, head)

    def input_block(block):
        rows = rows_of(block)
        th, cut = split(block)
        grad = dot_tt(r.act[0, th, :, cut], r.wq[...])
        grad += dot_tt(r.act[1, th, :, cut], r.wk[...])
        grad += dot_tt(r.act[2, th, :, cut], r.wv[...])
        r.cm[rows] += grad
        net.loop_tick(At.INPUT, block, blocks)

    each(blocks, input_block, INPUT_UNROLL)
    r.put("cm", 0)
    net.tick(At.END)


class Refs:
    def __init__(self, names, refs):
        self.__dict__.update(zip(names, refs))
        self.pending = {}
        self.out = {}

    def fetch(self, name, source, target, sem):
        copy = pltpu.make_async_copy(source, target, sem)
        copy.start()
        self.pending[name] = copy

    def wait(self, *names):
        for name in names:
            self.pending.pop(name).wait()

    def put(self, name, at):
        source, target, sem = self.outs[name, at]
        copy = pltpu.make_async_copy(source, target, sem)
        copy.start()
        self.out[name, at] = copy

    def finished(self, name):
        for key in [key for key in self.out if key[0] == name]:
            self.out.pop(key).wait()

    def drain(self):
        for copy in self.out.values():
            copy.wait()


FETCHED = ("x", "wq", "wk", "wv", "wo", "dual", "cm", "cd")


def scratch_of(tokens, width, hidden):
    vmem = pltpu.VMEM
    wide = (hidden, tokens // HALF, HALF, HALF)
    names = dict(
        x=vmem((tokens, width), bf16),
        wq=vmem((width, width), bf16),
        wk=vmem((width, width), bf16),
        wv=vmem((width, width), bf16),
        wo=vmem((width, width), bf16),
        dual=vmem((tokens, width), f32),
        cm=vmem((tokens, width), f32),
        cd=vmem((tokens, width), f32),
        qt=vmem((width, tokens), bf16),
        kt=vmem((width, tokens), bf16),
        vt=vmem((width, tokens), bf16),
        mt=vmem((width, tokens), bf16),
        inv_total=vmem((HEADS, tokens), f32),
        centred=vmem((HEADS, tokens), f32),
        n1=vmem((tokens, width), f32),
        i1=vmem((tokens, 1), f32),
        fl=vmem((tokens, width), bf16),
        act=vmem(wide, bf16),
        slope=vmem(wide, bf16),
        gb=vmem((tokens, width), bf16),
    )
    for qb in range(tokens // BLOCK):
        names[f"p{qb}"] = vmem((HEADS, (qb + 1) * BLOCK, BLOCK), bf16)
        names[f"g{qb}"] = vmem(((qb + 1) * BLOCK, BLOCK), bf16)
        names[f"h{qb}"] = vmem(((qb + 1) * BLOCK, BLOCK), bf16)
    return names


def begin(r, tokens):
    blocks = tokens // BLOCK
    r.count = r.count_ref[0]
    r.p = [getattr(r, f"p{qb}") for qb in range(blocks)]
    r.gs = [[getattr(r, f"{s}{qb}") for qb in range(blocks)] for s in "gh"]
    for at, name in enumerate(FETCHED):
        r.fetch(name, getattr(r, name + "_hbm"), getattr(r, name), r.sems.at[at])
    base = len(FETCHED)
    r.outs = {
        ("lo", 0): (r.gwi.at[0], r.lo_out.at[0:HALF], r.sems.at[base]),
        ("lo", 1): (r.gwi.at[1], r.lo_out.at[HALF : 2 * HALF], r.sems.at[base + 1]),
        ("dual", 0): (r.dual, r.dual_out, r.sems.at[base + 2]),
        ("cm", 0): (r.cm, r.gx_out, r.sems.at[base + 3]),
    }
    return base + 4


class Quiet:
    def tick(self, *place):
        pass

    def loop_tick(self, place, at, count):
        pass


class At:
    (PROJECT, ATTEND, HIDDEN, HALVES, OTHERS, HALVES2, BRANCH, OUT, PRE, IN, FIRST, W_OUTPUT,
     VALUES, W_VALUE, SCORES, INPUT, END) = range(17)


class Kind:
    (W_X, W_Y, W_CORE, W_PASS, W_TURN, W_BIAS, F_CORE, F_AWAY, F_OWN, F_BACK, A_OUT, A_BACK,
     V_STEP) = range(13)


class Net:
    def __init__(self, r, plan):
        self.r = r
        self.plan = plan
        b, w = lax.axis_index("batch"), lax.axis_index("wide")
        z, y, x, c = b // 2, b % 2, w // 2, w % 2
        self.y, self.x, self.c, self.w = y, x, c, w
        self.core = (b, x * 2 + 1 - c)
        self.ex = (b, (1 - x) * 2 + c)
        self.diagonal = (b, (1 - x) * 2 + 1 - c)
        self.why = (z * 2 + 1 - y, w)
        self.odd, self.high = z % 2, z // 2
        self.next = ((z + 1 - 2 * self.odd) * 2 + y, w)
        self.far = (((z + 2) % 4) * 2 + y, w)
        self.table = {}
        self.used = set()
        def pair(peer, bit):
            return bit, 2, [(peer, 1 - bit)]

        self.axes = (
            pair(self.core, c),
            pair(self.ex, x),
            pair(self.why, y),
            pair(self.next, self.odd),
            pair(self.far, self.high),
            (z, 4, [(((z + k) % 4 * 2 + y, w), (z + k) % 4) for k in (1, 2, 3)]),
            (w, 4, [(to, to[1]) for to in (self.core, self.ex, self.diagonal)]),
            (b, 8, [(((b + k) % 8, w), (b + k) % 8) for k in range(1, 8)]),
        )
        self.units = []
        self.parts = []
        self.describe()

    def copy(self, name, to, source, target):
        self.table[name] = (len(self.table), to, source, target)

    def build(self, name):
        index, to, source, target = self.table[name]
        return pltpu.make_async_remote_copy(
            src_ref=source(),
            dst_ref=target(),
            send_sem=self.r.send_sem.at[index],
            recv_sem=self.r.recv_sem.at[index],
            device_id=to,
            device_id_type=pl.DeviceIdType.MESH,
        )

    def start(self, *names):
        for name in names:
            self.used.add(name)
            self.build(name).start()

    def got(self, *names):
        for name in names:
            self.build(name).wait_recv()

    def tick(self, *place):
        for event, *args in self.plan.get(place, ()):
            event(self, *args)

    def loop_tick(self, place, at, count):
        for k in range(count):
            if self.plan.get((place, k)):
                self.guard(at, k, place)

    def guard(self, at, k, place):
        if isinstance(at, int):
            if at == k:
                self.tick(place, k)
        else:
            pl.when(at == k)(functools.partial(self.tick, place, k))

    def cut(self, base, size, mine, peers):
        keep = lambda: self.span(base() + mine * size, size)
        gives = [lambda at=at: self.span(base() + at * size, size) for _, at in peers]
        return keep, gives, lambda: base() + mine * size

    def group(self, act, *name):
        k = 0
        while (*name, k) in self.table:
            act((*name, k))
            k += 1
        return k

    def span(self, start, size):
        return pl.ds(pl.multiple_of(start, size), size)

    def describe(self):
        r, copy, span = self.r, self.copy, self.span
        own = (r.wi_hbm, r.wo2_hbm)
        held = (r.wi, r.wo2)
        for m in range(2):
            copy((Kind.W_CORE, m), self.core, lambda m=m: own[m], lambda m=m: held[m].at[1])
            for q, (mine, other) in enumerate(self.slices(m)):
                copy((Kind.W_X, m, q), self.ex, lambda m=m, f=mine: own[m].at[f()], lambda m=m, f=mine: held[m].at[2, f()])
                copy((Kind.W_PASS, m, q), self.core, lambda m=m, f=mine: held[m].at[2, f()], lambda m=m, f=mine: held[m].at[3, f()])
                if other is not None:
                    copy((Kind.W_Y, m, q), self.why, lambda m=m, f=mine: held[m].at[2, f()], lambda m=m, f=mine: held[m].at[2, f()])
                    copy((Kind.W_TURN, m, q), self.core, lambda m=m, f=other: held[m].at[2, f()], lambda m=m, f=other: held[m].at[3, f()])
        for slot, to in ((1, self.core), (2, self.ex), (3, self.diagonal)):
            copy((Kind.W_BIAS, slot), to, lambda: r.bi.at[0], lambda slot=slot: r.bi.at[slot])

        for m in range(2):
            for slot in (3, 1):
                received = r.rca if slot == 3 else r.rcd
                copy((Kind.F_CORE, m, slot), self.core, lambda m=m, s=slot: self.grad(m).at[s], lambda m=m, t=received: t.at[m])
        for u, (m, start, size, order) in enumerate(UNITS):
            grad, out = self.grad(m), r.fout.at[m]
            base = lambda f=start: f
            both, offset, levels, back = True, 0, [], []
            for level, axis in enumerate(order):
                mine, parts, peers = self.axes[axis]
                if axis == X:
                    both = False
                    keep = lambda f=base, s=size: span(f(), s)
                    gives = [keep]
                else:
                    size //= parts
                    keep, gives, base = self.cut(base, size, mine, peers)
                    back.append((axis, keep))
                landing = [[], []]
                for k, (to, _) in enumerate(peers):
                    for slot, kind, wanted in ((2, Kind.F_AWAY, both or axis == X), (0, Kind.F_OWN, axis != X)):
                        if wanted:
                            target = r.rf.at[u, offset : offset + size]
                            offset += size
                            landing[slot // 2].append(target)
                            copy((kind, u, level, k), to, lambda g=grad, s=slot, f=gives[k]: g.at[s, f()], lambda t=target: t)
                levels.append((axis, keep, landing))
            for step, (axis, keep) in enumerate(reversed(back)):
                for k, (to, _) in enumerate(self.axes[axis][2]):
                    copy((Kind.F_BACK, u, step, k), to, lambda o=out, f=keep: o.at[f()], lambda o=out, f=keep: o.at[f()])
            self.units.append((m, levels))

        for n in range(2 + PARTS):
            if n < 2:
                grad, received, out = r.gw.at[n], r.ra.at[n], r.aout.at[n]
            else:
                grad, received, out = r.gqk.at[n - 2], r.rq.at[n - 2], r.qout.at[n - 2]
            size = grad.shape[0]
            base = lambda: 0
            offset, levels = 0, []
            for level, axis in enumerate(CHUNKS[n]):
                mine, parts, peers = self.axes[axis]
                size //= parts
                keep, gives, base = self.cut(base, size, mine, peers)
                landing = []
                for k, (to, _) in enumerate(peers):
                    target = received.at[offset : offset + size]
                    offset += size
                    landing.append(target)
                    copy((Kind.A_OUT, n, level, k), to, lambda g=grad, f=gives[k]: g.at[f()], lambda t=target: t)
                    copy((Kind.A_BACK, n, level, k), to, lambda o=out, f=keep: o.at[f()], lambda o=out, f=keep: o.at[f()])
                levels.append((keep, landing))
            self.parts.append((grad, out, levels))

        for at, to in enumerate((self.core, self.ex, self.why, self.next, self.far)):
            copy((Kind.V_STEP, at), to, lambda at=at: r.vs.at[at], lambda at=at: r.vr.at[at])

    def enter(self):
        barrier = pltpu.get_barrier_semaphore()
        peers = [to for axis in (WIDE, BATCH) for to, _ in self.axes[axis][2]]
        for peer in peers:
            pl.semaphore_signal(barrier, inc=1, device_id=peer, device_id_type=pl.DeviceIdType.MESH)
        pl.semaphore_wait(barrier, len(peers))
        for slot in (1, 2, 3):
            self.start((Kind.W_BIAS, slot))
        for m in range(2):
            self.group(self.start, Kind.W_X, m)
        self.start((Kind.W_CORE, 0), (Kind.W_CORE, 1))

    def slices(self, m):
        y = self.y
        if m == 0:
            for q in range(4):
                yield (lambda q=q: self.span(y * 256 + q * 64, 64)), (lambda q=q: self.span((1 - y) * 256 + q * 64, 64))
        else:
            yield (lambda: self.span(y * 256, 128)), (lambda: self.span((1 - y) * 256, 128))
            for row in (128, 384):
                yield (lambda row=row: self.span(row, 128)), None

    def pass_x(self, m, q):
        self.got((Kind.W_X, m, q))
        if (Kind.W_Y, m, q) in self.table:
            self.start((Kind.W_Y, m, q))
        self.start((Kind.W_PASS, m, q))

    def pass_y(self, m, q):
        self.got((Kind.W_Y, m, q))
        self.start((Kind.W_TURN, m, q))

    def arrived_near(self, m):
        if m == 0:
            self.got((Kind.W_BIAS, 1), (Kind.W_BIAS, 2), (Kind.W_BIAS, 3))
        self.got((Kind.W_CORE, m))

    def arrived_far(self, m):
        self.group(self.got, Kind.W_PASS, m)
        self.group(self.got, Kind.W_TURN, m)

    def grad(self, m):
        return (self.r.gwo2, self.r.gwi)[m]

    def f_core(self, m, slot):
        self.start((Kind.F_CORE, m, slot))

    def f_begin(self, kind, m):
        for u, unit in enumerate(self.units):
            if unit[0] == m:
                self.group(self.start, kind, u, 0)

    def f_x(self, m):
        self.got((Kind.F_CORE, m, 3))
        grad = self.grad(m)
        grad[2] = grad[2] + self.r.rca[m]
        self.f_begin(Kind.F_AWAY, m)

    def f_near(self, m):
        self.got((Kind.F_CORE, m, 1))
        grad = self.grad(m)
        grad[0] = grad[0] + self.r.rcd[m]
        self.f_begin(Kind.F_OWN, m)

    def plus(self, total, landing):
        if len(landing) == 1:
            return total + landing[0][...]
        total = total.astype(f32)
        for part in landing:
            total += part[...].astype(f32)
        return total.astype(bf16)

    def f_step(self, u, level):
        m, levels = self.units[u]
        grad = self.grad(m)
        axis, keep, (landing_own, landing_away) = levels[level]
        s = keep()
        if landing_away:
            self.group(self.got, Kind.F_AWAY, u, level)
            if axis != X:
                grad[2, s] = self.plus(grad[2, s], landing_away)
        if landing_own:
            self.group(self.got, Kind.F_OWN, u, level)
        total = self.plus(grad[0, s], landing_away if axis == X else landing_own)
        if level == len(levels) - 1:
            self.r.fout[m, s] = total
            self.group(self.start, Kind.F_BACK, u, 0)
        else:
            grad[0, s] = total
            self.group(self.start, Kind.F_AWAY, u, level + 1)
            self.group(self.start, Kind.F_OWN, u, level + 1)

    def f_back(self, u, step):
        self.group(self.got, Kind.F_BACK, u, step)
        if not self.group(self.start, Kind.F_BACK, u, step + 1):
            self.r.put("f", u)

    def a_core(self, n):
        self.group(self.start, Kind.A_OUT, n, 0)

    def a_step(self, n, level):
        grad, out, levels = self.parts[n]
        self.group(self.got, Kind.A_OUT, n, level)
        keep, landing = levels[level]
        s = keep()
        total = self.plus(grad[s], landing)
        if level + 1 < len(levels):
            grad[s] = total
            self.group(self.start, Kind.A_OUT, n, level + 1)
        else:
            out[s] = total
            self.group(self.start, Kind.A_BACK, n, level)

    def a_back(self, n, level):
        self.group(self.got, Kind.A_BACK, n, level)
        if level:
            self.group(self.start, Kind.A_BACK, n, level - 1)
        else:
            self.r.put("a", n)

    def v_core(self):
        r = self.r
        x, c = self.x, self.c
        r.vs[0, 0:8] = r.gvec[...]
        r.vs[0, pl.ds(8 + x * 2 + c, 1)] = r.gbi[0]
        r.vs[0, pl.ds(8 + x * 2 + 1 - c, 1)] = r.gbi[1]
        r.vs[0, pl.ds(8 + (1 - x) * 2 + c, 1)] = r.gbi[2]
        r.vs[0, pl.ds(8 + (1 - x) * 2 + 1 - c, 1)] = r.gbi[3]
        self.start((Kind.V_STEP, 0))

    def v_next(self, at):
        r = self.r
        self.got((Kind.V_STEP, at))
        r.vs[at + 1] = r.vs[at] + r.vr[at]
        if at < 4:
            self.start((Kind.V_STEP, at + 1))
        else:
            r.vs[5, 12:13] = r.vs[5, pl.ds(8 + self.w, 1)]
            r.put("v", 0)

    def leave(self):
        for name in self.table:
            if name in self.used:
                self.build(name).wait_send()


def plain_kernel(names, *refs):
    r = Refs(names, refs)
    begin(r, r.x.shape[0])
    layer(r, Quiet())
    r.drain()


ANY = pl.BlockSpec(memory_space=pl.ANY)
IN_VMEM = pl.BlockSpec(memory_space=pltpu.VMEM)
IN_SMEM = pl.BlockSpec(memory_space=pltpu.SMEM)
COST = pl.CostEstimate(
    flops=25 * 10**9, bytes_accessed=30 << 20, transcendentals=12 << 20
)


def plain_layer(operands, count, vectors, wi, bi, wo2):
    tokens, width = operands["x_hbm"].shape
    hidden = wi.shape[0]
    shape = jax.ShapeDtypeStruct
    ins = {name: (value, ANY) for name, value in operands.items()}
    ins.update(count_ref=(count, IN_SMEM))
    ins.update({name: (value, IN_VMEM) for name, value in vectors.items()})
    ins.update(wi=(wi, IN_VMEM), bi=(bi, IN_VMEM), wo2=(wo2, IN_VMEM))
    outs = dict(
        lo_out=(shape((tokens, width), bf16), ANY),
        dual_out=(shape((tokens, width), f32), ANY),
        gx_out=(shape((tokens, width), f32), ANY),
        gw=(shape((2, width, width), bf16), IN_VMEM),
        gqk=(shape((PARTS, width, 2 * width // PARTS), bf16), IN_VMEM),
        gwi=(shape((hidden, width, HALF), bf16), IN_VMEM),
        gwo2=(shape((hidden, HALF, width), bf16), IN_VMEM),
        gvec=(shape((8, width), f32), IN_VMEM),
        gbi=(shape((hidden, 1, HALF), f32), IN_VMEM),
    )
    scratch = scratch_of(tokens, width, hidden)
    scratch["sems"] = pltpu.SemaphoreType.DMA((len(FETCHED) + 4,))
    names = list(ins) + list(outs) + list(scratch)
    return pl.pallas_call(
        functools.partial(plain_kernel, names),
        out_shape=[o[0] for o in outs.values()],
        in_specs=[i[1] for i in ins.values()],
        out_specs=[o[1] for o in outs.values()],
        scratch_shapes=list(scratch.values()),
        compiler_params=pltpu.CompilerParams(vmem_limit_bytes=62 << 20),
        cost_estimate=COST,
    )(*[i[0] for i in ins.values()])


def sort_out(layer_in, dual_in, long_count, w_query, w_key, w_value, w_output, gain_one, shift_one,
             w_in, bias_in, w_out, bias_out, gain_two, shift_two, cot_main, cot_dual):
    operands = dict(
        x_hbm=layer_in, wq_hbm=w_query, wk_hbm=w_key, wv_hbm=w_value, wo_hbm=w_output,
        dual_hbm=dual_in, cm_hbm=cot_main, cd_hbm=cot_dual,
    )
    vectors = dict(
        gain_one=gain_one, shift_one=shift_one, gain_two=gain_two, shift_two=shift_two, bias_out=bias_out
    )
    return operands, long_count, vectors, w_in, bias_in, w_out


def plain_body(*args):
    operands, count, vectors, w_in, bias_in, w_out = sort_out(*args)
    width = w_in.shape[0]
    w_in_all = lax.all_gather(w_in, "wide", axis=1, tiled=True)
    bias_all = lax.all_gather(bias_in, "wide", axis=0, tiled=True)
    w_out_all = lax.all_gather(w_out, "wide", axis=0, tiled=True)
    hidden = w_in_all.shape[1] // HALF
    wi = w_in_all.reshape(width, hidden, HALF).transpose(1, 0, 2)
    wo2 = w_out_all.reshape(hidden, HALF, width)
    bi = bias_all.astype(f32).reshape(hidden, 1, HALF)
    lo, dual, gx, gw, gqk, gwi, gwo2, gvec, gbi = plain_layer(operands, count, vectors, wi, bi, wo2)
    gwi = gwi.transpose(1, 0, 2).reshape(w_in_all.shape)
    gwo2 = gwo2.reshape(w_out_all.shape)
    gwi = lax.psum(lax.psum_scatter(gwi, "wide", scatter_dimension=1, tiled=True), "batch")
    gwo2 = lax.psum(lax.psum_scatter(gwo2, "wide", scatter_dimension=0, tiled=True), "batch")
    gbi = lax.psum_scatter(gbi.reshape(-1), "wide", scatter_dimension=0, tiled=True)
    gbi = lax.psum(gbi, "batch")
    gw, gqk, gvec = lax.psum((gw, gqk, gvec), ("batch", "wide"))
    gw, gqk = gw.astype(f32), gqk.astype(f32)
    part = width // PARTS
    gq = jnp.concatenate(list(gqk[:, :, :part]), axis=1)
    gk = jnp.concatenate(list(gqk[:, :, part:]), axis=1)
    return (lo, dual, gx, gq, gk, gw[1], gw[0], gvec[0], gvec[1], gwi.astype(f32), gbi,
            gwo2.astype(f32), gvec[2], gvec[3], gvec[4])


def steps():
    n = Net
    plan = {}
    plan[(At.ATTEND, 0)] = (
        (n.pass_x, 0, 0),
    )
    plan[(At.ATTEND, 3)] = (
        (n.pass_x, 0, 1),
    )
    plan[(At.ATTEND, 5)] = (
        (n.pass_x, 0, 2),
    )
    plan[(At.ATTEND, 7)] = (
        (n.pass_x, 0, 3),
    )
    plan[(At.ATTEND, 8)] = (
        (n.pass_y, 0, 0),
    )
    plan[(At.HIDDEN,)] = (
        (n.pass_y, 0, 1),
        (n.pass_x, 1, 0),
        (n.arrived_near, 0),
    )
    plan[(At.HALVES, 3)] = (
        (n.pass_y, 0, 2),
    )
    plan[(At.OTHERS,)] = (
        (n.pass_y, 0, 3),
        (n.pass_x, 1, 1),
        (n.pass_x, 1, 2),
        (n.arrived_far, 0),
    )
    plan[(At.HALVES2, 1)] = (
        (n.pass_y, 1, 0),
    )
    plan[(At.OUT, 3)] = (
        (n.f_core, 0, 3),
    )
    plan[(At.OUT, 1)] = (
        (n.f_core, 0, 1),
    )
    plan[(At.PRE, 2)] = (
        (n.f_x, 0),
    )
    plan[(At.PRE, 3)] = (
        (n.f_near, 0),
    )
    plan[(At.IN, 3)] = (
        (n.f_core, 1, 3),
    )
    plan[(At.IN, 1)] = (
        (n.f_core, 1, 1),
    )
    plan[(At.FIRST, 1)] = (
        (n.f_x, 1),
    )
    plan[(At.FIRST, 3)] = (
        (n.f_near, 1),
    )
    plan[(At.W_OUTPUT,)] = (
        (n.a_core, 0),
        (n.f_step, 1, 0),
        (n.v_core,),
        (n.f_step, 0, 0),
    )
    plan[(At.VALUES, 6)] = (
        (n.a_step, 0, 0),
        (n.v_next, 0),
    )
    plan[(At.W_VALUE,)] = (
        (n.a_core, 1),
    )
    plan[(At.SCORES, 1)] = (
        (n.f_step, 0, 1),
    )
    plan[(At.SCORES, 2)] = (
        (n.a_core, 2),
        (n.a_step, 1, 0),
        (n.f_step, 2, 0),
    )
    plan[(At.SCORES, 3)] = (
        (n.a_step, 0, 1),
    )
    plan[(At.SCORES, 4)] = (
        (n.a_core, 3),
        (n.a_step, 2, 0),
        (n.v_next, 1),
    )
    plan[(At.SCORES, 5)] = (
        (n.f_step, 3, 0),
    )
    plan[(At.SCORES, 6)] = (
        (n.f_step, 1, 1),
        (n.a_step, 3, 0),
        (n.a_core, 4),
        (n.a_step, 1, 1),
        (n.f_step, 2, 1),
    )
    plan[(At.SCORES, 7)] = (
        (n.a_step, 0, 2),
    )
    plan[(At.SCORES, 8)] = (
        (n.a_core, 5),
        (n.a_step, 4, 0),
        (n.f_step, 0, 2),
        (n.v_next, 2),
    )
    plan[(At.INPUT, 1)] = (
        (n.a_step, 2, 1),
        (n.a_step, 3, 1),
        (n.f_step, 3, 1),
    )
    plan[(At.INPUT, 3)] = (
        (n.a_step, 1, 2),
        (n.f_step, 1, 2),
        (n.f_step, 2, 2),
    )
    plan[(At.END,)] = (
        (n.a_step, 4, 1),
        (n.a_step, 0, 3),
        (n.a_step, 5, 0),
        (n.v_next, 3),
        (n.a_step, 2, 2),
        (n.f_step, 3, 2),
        (n.f_step, 1, 3),
        (n.f_back, 0, 0),
        (n.a_step, 4, 2),
        (n.a_step, 3, 2),
        (n.a_step, 5, 1),
        (n.a_step, 1, 3),
        (n.a_step, 2, 3),
        (n.f_step, 2, 3),
        (n.f_step, 3, 3),
        (n.f_back, 1, 0),
        (n.a_step, 3, 3),
        (n.a_back, 0, 3),
        (n.v_next, 4),
        (n.f_back, 0, 1),
        (n.a_back, 2, 3),
        (n.a_step, 4, 3),
        (n.a_step, 5, 2),
        (n.a_back, 3, 3),
        (n.f_back, 3, 0),
        (n.a_back, 1, 3),
        (n.f_back, 2, 0),
        (n.a_back, 0, 2),
        (n.a_back, 2, 2),
        (n.f_back, 1, 1),
        (n.f_back, 3, 1),
        (n.a_back, 4, 3),
        (n.a_back, 5, 2),
        (n.a_back, 1, 2),
        (n.a_back, 3, 2),
        (n.f_back, 2, 1),
        (n.a_back, 0, 1),
        (n.a_back, 4, 2),
        (n.a_back, 2, 1),
        (n.a_back, 5, 1),
        (n.f_back, 1, 2),
        (n.a_back, 0, 0),
        (n.a_back, 3, 1),
        (n.a_back, 1, 1),
        (n.a_back, 2, 0),
        (n.a_back, 4, 1),
        (n.f_back, 3, 2),
        (n.a_back, 3, 0),
        (n.f_back, 2, 2),
        (n.a_back, 1, 0),
        (n.a_back, 5, 0),
        (n.a_back, 4, 0),
    )
    plan[(At.BRANCH,)] = (
        (n.arrived_near, 1),
        (n.arrived_far, 1),
    )
    return plan


COPIES = 224


def tuned_kernel(names, *refs):
    r = Refs(names, refs)
    base = begin(r, r.x.shape[0])
    sems = r.sems
    for u, (m, start, size, _) in enumerate(UNITS):
        cut = slice(start, start + size)
        r.outs["f", u] = (r.fout.at[m, cut], r.f_out.at[m, cut], sems.at[base + u])
    for n in range(2 + PARTS):
        pair = (r.aout.at[n], r.a_out.at[n]) if n < 2 else (r.qout.at[n - 2], r.q_out.at[n - 2])
        r.outs["a", n] = (*pair, sems.at[base + len(UNITS) + n])
    r.outs["v", 0] = (r.vs.at[5], r.v_out, sems.at[base + len(UNITS) + 2 + PARTS])
    r.fetch("wi", r.wi_hbm, r.wi.at[0], sems.at[base + len(UNITS) + 3 + PARTS])
    r.fetch("wo2", r.wo2_hbm, r.wo2.at[0], sems.at[base + len(UNITS) + 4 + PARTS])
    r.bi[0] = jnp.broadcast_to(r.bias_in[...].astype(f32)[None], r.bi.shape[1:])
    net = Net(r, steps())
    net.enter()
    r.wait("wi", "wo2")
    layer(r, net)
    net.leave()
    r.drain()


def tuned_layer(operands, count, vectors, w_in, bias_in, w_out):
    tokens, width = operands["x_hbm"].shape
    hidden = 4
    part = 2 * width // PARTS
    shape = jax.ShapeDtypeStruct
    vmem = pltpu.VMEM
    ins = {name: (value, ANY) for name, value in operands.items()}
    ins.update(count_ref=(count, IN_SMEM))
    ins.update({name: (value, IN_VMEM) for name, value in vectors.items()})
    ins.update(wi_hbm=(w_in, ANY), wo2_hbm=(w_out, ANY), bias_in=(bias_in, IN_VMEM))
    outs = dict(
        lo_out=shape((tokens, width), bf16),
        dual_out=shape((tokens, width), f32),
        gx_out=shape((tokens, width), f32),
        f_out=shape((2, HALF, width), bf16),
        a_out=shape((2, width, width), bf16),
        q_out=shape((PARTS, width, part), bf16),
        v_out=shape((16, width), f32),
    )
    scratch = scratch_of(tokens, width, hidden)
    scratch.update(
        wi=vmem((hidden, width, HALF), bf16),
        wo2=vmem((hidden, HALF, width), bf16),
        bi=vmem((hidden, 8, HALF), f32),
        gw=vmem((2, width, width), bf16),
        gqk=vmem((PARTS, width, part), bf16),
        gwi=vmem((hidden, width, HALF), bf16),
        gwo2=vmem((hidden, HALF, width), bf16),
        gvec=vmem((8, width), f32),
        gbi=vmem((hidden, 1, HALF), f32),
        rca=vmem((2, HALF, width), bf16),
        rcd=vmem((2, HALF, width), bf16),
        rf=vmem((len(UNITS), max(unit[2] for unit in UNITS) * 15 // 8, width), bf16),
        fout=vmem((2, HALF, width), bf16),
        ra=vmem((2, width * 31 // 32, width), bf16),
        aout=vmem((2, width, width), bf16),
        rq=vmem((PARTS, width * 31 // 32, part), bf16),
        qout=vmem((PARTS, width, part), bf16),
        vs=vmem((6, 16, width), f32),
        vr=vmem((5, 16, width), f32),
        sems=pltpu.SemaphoreType.DMA((len(FETCHED) + 4 + len(UNITS) + 5 + PARTS,)),
        send_sem=pltpu.SemaphoreType.DMA((COPIES,)),
        recv_sem=pltpu.SemaphoreType.DMA((COPIES,)),
    )
    names = list(ins) + list(outs) + list(scratch)
    return pl.pallas_call(
        functools.partial(tuned_kernel, names),
        out_shape=list(outs.values()),
        in_specs=[i[1] for i in ins.values()],
        out_specs=[ANY] * len(outs),
        scratch_shapes=list(scratch.values()),
        compiler_params=pltpu.CompilerParams(
            vmem_limit_bytes=int(63.5 * 2**20), collective_id=0, has_side_effects=True
        ),
        cost_estimate=COST,
    )(*[i[0] for i in ins.values()])


def widen_kernel(lo, dual, gx, f, a, q, v, lo_out, dual_out, gx_out, gq, gk, gv, go, gwi, gwo,
                 gg1, gs1, gbi, gbo, gg2, gs2, f_low, a_low, q_low, lo_held, dual_held, gx_held, wide, sems):
    def copy(source, target, at):
        made = pltpu.make_async_copy(source, target, sems.at[at])
        made.start()
        return made

    low = [copy(*pair, at) for at, pair in enumerate(((f, f_low), (a, a_low), (q, q_low)))]
    moves = []
    for source, held, target in ((dual, dual_held, dual_out), (gx, gx_held, gx_out), (lo, lo_held, lo_out)):
        for at in range(source.shape[0] // BLOCK):
            rows = rows_of(at)
            moves.append((source.at[rows], held.at[rows], target.at[rows]))
    loads = [copy(source, held, 3 + at) for at, (source, held, _) in enumerate(moves)]
    stores = []

    def store(source, target):
        stores.append(copy(source, target, 3 + len(moves) + len(stores)))

    def widened(at, value, target):
        wide[at] = value.astype(f32)
        store(wide.at[at], target)

    for at, out in enumerate((gg1, gs1, gbo, gg2, gs2)):
        out[...] = v[at]
    gbi[...] = v[12]
    low[0].wait()
    widened(0, f_low[0], gwo)
    widened(1, f_low[1], gwi)
    low[1].wait()
    widened(2, a_low[0], go)
    widened(3, a_low[1], gv)
    low[2].wait()
    part = q.shape[2] // 2
    for at, target in ((4, gq), (5, gk)):
        cols = span_of(at - 4, part)
        for p in range(PARTS):
            wide[at, :, p * part : (p + 1) * part] = q_low[p, :, cols].astype(f32)
        store(wide.at[at], target)
    for load, (_, held, target) in zip(loads, moves):
        load.wait()
        store(held, target)
    for made in stores:
        made.wait()


def widen(lo, dual, gx, f, a, q, v):
    width = f.shape[2]
    shape = jax.ShapeDtypeStruct
    matrix = (shape((width, width), f32), ANY)
    vector = (shape((width,), f32), IN_VMEM)
    outs = [(shape(t.shape, t.dtype), ANY) for t in (lo, dual, gx)] + [matrix] * 6 + [vector] * 6
    return pl.pallas_call(
        widen_kernel,
        out_shape=[o[0] for o in outs],
        in_specs=[ANY] * 6 + [IN_VMEM],
        out_specs=[o[1] for o in outs],
        scratch_shapes=[
            pltpu.VMEM(f.shape, bf16),
            pltpu.VMEM(a.shape, bf16),
            pltpu.VMEM(q.shape, bf16),
            *[pltpu.VMEM(t.shape, t.dtype) for t in (lo, dual, gx)],
            pltpu.VMEM((6, width, width), f32),
            pltpu.SemaphoreType.DMA((9 + 6 * (lo.shape[0] // BLOCK),)),
        ],
        compiler_params=pltpu.CompilerParams(vmem_limit_bytes=int(63.5 * 2**20)),
        cost_estimate=pl.CostEstimate(flops=0, bytes_accessed=19 << 20, transcendentals=0),
    )(lo, dual, gx, f, a, q, v)


def tuned_body(*args):
    (lo, dual, gx, gq, gk, gv, go, gwi, gwo, gg1, gs1, gbi, gbo, gg2, gs2) = widen(*tuned_layer(*sort_out(*args)))
    return lo, dual, gx, gq, gk, gv, go, gg1, gs1, gwi, gbi, gwo, gbo, gg2, gs2


def solution(mesh):
    tokens = P(("batch", "wide"), None)
    fits = mesh.shape["batch"] == 8 and mesh.shape["wide"] == 4
    return jax.shard_map(
        tuned_body if fits else plain_body,
        mesh=mesh,
        in_specs=(tokens, tokens, P(("batch", "wide")), P(), P(), P(), P(), P(), P(), P(None, "wide"), P("wide"),
                  P("wide", None), P(), P(), P(), tokens, tokens),
        out_specs=(tokens, tokens, tokens, P(), P(), P(), P(), P(), P(), P(None, "wide"), P("wide"),
                   P("wide", None), P(), P(), P()),
        check_vma=False,
    )
```

```python
import functools

import jax
import jax.numpy as jnp
from jax import lax
from jax.experimental import pallas as pl
from jax.experimental.pallas import tpu as pltpu
from jax.sharding import PartitionSpec as P

HEADS = 8
HEAD_DIM = 64
EPSILON = 1e-05
MASKED = -1000000000.0
BLOCK = 256
HALF = 512
PARTS = 4
PRE_UNROLL = 1
HALF_UNROLL = NORM_UNROLL = SECOND_UNROLL = FIRST_UNROLL = INPUT_UNROLL = 2
CORE, X, Y, NEXT, FAR, ZED, WIDE, BATCH = range(8)
UNITS = (
    (0, 0, 256, (Y, X, NEXT, FAR)),
    (0, 256, 256, (X, Y, ZED)),
    (1, 0, 256, (NEXT, X, Y, FAR)),
    (1, 256, 256, (FAR, NEXT, X, Y)),
)
CHUNKS = (
    (CORE, Y, FAR, X, NEXT),
    (CORE, X, Y, ZED),
    (CORE, Y, X, ZED),
    (CORE, ZED, Y, X),
    (CORE, Y, X, ZED),
    (WIDE, Y, ZED),
)

bf16 = jnp.bfloat16
f32 = jnp.float32


def contract(left, right, a, b):
    return lax.dot_general(
        left, right, (((a,), (b,)), ((), ())), preferred_element_type=f32
    )


def dot_nn(left, right):
    return contract(left, right, 1, 0)


def dot_nt(left, right):
    return contract(left, right, 1, 1)


def dot_tn(left, right):
    return contract(left, right, 0, 0)


def dot_tt(left, right):
    return contract(left, right, 0, 1)


def span_of(at, size):
    if isinstance(at, int):
        return slice(at * size, (at + 1) * size)
    return pl.ds(pl.multiple_of(at * size, size), size)


def rows_of(block):
    return span_of(block, BLOCK)


def head_of(head):
    return span_of(head, HEAD_DIM)


def split(block):
    return block // 2, span_of(block % 2, BLOCK)


def each(count, step, unroll=1):
    def several(at, _):
        for k in range(unroll):
            step(at * unroll + k)
        return 0

    lax.fori_loop(0, count // unroll, several, 0)


def row_mean(value):
    return jnp.mean(value, axis=-1, keepdims=True)


def col_sum(value):
    return jnp.sum(value, axis=0, keepdims=True)


def joined(value):
    return value.reshape(value.shape[0] * value.shape[1], value.shape[2])


def layer(r, net):
    tokens, width = r.x.shape
    blocks = tokens // BLOCK
    hidden = r.wi.shape[0]
    slots = tuple(range(hidden))

    r.wait("x", "wq", "wk", "wv")
    for block in range(blocks):
        cols = rows_of(block)
        xb = r.x[cols]
        r.qt[:, cols] = (dot_tt(r.wq[...], xb) * HEAD_DIM**-0.5).astype(bf16)
        r.kt[:, cols] = dot_tt(r.wk[...], xb).astype(bf16)
        r.vt[:, cols] = dot_tt(r.wv[...], xb).astype(bf16)
    net.tick(At.PROJECT)

    row_at = lax.broadcasted_iota(jnp.int32, (BLOCK, BLOCK), 0)
    col_at = lax.broadcasted_iota(jnp.int32, (BLOCK, BLOCK), 1)
    causal = row_at <= col_at
    away = jnp.where(r.count > 0, 0.0, 2e9).astype(f32)

    def soften(head, qb):
        hs = head_of(head)
        query = r.qt[hs, rows_of(qb)]
        parts = []
        peak_off = None
        for tb in range(qb + 1):
            scores = dot_tn(r.kt[hs, rows_of(tb)], query)
            if tb == qb:
                scores = jnp.where(causal, scores, MASKED)
            parts.append(scores)
            peak = jnp.max(scores, axis=0, keepdims=True)
            if tb < qb:
                peak_off = peak if peak_off is None else jnp.maximum(peak_off, peak)
        if peak_off is not None:
            peak = jnp.maximum(peak, peak_off - away)
        total = jnp.zeros((1, BLOCK), f32)
        for tb in range(qb + 1):
            expo = jnp.exp(parts[tb] - (peak if tb == qb else peak + away))
            total += jnp.sum(expo, axis=0, keepdims=True)
            r.p[qb][head, rows_of(tb)] = expo.astype(bf16)
        r.inv_total[pl.ds(head, 1), rows_of(qb)] = 1.0 / total

    def mix(head, qb):
        hs = head_of(head)
        mixed = dot_nn(r.vt[hs, : (qb + 1) * BLOCK], r.p[qb][head])
        mixed *= r.inv_total[pl.ds(head, 1), rows_of(qb)]
        r.mt[hs, rows_of(qb)] = mixed.astype(bf16)

    for head in range(HEADS + 1):
        for qb in range(blocks):
            if head < HEADS:
                soften(head, qb)
            if head > 0:
                mix(head - 1, qb)
        net.tick(At.ATTEND, head)

    r.wait("wo", "dual")
    gain_one, shift_one = r.gain_one[...][None], r.shift_one[...][None]

    def norm_block(block):
        rows = rows_of(block)
        attended = dot_tn(r.mt[:, rows], r.wo[...])
        r.dual[rows] += attended
        hidden_one = r.x[rows].astype(f32) + attended
        centre = hidden_one - row_mean(hidden_one)
        inverse = lax.rsqrt(row_mean(centre * centre) + EPSILON)
        normed = centre * inverse
        r.n1[rows] = normed
        r.i1[rows] = inverse
        r.fl[rows] = (normed * gain_one + shift_one).astype(bf16)

    each(blocks, norm_block, NORM_UNROLL)

    def half_block(block, pair, place):
        first_low = r.fl[rows_of(block)]
        th, rows = split(block)
        for j in pair:
            pre = dot_nn(first_low, r.wi[j]) + r.bi[j, 0:1]
            phi = 0.5 + 0.5 * lax.erf(pre * 0.7071067811865476)
            bell = jnp.exp(-0.5 * pre * pre) * 0.3989422804014327
            r.act[j, th, rows] = (pre * phi).astype(bf16)
            r.slope[j, th, rows] = (phi + pre * bell).astype(bf16)
        net.loop_tick(place, block, blocks)

    net.tick(At.HIDDEN)
    each(blocks, lambda block: half_block(block, slots[:2], At.HALVES), HALF_UNROLL)
    net.tick(At.OTHERS)
    each(blocks, lambda block: half_block(block, slots[2:], At.HALVES2), HALF_UNROLL)

    r.wait("cm", "cd")
    net.tick(At.BRANCH)
    gain_two, shift_two = r.gain_two[...][None], r.shift_two[...][None]
    bias_out = r.bias_out[...][None]
    r.gvec[...] = jnp.zeros_like(r.gvec)

    def second_block(block):
        rows = rows_of(block)
        th, cut = split(block)
        branch = dot_nn(r.act[0, th, cut], r.wo2[0])
        for j in slots[1:]:
            branch += dot_nn(r.act[j, th, cut], r.wo2[j])
        branch += bias_out
        r.dual[rows] += branch
        hidden_two = r.n1[rows] * gain_one + shift_one + branch
        centre = hidden_two - row_mean(hidden_two)
        inverse = lax.rsqrt(row_mean(centre * centre) + EPSILON)
        normed = centre * inverse
        r.gwi[th, cut] = (normed * gain_two + shift_two).astype(bf16)
        grad = r.cm[rows]
        r.gvec[3:4] += col_sum(grad * normed)
        r.gvec[4:5] += col_sum(grad)
        scaled = grad * gain_two
        g_sum = inverse * (
            scaled - row_mean(scaled) - normed * row_mean(scaled * normed)
        )
        r.cm[rows] = g_sum
        g_branch = (g_sum + r.cd[rows]).astype(bf16)
        r.gb[rows] = g_branch
        r.gvec[2:3] += col_sum(g_branch.astype(f32))

    each(blocks, second_block, SECOND_UNROLL)
    r.put("lo", 0)
    r.put("lo", 1)
    r.put("dual", 0)

    for j in reversed(slots):
        r.gwo2[j] = dot_tn(joined(r.act[j]), r.gb[...]).astype(bf16)
        net.tick(At.OUT, j)
    r.gbi[...] = jnp.zeros_like(r.gbi)

    def pre_block(block):
        g_branch = r.gb[rows_of(block)]
        th, rows = split(block)
        for j in slots:
            g_act = dot_nt(g_branch, r.wo2[j])
            g_pre = (g_act * r.slope[j, th, rows].astype(f32)).astype(bf16)
            r.slope[j, th, rows] = g_pre
            r.gbi[j] += col_sum(g_pre.astype(f32))
        net.loop_tick(At.PRE, block, blocks)

    each(blocks, pre_block, PRE_UNROLL)
    r.finished("lo")
    for j in reversed(slots):
        r.gwi[j] = dot_tn(r.fl[...], joined(r.slope[j])).astype(bf16)
        net.tick(At.IN, j)

    def first_block(block):
        rows = rows_of(block)
        th, cut = split(block)
        g_first = dot_nt(r.slope[0, th, cut], r.wi[0])
        for j in slots[1:]:
            g_first += dot_nt(r.slope[j, th, cut], r.wi[j])
        g_first += r.cm[rows]
        normed = r.n1[rows]
        r.gvec[0:1] += col_sum(g_first * normed)
        r.gvec[1:2] += col_sum(g_first)
        scaled = g_first * gain_one
        g_resid = r.i1[rows] * (
            scaled - row_mean(scaled) - normed * row_mean(scaled * normed)
        )
        r.cm[rows] = g_resid
        g_att = (g_resid + r.cd[rows]).astype(bf16)
        r.gb[rows] = g_att
        g_mixed = dot_nt(r.wo[...], g_att)
        g_mixed = g_mixed.reshape(HEADS, HEAD_DIM, BLOCK) * r.inv_total[:, rows][:, None]
        g_mixed = g_mixed.reshape(width, BLOCK).astype(bf16)
        r.act[3, th, :, cut] = g_mixed
        centred = g_mixed.astype(f32) * r.mt[:, rows].astype(f32)
        r.centred[:, rows] = jnp.sum(centred.reshape(HEADS, HEAD_DIM, BLOCK), axis=1)
        net.loop_tick(At.FIRST, block, blocks)

    each(blocks, first_block, FIRST_UNROLL)
    r.gw[0] = dot_nn(r.mt[...], r.gb[...]).astype(bf16)
    net.tick(At.W_OUTPUT)
    for th in range(2):
        r.slope[0, th] = r.x[th * HALF : (th + 1) * HALF].T

    def columns(which, head, block):
        th, cut = split(block)
        return which, th, head_of(head), cut

    def back_values(head, tb):
        total = None
        for qb in range(tb, blocks):
            part = dot_nt(r.act[columns(3, head, qb)], r.p[qb][head, rows_of(tb)])
            total = part if total is None else total + part
        r.act[columns(2, head, tb)] = total.astype(bf16)

    def back_scores(head, qb, slot):
        got = r.act[columns(3, head, qb)]
        centred = r.centred[pl.ds(head, 1), rows_of(qb)]
        for tb in range(qb + 1):
            g_probs = dot_tn(r.vt[head_of(head), rows_of(tb)], got)
            probs = r.p[qb][head, rows_of(tb)].astype(f32)
            slot[qb][rows_of(tb)] = (probs * (g_probs - centred)).astype(bf16)

    def back_query(head, qb, slot):
        g_query = dot_nn(r.kt[head_of(head), : (qb + 1) * BLOCK], slot[qb][...])
        r.act[columns(0, head, qb)] = (g_query * HEAD_DIM**-0.5).astype(bf16)

    def back_keys(head, tb, slot):
        total = None
        for qb in range(tb, blocks):
            part = dot_nt(r.qt[head_of(head), rows_of(qb)], slot[qb][rows_of(tb)])
            total = part if total is None else total + part
        r.act[columns(1, head, tb)] = total.astype(bf16)

    def against_x(which, rows):
        total = dot_nt(r.slope[0, 0], r.act[which, 0, rows])
        return (total + dot_nt(r.slope[0, 1], r.act[which, 1, rows])).astype(bf16)

    for head in range(HEADS):
        for tb in range(blocks):
            back_values(head, tb)
        net.tick(At.VALUES, head)
    r.gw[1] = against_x(2, slice(0, width))
    net.tick(At.W_VALUE)
    size = HEADS // PARTS
    part_width = size * HEAD_DIM

    for head in range(HEADS + 1):
        for block in range(blocks):
            if head < HEADS:
                back_scores(head, block, r.gs[head % 2])
            if head > 0:
                back_query(head - 1, block, r.gs[(head - 1) % 2])
                back_keys(head - 1, block, r.gs[(head - 1) % 2])
        if head > 0 and head % size == 0:
            part = head // size - 1
            rows = span_of(part, part_width)
            r.gqk[part, :, :part_width] = against_x(0, rows)
            r.gqk[part, :, part_width:] = against_x(1, rows)
        net.tick(At.SCORES, head)

    def input_block(block):
        rows = rows_of(block)
        th, cut = split(block)
        grad = dot_tt(r.act[0, th, :, cut], r.wq[...])
        grad += dot_tt(r.act[1, th, :, cut], r.wk[...])
        grad += dot_tt(r.act[2, th, :, cut], r.wv[...])
        r.cm[rows] += grad
        net.loop_tick(At.INPUT, block, blocks)

    each(blocks, input_block, INPUT_UNROLL)
    r.put("cm", 0)
    net.tick(At.END)


class Refs:
    def __init__(self, names, refs):
        self.__dict__.update(zip(names, refs))
        self.pending = {}
        self.out = {}

    def fetch(self, name, source, target, sem):
        copy = pltpu.make_async_copy(source, target, sem)
        copy.start()
        self.pending[name] = copy

    def wait(self, *names):
        for name in names:
            self.pending.pop(name).wait()

    def put(self, name, at):
        source, target, sem = self.outs[name, at]
        copy = pltpu.make_async_copy(source, target, sem)
        copy.start()
        self.out[name, at] = copy

    def finished(self, name):
        for key in [key for key in self.out if key[0] == name]:
            self.out.pop(key).wait()

    def drain(self):
        for copy in self.out.values():
            copy.wait()


FETCHED = ("x", "wq", "wk", "wv", "wo", "dual", "cm", "cd")


def scratch_of(tokens, width, hidden):
    vmem = pltpu.VMEM
    wide = (hidden, tokens // HALF, HALF, HALF)
    names = dict(
        x=vmem((tokens, width), bf16),
        wq=vmem((width, width), bf16),
        wk=vmem((width, width), bf16),
        wv=vmem((width, width), bf16),
        wo=vmem((width, width), bf16),
        dual=vmem((tokens, width), f32),
        cm=vmem((tokens, width), f32),
        cd=vmem((tokens, width), f32),
        qt=vmem((width, tokens), bf16),
        kt=vmem((width, tokens), bf16),
        vt=vmem((width, tokens), bf16),
        mt=vmem((width, tokens), bf16),
        inv_total=vmem((HEADS, tokens), f32),
        centred=vmem((HEADS, tokens), f32),
        n1=vmem((tokens, width), f32),
        i1=vmem((tokens, 1), f32),
        fl=vmem((tokens, width), bf16),
        act=vmem(wide, bf16),
        slope=vmem(wide, bf16),
        gb=vmem((tokens, width), bf16),
    )
    for qb in range(tokens // BLOCK):
        names[f"p{qb}"] = vmem((HEADS, (qb + 1) * BLOCK, BLOCK), bf16)
        names[f"g{qb}"] = vmem(((qb + 1) * BLOCK, BLOCK), bf16)
        names[f"h{qb}"] = vmem(((qb + 1) * BLOCK, BLOCK), bf16)
    return names


def begin(r, tokens):
    blocks = tokens // BLOCK
    r.count = r.count_ref[0]
    r.p = [getattr(r, f"p{qb}") for qb in range(blocks)]
    r.gs = [[getattr(r, f"{s}{qb}") for qb in range(blocks)] for s in "gh"]
    for at, name in enumerate(FETCHED):
        r.fetch(name, getattr(r, name + "_hbm"), getattr(r, name), r.sems.at[at])
    base = len(FETCHED)
    r.outs = {
        ("lo", 0): (r.gwi.at[0], r.lo_out.at[0:HALF], r.sems.at[base]),
        ("lo", 1): (r.gwi.at[1], r.lo_out.at[HALF : 2 * HALF], r.sems.at[base + 1]),
        ("dual", 0): (r.dual, r.dual_out, r.sems.at[base + 2]),
        ("cm", 0): (r.cm, r.gx_out, r.sems.at[base + 3]),
    }
    return base + 4


class Quiet:
    def tick(self, *place):
        pass

    def loop_tick(self, place, at, count):
        pass


class At:
    (PROJECT, ATTEND, HIDDEN, HALVES, OTHERS, HALVES2, BRANCH, OUT, PRE, IN, FIRST, W_OUTPUT,
     VALUES, W_VALUE, SCORES, INPUT, END) = range(17)


class Kind:
    (W_X, W_Y, W_CORE, W_PASS, W_TURN, W_BIAS, F_CORE, F_AWAY, F_OWN, F_BACK, A_OUT, A_BACK,
     V_STEP) = range(13)


class Net:
    def __init__(self, r, plan):
        self.r = r
        self.plan = plan
        b, w = lax.axis_index("batch"), lax.axis_index("wide")
        z, y, x, c = b // 2, b % 2, w // 2, w % 2
        self.y, self.x, self.c, self.w = y, x, c, w
        self.core = (b, x * 2 + 1 - c)
        self.ex = (b, (1 - x) * 2 + c)
        self.diagonal = (b, (1 - x) * 2 + 1 - c)
        self.why = (z * 2 + 1 - y, w)
        self.odd, self.high = z % 2, z // 2
        self.next = ((z + 1 - 2 * self.odd) * 2 + y, w)
        self.far = (((z + 2) % 4) * 2 + y, w)
        self.table = {}
        self.used = set()
        def pair(peer, bit):
            return bit, 2, [(peer, 1 - bit)]

        self.axes = (
            pair(self.core, c),
            pair(self.ex, x),
            pair(self.why, y),
            pair(self.next, self.odd),
            pair(self.far, self.high),
            (z, 4, [(((z + k) % 4 * 2 + y, w), (z + k) % 4) for k in (1, 2, 3)]),
            (w, 4, [(to, to[1]) for to in (self.core, self.ex, self.diagonal)]),
            (b, 8, [(((b + k) % 8, w), (b + k) % 8) for k in range(1, 8)]),
        )
        self.units = []
        self.parts = []
        self.describe()

    def copy(self, name, to, source, target):
        self.table[name] = (len(self.table), to, source, target)

    def build(self, name):
        index, to, source, target = self.table[name]
        return pltpu.make_async_remote_copy(
            src_ref=source(),
            dst_ref=target(),
            send_sem=self.r.send_sem.at[index],
            recv_sem=self.r.recv_sem.at[index],
            device_id=to,
            device_id_type=pl.DeviceIdType.MESH,
        )

    def start(self, *names):
        for name in names:
            self.used.add(name)
            self.build(name).start()

    def got(self, *names):
        for name in names:
            self.build(name).wait_recv()

    def tick(self, *place):
        for event, *args in self.plan.get(place, ()):
            event(self, *args)

    def loop_tick(self, place, at, count):
        for k in range(count):
            if self.plan.get((place, k)):
                self.guard(at, k, place)

    def guard(self, at, k, place):
        if isinstance(at, int):
            if at == k:
                self.tick(place, k)
        else:
            pl.when(at == k)(functools.partial(self.tick, place, k))

    def cut(self, base, size, mine, peers):
        keep = lambda: self.span(base() + mine * size, size)
        gives = [lambda at=at: self.span(base() + at * size, size) for _, at in peers]
        return keep, gives, lambda: base() + mine * size

    def group(self, act, *name):
        k = 0
        while (*name, k) in self.table:
            act((*name, k))
            k += 1
        return k

    def span(self, start, size):
        return pl.ds(pl.multiple_of(start, size), size)

    def describe(self):
        r, copy, span = self.r, self.copy, self.span
        own = (r.wi_hbm, r.wo2_hbm)
        held = (r.wi, r.wo2)
        for m in range(2):
            copy((Kind.W_CORE, m), self.core, lambda m=m: own[m], lambda m=m: held[m].at[1])
            for q, (mine, other) in enumerate(self.slices(m)):
                copy((Kind.W_X, m, q), self.ex, lambda m=m, f=mine: own[m].at[f()], lambda m=m, f=mine: held[m].at[2, f()])
                copy((Kind.W_PASS, m, q), self.core, lambda m=m, f=mine: held[m].at[2, f()], lambda m=m, f=mine: held[m].at[3, f()])
                if other is not None:
                    copy((Kind.W_Y, m, q), self.why, lambda m=m, f=mine: held[m].at[2, f()], lambda m=m, f=mine: held[m].at[2, f()])
                    copy((Kind.W_TURN, m, q), self.core, lambda m=m, f=other: held[m].at[2, f()], lambda m=m, f=other: held[m].at[3, f()])
        for slot, to in ((1, self.core), (2, self.ex), (3, self.diagonal)):
            copy((Kind.W_BIAS, slot), to, lambda: r.bi.at[0], lambda slot=slot: r.bi.at[slot])

        for m in range(2):
            for slot in (3, 1):
                received = r.rca if slot == 3 else r.rcd
                copy((Kind.F_CORE, m, slot), self.core, lambda m=m, s=slot: self.grad(m).at[s], lambda m=m, t=received: t.at[m])
        for u, (m, start, size, order) in enumerate(UNITS):
            grad, out = self.grad(m), r.fout.at[m]
            base = lambda f=start: f
            both, offset, levels, back = True, 0, [], []
            for level, axis in enumerate(order):
                mine, parts, peers = self.axes[axis]
                if axis == X:
                    both = False
                    keep = lambda f=base, s=size: span(f(), s)
                    gives = [keep]
                else:
                    size //= parts
                    keep, gives, base = self.cut(base, size, mine, peers)
                    back.append((axis, keep))
                landing = [[], []]
                for k, (to, _) in enumerate(peers):
                    for slot, kind, wanted in ((2, Kind.F_AWAY, both or axis == X), (0, Kind.F_OWN, axis != X)):
                        if wanted:
                            target = r.rf.at[u, offset : offset + size]
                            offset += size
                            landing[slot // 2].append(target)
                            copy((kind, u, level, k), to, lambda g=grad, s=slot, f=gives[k]: g.at[s, f()], lambda t=target: t)
                levels.append((axis, keep, landing))
            for step, (axis, keep) in enumerate(reversed(back)):
                for k, (to, _) in enumerate(self.axes[axis][2]):
                    copy((Kind.F_BACK, u, step, k), to, lambda o=out, f=keep: o.at[f()], lambda o=out, f=keep: o.at[f()])
            self.units.append((m, levels))

        for n in range(2 + PARTS):
            if n < 2:
                grad, received, out = r.gw.at[n], r.ra.at[n], r.aout.at[n]
            else:
                grad, received, out = r.gqk.at[n - 2], r.rq.at[n - 2], r.qout.at[n - 2]
            size = grad.shape[0]
            base = lambda: 0
            offset, levels = 0, []
            for level, axis in enumerate(CHUNKS[n]):
                mine, parts, peers = self.axes[axis]
                size //= parts
                keep, gives, base = self.cut(base, size, mine, peers)
                landing = []
                for k, (to, _) in enumerate(peers):
                    target = received.at[offset : offset + size]
                    offset += size
                    landing.append(target)
                    copy((Kind.A_OUT, n, level, k), to, lambda g=grad, f=gives[k]: g.at[f()], lambda t=target: t)
                    copy((Kind.A_BACK, n, level, k), to, lambda o=out, f=keep: o.at[f()], lambda o=out, f=keep: o.at[f()])
                levels.append((keep, landing))
            self.parts.append((grad, out, levels))

        for at, to in enumerate((self.core, self.ex, self.why, self.next, self.far)):
            copy((Kind.V_STEP, at), to, lambda at=at: r.vs.at[at], lambda at=at: r.vr.at[at])

    def enter(self):
        barrier = pltpu.get_barrier_semaphore()
        peers = [to for axis in (WIDE, BATCH) for to, _ in self.axes[axis][2]]
        for peer in peers:
            pl.semaphore_signal(barrier, inc=1, device_id=peer, device_id_type=pl.DeviceIdType.MESH)
        pl.semaphore_wait(barrier, len(peers))
        for slot in (1, 2, 3):
            self.start((Kind.W_BIAS, slot))
        for m in range(2):
            self.group(self.start, Kind.W_X, m)
        self.start((Kind.W_CORE, 0), (Kind.W_CORE, 1))

    def slices(self, m):
        y = self.y
        if m == 0:
            for q in range(4):
                yield (lambda q=q: self.span(y * 256 + q * 64, 64)), (lambda q=q: self.span((1 - y) * 256 + q * 64, 64))
        else:
            yield (lambda: self.span(y * 256, 128)), (lambda: self.span((1 - y) * 256, 128))
            for row in (128, 384):
                yield (lambda row=row: self.span(row, 128)), None

    def pass_x(self, m, q):
        self.got((Kind.W_X, m, q))
        if (Kind.W_Y, m, q) in self.table:
            self.start((Kind.W_Y, m, q))
        self.start((Kind.W_PASS, m, q))

    def pass_y(self, m, q):
        self.got((Kind.W_Y, m, q))
        self.start((Kind.W_TURN, m, q))

    def arrived_near(self, m):
        if m == 0:
            self.got((Kind.W_BIAS, 1), (Kind.W_BIAS, 2), (Kind.W_BIAS, 3))
        self.got((Kind.W_CORE, m))

    def arrived_far(self, m):
        self.group(self.got, Kind.W_PASS, m)
        self.group(self.got, Kind.W_TURN, m)

    def grad(self, m):
        return (self.r.gwo2, self.r.gwi)[m]

    def f_core(self, m, slot):
        self.start((Kind.F_CORE, m, slot))

    def f_begin(self, kind, m):
        for u, unit in enumerate(self.units):
            if unit[0] == m:
                self.group(self.start, kind, u, 0)

    def f_x(self, m):
        self.got((Kind.F_CORE, m, 3))
        grad = self.grad(m)
        grad[2] = grad[2] + self.r.rca[m]
        self.f_begin(Kind.F_AWAY, m)

    def f_near(self, m):
        self.got((Kind.F_CORE, m, 1))
        grad = self.grad(m)
        grad[0] = grad[0] + self.r.rcd[m]
        self.f_begin(Kind.F_OWN, m)

    def plus(self, total, landing):
        if len(landing) == 1:
            return total + landing[0][...]
        total = total.astype(f32)
        for part in landing:
            total += part[...].astype(f32)
        return total.astype(bf16)

    def f_step(self, u, level):
        m, levels = self.units[u]
        grad = self.grad(m)
        axis, keep, (landing_own, landing_away) = levels[level]
        s = keep()
        if landing_away:
            self.group(self.got, Kind.F_AWAY, u, level)
            if axis != X:
                grad[2, s] = self.plus(grad[2, s], landing_away)
        if landing_own:
            self.group(self.got, Kind.F_OWN, u, level)
        total = self.plus(grad[0, s], landing_away if axis == X else landing_own)
        if level == len(levels) - 1:
            self.r.fout[m, s] = total
            self.group(self.start, Kind.F_BACK, u, 0)
        else:
            grad[0, s] = total
            self.group(self.start, Kind.F_AWAY, u, level + 1)
            self.group(self.start, Kind.F_OWN, u, level + 1)

    def f_back(self, u, step):
        self.group(self.got, Kind.F_BACK, u, step)
        if not self.group(self.start, Kind.F_BACK, u, step + 1):
            self.r.put("f", u)

    def a_core(self, n):
        self.group(self.start, Kind.A_OUT, n, 0)

    def a_step(self, n, level):
        grad, out, levels = self.parts[n]
        self.group(self.got, Kind.A_OUT, n, level)
        keep, landing = levels[level]
        s = keep()
        total = self.plus(grad[s], landing)
        if level + 1 < len(levels):
            grad[s] = total
            self.group(self.start, Kind.A_OUT, n, level + 1)
        else:
            out[s] = total
            self.group(self.start, Kind.A_BACK, n, level)

    def a_back(self, n, level):
        self.group(self.got, Kind.A_BACK, n, level)
        if level:
            self.group(self.start, Kind.A_BACK, n, level - 1)
        else:
            self.r.put("a", n)

    def v_core(self):
        r = self.r
        x, c = self.x, self.c
        r.vs[0, 0:8] = r.gvec[...]
        r.vs[0, pl.ds(8 + x * 2 + c, 1)] = r.gbi[0]
        r.vs[0, pl.ds(8 + x * 2 + 1 - c, 1)] = r.gbi[1]
        r.vs[0, pl.ds(8 + (1 - x) * 2 + c, 1)] = r.gbi[2]
        r.vs[0, pl.ds(8 + (1 - x) * 2 + 1 - c, 1)] = r.gbi[3]
        self.start((Kind.V_STEP, 0))

    def v_next(self, at):
        r = self.r
        self.got((Kind.V_STEP, at))
        r.vs[at + 1] = r.vs[at] + r.vr[at]
        if at < 4:
            self.start((Kind.V_STEP, at + 1))
        else:
            r.vs[5, 12:13] = r.vs[5, pl.ds(8 + self.w, 1)]
            r.put("v", 0)

    def leave(self):
        for name in self.table:
            if name in self.used:
                self.build(name).wait_send()


def plain_kernel(names, *refs):
    r = Refs(names, refs)
    begin(r, r.x.shape[0])
    layer(r, Quiet())
    r.drain()


ANY = pl.BlockSpec(memory_space=pl.ANY)
IN_VMEM = pl.BlockSpec(memory_space=pltpu.VMEM)
IN_SMEM = pl.BlockSpec(memory_space=pltpu.SMEM)
COST = pl.CostEstimate(
    flops=25 * 10**9, bytes_accessed=30 << 20, transcendentals=12 << 20
)


def plain_layer(operands, count, vectors, wi, bi, wo2):
    tokens, width = operands["x_hbm"].shape
    hidden = wi.shape[0]
    shape = jax.ShapeDtypeStruct
    ins = {name: (value, ANY) for name, value in operands.items()}
    ins.update(count_ref=(count, IN_SMEM))
    ins.update({name: (value, IN_VMEM) for name, value in vectors.items()})
    ins.update(wi=(wi, IN_VMEM), bi=(bi, IN_VMEM), wo2=(wo2, IN_VMEM))
    outs = dict(
        lo_out=(shape((tokens, width), bf16), ANY),
        dual_out=(shape((tokens, width), f32), ANY),
        gx_out=(shape((tokens, width), f32), ANY),
        gw=(shape((2, width, width), bf16), IN_VMEM),
        gqk=(shape((PARTS, width, 2 * width // PARTS), bf16), IN_VMEM),
        gwi=(shape((hidden, width, HALF), bf16), IN_VMEM),
        gwo2=(shape((hidden, HALF, width), bf16), IN_VMEM),
        gvec=(shape((8, width), f32), IN_VMEM),
        gbi=(shape((hidden, 1, HALF), f32), IN_VMEM),
    )
    scratch = scratch_of(tokens, width, hidden)
    scratch["sems"] = pltpu.SemaphoreType.DMA((len(FETCHED) + 4,))
    names = list(ins) + list(outs) + list(scratch)
    return pl.pallas_call(
        functools.partial(plain_kernel, names),
        out_shape=[o[0] for o in outs.values()],
        in_specs=[i[1] for i in ins.values()],
        out_specs=[o[1] for o in outs.values()],
        scratch_shapes=list(scratch.values()),
        compiler_params=pltpu.CompilerParams(vmem_limit_bytes=62 << 20),
        cost_estimate=COST,
    )(*[i[0] for i in ins.values()])


def sort_out(layer_in, dual_in, long_count, w_query, w_key, w_value, w_output, gain_one, shift_one,
             w_in, bias_in, w_out, bias_out, gain_two, shift_two, cot_main, cot_dual):
    operands = dict(
        x_hbm=layer_in, wq_hbm=w_query, wk_hbm=w_key, wv_hbm=w_value, wo_hbm=w_output,
        dual_hbm=dual_in, cm_hbm=cot_main, cd_hbm=cot_dual,
    )
    vectors = dict(
        gain_one=gain_one, shift_one=shift_one, gain_two=gain_two, shift_two=shift_two, bias_out=bias_out
    )
    return operands, long_count, vectors, w_in, bias_in, w_out


def plain_body(*args):
    operands, count, vectors, w_in, bias_in, w_out = sort_out(*args)
    width = w_in.shape[0]
    w_in_all = lax.all_gather(w_in, "wide", axis=1, tiled=True)
    bias_all = lax.all_gather(bias_in, "wide", axis=0, tiled=True)
    w_out_all = lax.all_gather(w_out, "wide", axis=0, tiled=True)
    hidden = w_in_all.shape[1] // HALF
    wi = w_in_all.reshape(width, hidden, HALF).transpose(1, 0, 2)
    wo2 = w_out_all.reshape(hidden, HALF, width)
    bi = bias_all.astype(f32).reshape(hidden, 1, HALF)
    lo, dual, gx, gw, gqk, gwi, gwo2, gvec, gbi = plain_layer(operands, count, vectors, wi, bi, wo2)
    gwi = gwi.transpose(1, 0, 2).reshape(w_in_all.shape)
    gwo2 = gwo2.reshape(w_out_all.shape)
    gwi = lax.psum(lax.psum_scatter(gwi, "wide", scatter_dimension=1, tiled=True), "batch")
    gwo2 = lax.psum(lax.psum_scatter(gwo2, "wide", scatter_dimension=0, tiled=True), "batch")
    gbi = lax.psum_scatter(gbi.reshape(-1), "wide", scatter_dimension=0, tiled=True)
    gbi = lax.psum(gbi, "batch")
    gw, gqk, gvec = lax.psum((gw, gqk, gvec), ("batch", "wide"))
    gw, gqk = gw.astype(f32), gqk.astype(f32)
    part = width // PARTS
    gq = jnp.concatenate(list(gqk[:, :, :part]), axis=1)
    gk = jnp.concatenate(list(gqk[:, :, part:]), axis=1)
    return (lo, dual, gx, gq, gk, gw[1], gw[0], gvec[0], gvec[1], gwi.astype(f32), gbi,
            gwo2.astype(f32), gvec[2], gvec[3], gvec[4])


def steps():
    n = Net
    plan = {}
    plan[(At.ATTEND, 0)] = (
        (n.pass_x, 0, 0),
    )
    plan[(At.ATTEND, 3)] = (
        (n.pass_x, 0, 1),
    )
    plan[(At.ATTEND, 5)] = (
        (n.pass_x, 0, 2),
    )
    plan[(At.ATTEND, 7)] = (
        (n.pass_x, 0, 3),
    )
    plan[(At.ATTEND, 8)] = (
        (n.pass_y, 0, 0),
    )
    plan[(At.HIDDEN,)] = (
        (n.pass_y, 0, 1),
        (n.pass_x, 1, 0),
        (n.arrived_near, 0),
    )
    plan[(At.HALVES, 3)] = (
        (n.pass_y, 0, 2),
    )
    plan[(At.OTHERS,)] = (
        (n.pass_y, 0, 3),
        (n.pass_x, 1, 1),
        (n.pass_x, 1, 2),
        (n.arrived_far, 0),
    )
    plan[(At.HALVES2, 1)] = (
        (n.pass_y, 1, 0),
    )
    plan[(At.OUT, 3)] = (
        (n.f_core, 0, 3),
    )
    plan[(At.OUT, 1)] = (
        (n.f_core, 0, 1),
    )
    plan[(At.PRE, 2)] = (
        (n.f_x, 0),
    )
    plan[(At.PRE, 3)] = (
        (n.f_near, 0),
    )
    plan[(At.IN, 3)] = (
        (n.f_core, 1, 3),
    )
    plan[(At.IN, 1)] = (
        (n.f_core, 1, 1),
    )
    plan[(At.FIRST, 1)] = (
        (n.f_x, 1),
    )
    plan[(At.FIRST, 3)] = (
        (n.f_near, 1),
    )
    plan[(At.W_OUTPUT,)] = (
        (n.v_core,),
        (n.f_step, 1, 0),
        (n.a_core, 0),
        (n.f_step, 0, 0),
    )
    plan[(At.VALUES, 5)] = (
        (n.v_next, 0),
    )
    plan[(At.VALUES, 7)] = (
        (n.a_step, 0, 0),
    )
    plan[(At.W_VALUE,)] = (
        (n.a_core, 1),
    )
    plan[(At.SCORES, 1)] = (
        (n.f_step, 0, 1),
        (n.f_step, 1, 1),
    )
    plan[(At.SCORES, 2)] = (
        (n.a_core, 2),
        (n.a_step, 1, 0),
        (n.f_step, 2, 0),
        (n.v_next, 1),
    )
    plan[(At.SCORES, 3)] = (
        (n.a_step, 0, 1),
    )
    plan[(At.SCORES, 4)] = (
        (n.a_step, 2, 0),
        (n.a_core, 3),
        (n.f_step, 3, 0),
    )
    plan[(At.SCORES, 5)] = (
        (n.f_step, 0, 2),
        (n.v_next, 2),
    )
    plan[(At.SCORES, 6)] = (
        (n.a_step, 3, 0),
        (n.a_step, 1, 1),
        (n.a_core, 4),
    )
    plan[(At.SCORES, 7)] = (
        (n.f_step, 1, 2),
        (n.a_step, 2, 1),
    )
    plan[(At.SCORES, 8)] = (
        (n.a_core, 5),
        (n.a_step, 0, 2),
        (n.f_step, 2, 1),
        (n.a_step, 4, 0),
        (n.f_step, 3, 1),
    )
    plan[(At.INPUT, 1)] = (
        (n.f_step, 0, 3),
        (n.v_next, 3),
        (n.a_step, 1, 2),
    )
    plan[(At.INPUT, 3)] = (
        (n.a_step, 2, 2),
    )
    plan[(At.END,)] = (
        (n.f_step, 2, 2),
        (n.a_step, 3, 1),
        (n.a_step, 4, 1),
        (n.a_step, 0, 3),
        (n.a_step, 5, 0),
        (n.f_back, 1, 0),
        (n.f_back, 0, 0),
        (n.f_step, 3, 2),
        (n.a_step, 3, 2),
        (n.v_next, 4),
        (n.a_step, 4, 2),
        (n.a_step, 0, 4),
        (n.a_step, 5, 1),
        (n.a_step, 1, 3),
        (n.a_step, 3, 3),
        (n.f_back, 0, 1),
        (n.a_step, 2, 3),
        (n.f_step, 2, 3),
        (n.f_back, 1, 1),
        (n.a_back, 0, 4),
        (n.f_step, 3, 3),
        (n.a_back, 3, 3),
        (n.a_step, 4, 3),
        (n.a_step, 5, 2),
        (n.a_back, 0, 3),
        (n.f_back, 0, 2),
        (n.a_back, 1, 3),
        (n.f_back, 3, 0),
        (n.a_back, 2, 3),
        (n.a_back, 3, 2),
        (n.f_back, 2, 0),
        (n.a_back, 4, 3),
        (n.a_back, 5, 2),
        (n.a_back, 2, 2),
        (n.a_back, 1, 2),
        (n.f_back, 3, 1),
        (n.a_back, 0, 2),
        (n.f_back, 2, 1),
        (n.a_back, 4, 2),
        (n.a_back, 5, 1),
        (n.a_back, 2, 1),
        (n.a_back, 3, 1),
        (n.a_back, 1, 1),
        (n.a_back, 2, 0),
        (n.a_back, 0, 1),
        (n.a_back, 3, 0),
        (n.a_back, 1, 0),
        (n.a_back, 4, 1),
        (n.f_back, 2, 2),
        (n.a_back, 0, 0),
        (n.a_back, 5, 0),
        (n.f_back, 3, 2),
        (n.a_back, 4, 0),
    )
    plan[(At.BRANCH,)] = (
        (n.arrived_near, 1),
        (n.arrived_far, 1),
    )
    return plan


COPIES = 224


def tuned_kernel(names, *refs):
    r = Refs(names, refs)
    base = begin(r, r.x.shape[0])
    sems = r.sems
    for u, (m, start, size, _) in enumerate(UNITS):
        cut = slice(start, start + size)
        r.outs["f", u] = (r.fout.at[m, cut], r.f_out.at[m, cut], sems.at[base + u])
    for n in range(2 + PARTS):
        pair = (r.aout.at[n], r.a_out.at[n]) if n < 2 else (r.qout.at[n - 2], r.q_out.at[n - 2])
        r.outs["a", n] = (*pair, sems.at[base + len(UNITS) + n])
    r.outs["v", 0] = (r.vs.at[5], r.v_out, sems.at[base + len(UNITS) + 2 + PARTS])
    r.fetch("wi", r.wi_hbm, r.wi.at[0], sems.at[base + len(UNITS) + 3 + PARTS])
    r.fetch("wo2", r.wo2_hbm, r.wo2.at[0], sems.at[base + len(UNITS) + 4 + PARTS])
    r.bi[0] = jnp.broadcast_to(r.bias_in[...].astype(f32)[None], r.bi.shape[1:])
    net = Net(r, steps())
    net.enter()
    r.wait("wi", "wo2")
    layer(r, net)
    net.leave()
    r.drain()


def tuned_layer(operands, count, vectors, w_in, bias_in, w_out):
    tokens, width = operands["x_hbm"].shape
    hidden = 4
    part = 2 * width // PARTS
    shape = jax.ShapeDtypeStruct
    vmem = pltpu.VMEM
    ins = {name: (value, ANY) for name, value in operands.items()}
    ins.update(count_ref=(count, IN_SMEM))
    ins.update({name: (value, IN_VMEM) for name, value in vectors.items()})
    ins.update(wi_hbm=(w_in, ANY), wo2_hbm=(w_out, ANY), bias_in=(bias_in, IN_VMEM))
    outs = dict(
        lo_out=shape((tokens, width), bf16),
        dual_out=shape((tokens, width), f32),
        gx_out=shape((tokens, width), f32),
        f_out=shape((2, HALF, width), bf16),
        a_out=shape((2, width, width), bf16),
        q_out=shape((PARTS, width, part), bf16),
        v_out=shape((16, width), f32),
    )
    scratch = scratch_of(tokens, width, hidden)
    scratch.update(
        wi=vmem((hidden, width, HALF), bf16),
        wo2=vmem((hidden, HALF, width), bf16),
        bi=vmem((hidden, 8, HALF), f32),
        gw=vmem((2, width, width), bf16),
        gqk=vmem((PARTS, width, part), bf16),
        gwi=vmem((hidden, width, HALF), bf16),
        gwo2=vmem((hidden, HALF, width), bf16),
        gvec=vmem((8, width), f32),
        gbi=vmem((hidden, 1, HALF), f32),
        rca=vmem((2, HALF, width), bf16),
        rcd=vmem((2, HALF, width), bf16),
        rf=vmem((len(UNITS), max(unit[2] for unit in UNITS) * 15 // 8, width), bf16),
        fout=vmem((2, HALF, width), bf16),
        ra=vmem((2, width * 31 // 32, width), bf16),
        aout=vmem((2, width, width), bf16),
        rq=vmem((PARTS, width * 31 // 32, part), bf16),
        qout=vmem((PARTS, width, part), bf16),
        vs=vmem((6, 16, width), f32),
        vr=vmem((5, 16, width), f32),
        sems=pltpu.SemaphoreType.DMA((len(FETCHED) + 4 + len(UNITS) + 5 + PARTS,)),
        send_sem=pltpu.SemaphoreType.DMA((COPIES,)),
        recv_sem=pltpu.SemaphoreType.DMA((COPIES,)),
    )
    names = list(ins) + list(outs) + list(scratch)
    return pl.pallas_call(
        functools.partial(tuned_kernel, names),
        out_shape=list(outs.values()),
        in_specs=[i[1] for i in ins.values()],
        out_specs=[ANY] * len(outs),
        scratch_shapes=list(scratch.values()),
        compiler_params=pltpu.CompilerParams(
            vmem_limit_bytes=int(63.5 * 2**20), collective_id=0, has_side_effects=True
        ),
        cost_estimate=COST,
    )(*[i[0] for i in ins.values()])


def widen_kernel(lo, dual, gx, f, a, q, v, lo_out, dual_out, gx_out, gq, gk, gv, go, gwi, gwo,
                 gg1, gs1, gbi, gbo, gg2, gs2, f_low, a_low, q_low, lo_held, dual_held, gx_held, wide, sems):
    def copy(source, target, at):
        made = pltpu.make_async_copy(source, target, sems.at[at])
        made.start()
        return made

    low = [copy(*pair, at) for at, pair in enumerate(((f, f_low), (a, a_low), (q, q_low)))]
    moves = []
    for source, held, target in ((dual, dual_held, dual_out), (gx, gx_held, gx_out), (lo, lo_held, lo_out)):
        for at in range(source.shape[0] // BLOCK):
            rows = rows_of(at)
            moves.append((source.at[rows], held.at[rows], target.at[rows]))
    loads = [copy(source, held, 3 + at) for at, (source, held, _) in enumerate(moves)]
    stores = []

    def store(source, target):
        stores.append(copy(source, target, 3 + len(moves) + len(stores)))

    def widened(at, value, target):
        wide[at] = value.astype(f32)
        store(wide.at[at], target)

    for at, out in enumerate((gg1, gs1, gbo, gg2, gs2)):
        out[...] = v[at]
    gbi[...] = v[12]
    low[0].wait()
    widened(0, f_low[0], gwo)
    widened(1, f_low[1], gwi)
    low[1].wait()
    widened(2, a_low[0], go)
    widened(3, a_low[1], gv)
    low[2].wait()
    part = q.shape[2] // 2
    for at, target in ((4, gq), (5, gk)):
        cols = span_of(at - 4, part)
        for p in range(PARTS):
            wide[at, :, p * part : (p + 1) * part] = q_low[p, :, cols].astype(f32)
        store(wide.at[at], target)
    for load, (_, held, target) in zip(loads, moves):
        load.wait()
        store(held, target)
    for made in stores:
        made.wait()


def widen(lo, dual, gx, f, a, q, v):
    width = f.shape[2]
    shape = jax.ShapeDtypeStruct
    matrix = (shape((width, width), f32), ANY)
    vector = (shape((width,), f32), IN_VMEM)
    outs = [(shape(t.shape, t.dtype), ANY) for t in (lo, dual, gx)] + [matrix] * 6 + [vector] * 6
    return pl.pallas_call(
        widen_kernel,
        out_shape=[o[0] for o in outs],
        in_specs=[ANY] * 6 + [IN_VMEM],
        out_specs=[o[1] for o in outs],
        scratch_shapes=[
            pltpu.VMEM(f.shape, bf16),
            pltpu.VMEM(a.shape, bf16),
            pltpu.VMEM(q.shape, bf16),
            *[pltpu.VMEM(t.shape, t.dtype) for t in (lo, dual, gx)],
            pltpu.VMEM((6, width, width), f32),
            pltpu.SemaphoreType.DMA((9 + 6 * (lo.shape[0] // BLOCK),)),
        ],
        compiler_params=pltpu.CompilerParams(vmem_limit_bytes=int(63.5 * 2**20)),
        cost_estimate=pl.CostEstimate(flops=0, bytes_accessed=19 << 20, transcendentals=0),
    )(lo, dual, gx, f, a, q, v)


def tuned_body(*args):
    (lo, dual, gx, gq, gk, gv, go, gwi, gwo, gg1, gs1, gbi, gbo, gg2, gs2) = widen(*tuned_layer(*sort_out(*args)))
    return lo, dual, gx, gq, gk, gv, go, gg1, gs1, gwi, gbi, gwo, gbo, gg2, gs2


def solution(mesh):
    tokens = P(("batch", "wide"), None)
    fits = mesh.shape["batch"] == 8 and mesh.shape["wide"] == 4
    return jax.shard_map(
        tuned_body if fits else plain_body,
        mesh=mesh,
        in_specs=(tokens, tokens, P(("batch", "wide")), P(), P(), P(), P(), P(), P(), P(None, "wide"), P("wide"),
                  P("wide", None), P(), P(), P(), tokens, tokens),
        out_specs=(tokens, tokens, tokens, P(), P(), P(), P(), P(), P(), P(None, "wide"), P("wide"),
                   P("wide", None), P(), P(), P()),
        check_vma=False,
    )
```

```python
import functools

import jax
import jax.numpy as jnp
from jax import lax
from jax.experimental import pallas as pl
from jax.experimental.pallas import tpu as pltpu
from jax.sharding import PartitionSpec as P

HEADS = 8
HEAD_DIM = 64
EPSILON = 1e-05
MASKED = -1000000000.0
BLOCK = 256
HALF = 512
PARTS = 4
PRE_UNROLL = 1
HALF_UNROLL = NORM_UNROLL = SECOND_UNROLL = FIRST_UNROLL = INPUT_UNROLL = 2
CORE, X, Y, NEXT, FAR, ZED, WIDE, BATCH = range(8)
UNITS = (
    (0, 0, 256, (X, Y, NEXT, FAR)),
    (0, 256, 256, (Y, X, ZED)),
    (1, 0, 256, (FAR, Y, NEXT, X)),
    (1, 256, 256, (NEXT, X, Y, FAR)),
)
CHUNKS = (
    (CORE, X, Y, NEXT, FAR),
    (CORE, Y, X, FAR, NEXT),
    (CORE, NEXT, Y, X, FAR),
    (CORE, NEXT, X, FAR, Y),
    (CORE, Y, X, ZED),
    (CORE, X, Y, ZED),
)

bf16 = jnp.bfloat16
f32 = jnp.float32


def contract(left, right, a, b):
    return lax.dot_general(
        left, right, (((a,), (b,)), ((), ())), preferred_element_type=f32
    )


def dot_nn(left, right):
    return contract(left, right, 1, 0)


def dot_nt(left, right):
    return contract(left, right, 1, 1)


def dot_tn(left, right):
    return contract(left, right, 0, 0)


def dot_tt(left, right):
    return contract(left, right, 0, 1)


def span_of(at, size):
    if isinstance(at, int):
        return slice(at * size, (at + 1) * size)
    return pl.ds(pl.multiple_of(at * size, size), size)


def rows_of(block):
    return span_of(block, BLOCK)


def head_of(head):
    return span_of(head, HEAD_DIM)


def split(block):
    return block // 2, span_of(block % 2, BLOCK)


def each(count, step, unroll=1):
    def several(at, _):
        for k in range(unroll):
            step(at * unroll + k)
        return 0

    lax.fori_loop(0, count // unroll, several, 0)


def row_mean(value):
    return jnp.mean(value, axis=-1, keepdims=True)


def col_sum(value):
    return jnp.sum(value, axis=0, keepdims=True)


def joined(value):
    return value.reshape(value.shape[0] * value.shape[1], value.shape[2])


def layer(r, net):
    tokens, width = r.x.shape
    blocks = tokens // BLOCK
    hidden = r.wi.shape[0]
    slots = tuple(range(hidden))

    r.wait("x", "wq", "wk", "wv")
    for block in range(blocks):
        cols = rows_of(block)
        xb = r.x[cols]
        r.qt[:, cols] = (dot_tt(r.wq[...], xb) * HEAD_DIM**-0.5).astype(bf16)
        r.kt[:, cols] = dot_tt(r.wk[...], xb).astype(bf16)
        r.vt[:, cols] = dot_tt(r.wv[...], xb).astype(bf16)
    net.tick(At.PROJECT)

    row_at = lax.broadcasted_iota(jnp.int32, (BLOCK, BLOCK), 0)
    col_at = lax.broadcasted_iota(jnp.int32, (BLOCK, BLOCK), 1)
    causal = row_at <= col_at
    away = jnp.where(r.count > 0, 0.0, 2e9).astype(f32)

    def soften(head, qb):
        hs = head_of(head)
        query = r.qt[hs, rows_of(qb)]
        parts = []
        peak_off = None
        for tb in range(qb + 1):
            scores = dot_tn(r.kt[hs, rows_of(tb)], query)
            if tb == qb:
                scores = jnp.where(causal, scores, MASKED)
            parts.append(scores)
            peak = jnp.max(scores, axis=0, keepdims=True)
            if tb < qb:
                peak_off = peak if peak_off is None else jnp.maximum(peak_off, peak)
        if peak_off is not None:
            peak = jnp.maximum(peak, peak_off - away)
        total = jnp.zeros((1, BLOCK), f32)
        for tb in range(qb + 1):
            expo = jnp.exp(parts[tb] - (peak if tb == qb else peak + away))
            total += jnp.sum(expo, axis=0, keepdims=True)
            r.p[qb][head, rows_of(tb)] = expo.astype(bf16)
        r.inv_total[pl.ds(head, 1), rows_of(qb)] = 1.0 / total

    def mix(head, qb):
        hs = head_of(head)
        mixed = dot_nn(r.vt[hs, : (qb + 1) * BLOCK], r.p[qb][head])
        mixed *= r.inv_total[pl.ds(head, 1), rows_of(qb)]
        r.mt[hs, rows_of(qb)] = mixed.astype(bf16)

    for head in range(HEADS + 1):
        for qb in range(blocks):
            if head < HEADS:
                soften(head, qb)
            if head > 0:
                mix(head - 1, qb)
        net.tick(At.ATTEND, head)

    r.wait("wo", "dual")
    gain_one, shift_one = r.gain_one[...][None], r.shift_one[...][None]

    def norm_block(block):
        rows = rows_of(block)
        attended = dot_tn(r.mt[:, rows], r.wo[...])
        r.dual[rows] += attended
        hidden_one = r.x[rows].astype(f32) + attended
        centre = hidden_one - row_mean(hidden_one)
        inverse = lax.rsqrt(row_mean(centre * centre) + EPSILON)
        normed = centre * inverse
        r.n1[rows] = normed
        r.i1[rows] = inverse
        r.fl[rows] = (normed * gain_one + shift_one).astype(bf16)

    each(blocks, norm_block, NORM_UNROLL)

    def half_block(block, pair, place):
        first_low = r.fl[rows_of(block)]
        th, rows = split(block)
        for j in pair:
            pre = dot_nn(first_low, r.wi[j]) + r.bi[j, 0:1]
            phi = 0.5 + 0.5 * lax.erf(pre * 0.7071067811865476)
            bell = jnp.exp(-0.5 * pre * pre) * 0.3989422804014327
            r.act[j, th, rows] = (pre * phi).astype(bf16)
            r.slope[j, th, rows] = (phi + pre * bell).astype(bf16)
        net.loop_tick(place, block, blocks)

    net.tick(At.HIDDEN)
    each(blocks, lambda block: half_block(block, slots[:2], At.HALVES), HALF_UNROLL)
    net.tick(At.OTHERS)
    each(blocks, lambda block: half_block(block, slots[2:], At.HALVES2), HALF_UNROLL)

    r.wait("cm", "cd")
    net.tick(At.BRANCH)
    gain_two, shift_two = r.gain_two[...][None], r.shift_two[...][None]
    bias_out = r.bias_out[...][None]
    r.gvec[...] = jnp.zeros_like(r.gvec)

    def second_block(block):
        rows = rows_of(block)
        th, cut = split(block)
        branch = dot_nn(r.act[0, th, cut], r.wo2[0])
        for j in slots[1:]:
            branch += dot_nn(r.act[j, th, cut], r.wo2[j])
        branch += bias_out
        r.dual[rows] += branch
        hidden_two = r.n1[rows] * gain_one + shift_one + branch
        centre = hidden_two - row_mean(hidden_two)
        inverse = lax.rsqrt(row_mean(centre * centre) + EPSILON)
        normed = centre * inverse
        r.gwi[th, cut] = (normed * gain_two + shift_two).astype(bf16)
        grad = r.cm[rows]
        r.gvec[3:4] += col_sum(grad * normed)
        r.gvec[4:5] += col_sum(grad)
        scaled = grad * gain_two
        g_sum = inverse * (
            scaled - row_mean(scaled) - normed * row_mean(scaled * normed)
        )
        r.cm[rows] = g_sum
        g_branch = (g_sum + r.cd[rows]).astype(bf16)
        r.gb[rows] = g_branch
        r.gvec[2:3] += col_sum(g_branch.astype(f32))

    each(blocks, second_block, SECOND_UNROLL)
    r.put("lo", 0)
    r.put("lo", 1)
    r.put("dual", 0)

    for j in reversed(slots):
        r.gwo2[j] = dot_tn(joined(r.act[j]), r.gb[...]).astype(bf16)
        net.tick(At.OUT, j)
    r.gbi[...] = jnp.zeros_like(r.gbi)

    def pre_block(block):
        g_branch = r.gb[rows_of(block)]
        th, rows = split(block)
        for j in slots:
            g_act = dot_nt(g_branch, r.wo2[j])
            g_pre = (g_act * r.slope[j, th, rows].astype(f32)).astype(bf16)
            r.slope[j, th, rows] = g_pre
            r.gbi[j] += col_sum(g_pre.astype(f32))
        net.loop_tick(At.PRE, block, blocks)

    each(blocks, pre_block, PRE_UNROLL)
    r.finished("lo")
    for j in reversed(slots):
        r.gwi[j] = dot_tn(r.fl[...], joined(r.slope[j])).astype(bf16)
        net.tick(At.IN, j)

    def first_block(block):
        rows = rows_of(block)
        th, cut = split(block)
        g_first = dot_nt(r.slope[0, th, cut], r.wi[0])
        for j in slots[1:]:
            g_first += dot_nt(r.slope[j, th, cut], r.wi[j])
        g_first += r.cm[rows]
        normed = r.n1[rows]
        r.gvec[0:1] += col_sum(g_first * normed)
        r.gvec[1:2] += col_sum(g_first)
        scaled = g_first * gain_one
        g_resid = r.i1[rows] * (
            scaled - row_mean(scaled) - normed * row_mean(scaled * normed)
        )
        r.cm[rows] = g_resid
        g_att = (g_resid + r.cd[rows]).astype(bf16)
        r.gb[rows] = g_att
        g_mixed = dot_nt(r.wo[...], g_att)
        g_mixed = g_mixed.reshape(HEADS, HEAD_DIM, BLOCK) * r.inv_total[:, rows][:, None]
        g_mixed = g_mixed.reshape(width, BLOCK).astype(bf16)
        r.act[3, th, :, cut] = g_mixed
        centred = g_mixed.astype(f32) * r.mt[:, rows].astype(f32)
        r.centred[:, rows] = jnp.sum(centred.reshape(HEADS, HEAD_DIM, BLOCK), axis=1)
        net.loop_tick(At.FIRST, block, blocks)

    each(blocks, first_block, FIRST_UNROLL)
    r.gw[0] = dot_nn(r.mt[...], r.gb[...]).astype(bf16)
    net.tick(At.W_OUTPUT)
    for th in range(2):
        r.slope[0, th] = r.x[th * HALF : (th + 1) * HALF].T

    def columns(which, head, block):
        th, cut = split(block)
        return which, th, head_of(head), cut

    def back_values(head, tb):
        total = None
        for qb in range(tb, blocks):
            part = dot_nt(r.act[columns(3, head, qb)], r.p[qb][head, rows_of(tb)])
            total = part if total is None else total + part
        r.act[columns(2, head, tb)] = total.astype(bf16)

    def back_scores(head, qb, slot):
        got = r.act[columns(3, head, qb)]
        centred = r.centred[pl.ds(head, 1), rows_of(qb)]
        for tb in range(qb + 1):
            g_probs = dot_tn(r.vt[head_of(head), rows_of(tb)], got)
            probs = r.p[qb][head, rows_of(tb)].astype(f32)
            slot[qb][rows_of(tb)] = (probs * (g_probs - centred)).astype(bf16)

    def back_query(head, qb, slot):
        g_query = dot_nn(r.kt[head_of(head), : (qb + 1) * BLOCK], slot[qb][...])
        r.act[columns(0, head, qb)] = (g_query * HEAD_DIM**-0.5).astype(bf16)

    def back_keys(head, tb, slot):
        total = None
        for qb in range(tb, blocks):
            part = dot_nt(r.qt[head_of(head), rows_of(qb)], slot[qb][rows_of(tb)])
            total = part if total is None else total + part
        r.act[columns(1, head, tb)] = total.astype(bf16)

    def against_x(which, rows):
        total = dot_nt(r.slope[0, 0], r.act[which, 0, rows])
        return (total + dot_nt(r.slope[0, 1], r.act[which, 1, rows])).astype(bf16)

    for head in range(HEADS):
        for tb in range(blocks):
            back_values(head, tb)
        net.tick(At.VALUES, head)
    r.gw[1] = against_x(2, slice(0, width))
    net.tick(At.W_VALUE)
    size = HEADS // PARTS
    part_width = size * HEAD_DIM

    for head in range(HEADS + 1):
        for block in range(blocks):
            if head < HEADS:
                back_scores(head, block, r.gs[head % 2])
            if head > 0:
                back_query(head - 1, block, r.gs[(head - 1) % 2])
                back_keys(head - 1, block, r.gs[(head - 1) % 2])
        if head > 0 and head % size == 0:
            part = head // size - 1
            rows = span_of(part, part_width)
            r.gqk[part, :, :part_width] = against_x(0, rows)
            r.gqk[part, :, part_width:] = against_x(1, rows)
        net.tick(At.SCORES, head)

    def input_block(block):
        rows = rows_of(block)
        th, cut = split(block)
        grad = dot_tt(r.act[0, th, :, cut], r.wq[...])
        grad += dot_tt(r.act[1, th, :, cut], r.wk[...])
        grad += dot_tt(r.act[2, th, :, cut], r.wv[...])
        r.cm[rows] += grad
        net.loop_tick(At.INPUT, block, blocks)

    each(blocks, input_block, INPUT_UNROLL)
    r.put("cm", 0)
    net.tick(At.END)


class Refs:
    def __init__(self, names, refs):
        self.__dict__.update(zip(names, refs))
        self.pending = {}
        self.out = {}

    def fetch(self, name, source, target, sem):
        copy = pltpu.make_async_copy(source, target, sem)
        copy.start()
        self.pending[name] = copy

    def wait(self, *names):
        for name in names:
            self.pending.pop(name).wait()

    def put(self, name, at):
        source, target, sem = self.outs[name, at]
        copy = pltpu.make_async_copy(source, target, sem)
        copy.start()
        self.out[name, at] = copy

    def finished(self, name):
        for key in [key for key in self.out if key[0] == name]:
            self.out.pop(key).wait()

    def drain(self):
        for copy in self.out.values():
            copy.wait()


FETCHED = ("x", "wq", "wk", "wv", "wo", "dual", "cm", "cd")


def scratch_of(tokens, width, hidden):
    vmem = pltpu.VMEM
    wide = (hidden, tokens // HALF, HALF, HALF)
    names = dict(
        x=vmem((tokens, width), bf16),
        wq=vmem((width, width), bf16),
        wk=vmem((width, width), bf16),
        wv=vmem((width, width), bf16),
        wo=vmem((width, width), bf16),
        dual=vmem((tokens, width), f32),
        cm=vmem((tokens, width), f32),
        cd=vmem((tokens, width), f32),
        qt=vmem((width, tokens), bf16),
        kt=vmem((width, tokens), bf16),
        vt=vmem((width, tokens), bf16),
        mt=vmem((width, tokens), bf16),
        inv_total=vmem((HEADS, tokens), f32),
        centred=vmem((HEADS, tokens), f32),
        n1=vmem((tokens, width), f32),
        i1=vmem((tokens, 1), f32),
        fl=vmem((tokens, width), bf16),
        act=vmem(wide, bf16),
        slope=vmem(wide, bf16),
        gb=vmem((tokens, width), bf16),
    )
    for qb in range(tokens // BLOCK):
        names[f"p{qb}"] = vmem((HEADS, (qb + 1) * BLOCK, BLOCK), bf16)
        names[f"g{qb}"] = vmem(((qb + 1) * BLOCK, BLOCK), bf16)
        names[f"h{qb}"] = vmem(((qb + 1) * BLOCK, BLOCK), bf16)
    return names


def begin(r, tokens):
    blocks = tokens // BLOCK
    r.count = r.count_ref[0]
    r.p = [getattr(r, f"p{qb}") for qb in range(blocks)]
    r.gs = [[getattr(r, f"{s}{qb}") for qb in range(blocks)] for s in "gh"]
    for at, name in enumerate(FETCHED):
        r.fetch(name, getattr(r, name + "_hbm"), getattr(r, name), r.sems.at[at])
    base = len(FETCHED)
    r.outs = {
        ("lo", 0): (r.gwi.at[0], r.lo_out.at[0:HALF], r.sems.at[base]),
        ("lo", 1): (r.gwi.at[1], r.lo_out.at[HALF : 2 * HALF], r.sems.at[base + 1]),
        ("dual", 0): (r.dual, r.dual_out, r.sems.at[base + 2]),
        ("cm", 0): (r.cm, r.gx_out, r.sems.at[base + 3]),
    }
    return base + 4


class Quiet:
    def tick(self, *place):
        pass

    def loop_tick(self, place, at, count):
        pass


class At:
    (PROJECT, ATTEND, HIDDEN, HALVES, OTHERS, HALVES2, BRANCH, OUT, PRE, IN, FIRST, W_OUTPUT,
     VALUES, W_VALUE, SCORES, INPUT, END) = range(17)


class Kind:
    (W_X, W_Y, W_CORE, W_PASS, W_TURN, W_BIAS, F_CORE, F_AWAY, F_OWN, F_BACK, A_OUT, A_BACK,
     V_STEP) = range(13)


class Net:
    def __init__(self, r, plan):
        self.r = r
        self.plan = plan
        b, w = lax.axis_index("batch"), lax.axis_index("wide")
        z, y, x, c = b // 2, b % 2, w // 2, w % 2
        self.y, self.x, self.c, self.w = y, x, c, w
        self.core = (b, x * 2 + 1 - c)
        self.ex = (b, (1 - x) * 2 + c)
        self.diagonal = (b, (1 - x) * 2 + 1 - c)
        self.why = (z * 2 + 1 - y, w)
        self.odd, self.high = z % 2, z // 2
        self.next = ((z + 1 - 2 * self.odd) * 2 + y, w)
        self.far = (((z + 2) % 4) * 2 + y, w)
        self.table = {}
        self.used = set()
        def pair(peer, bit):
            return bit, 2, [(peer, 1 - bit)]

        self.axes = (
            pair(self.core, c),
            pair(self.ex, x),
            pair(self.why, y),
            pair(self.next, self.odd),
            pair(self.far, self.high),
            (z, 4, [(((z + k) % 4 * 2 + y, w), (z + k) % 4) for k in (1, 2, 3)]),
            (w, 4, [(to, to[1]) for to in (self.core, self.ex, self.diagonal)]),
            (b, 8, [(((b + k) % 8, w), (b + k) % 8) for k in range(1, 8)]),
        )
        self.units = []
        self.parts = []
        self.describe()

    def copy(self, name, to, source, target):
        self.table[name] = (len(self.table), to, source, target)

    def build(self, name):
        index, to, source, target = self.table[name]
        return pltpu.make_async_remote_copy(
            src_ref=source(),
            dst_ref=target(),
            send_sem=self.r.send_sem.at[index],
            recv_sem=self.r.recv_sem.at[index],
            device_id=to,
            device_id_type=pl.DeviceIdType.MESH,
        )

    def start(self, *names):
        for name in names:
            self.used.add(name)
            self.build(name).start()

    def got(self, *names):
        for name in names:
            self.build(name).wait_recv()

    def tick(self, *place):
        for event, *args in self.plan.get(place, ()):
            event(self, *args)

    def loop_tick(self, place, at, count):
        for k in range(count):
            if self.plan.get((place, k)):
                self.guard(at, k, place)

    def guard(self, at, k, place):
        if isinstance(at, int):
            if at == k:
                self.tick(place, k)
        else:
            pl.when(at == k)(functools.partial(self.tick, place, k))

    def cut(self, base, size, mine, peers):
        keep = lambda: self.span(base() + mine * size, size)
        gives = [lambda at=at: self.span(base() + at * size, size) for _, at in peers]
        return keep, gives, lambda: base() + mine * size

    def group(self, act, *name):
        k = 0
        while (*name, k) in self.table:
            act((*name, k))
            k += 1
        return k

    def span(self, start, size):
        return pl.ds(pl.multiple_of(start, size), size)

    def describe(self):
        r, copy, span = self.r, self.copy, self.span
        own = (r.wi_hbm, r.wo2_hbm)
        held = (r.wi, r.wo2)
        for m in range(2):
            copy((Kind.W_CORE, m), self.core, lambda m=m: own[m], lambda m=m: held[m].at[1])
            for q, (mine, other) in enumerate(self.slices(m)):
                copy((Kind.W_X, m, q), self.ex, lambda m=m, f=mine: own[m].at[f()], lambda m=m, f=mine: held[m].at[2, f()])
                copy((Kind.W_PASS, m, q), self.core, lambda m=m, f=mine: held[m].at[2, f()], lambda m=m, f=mine: held[m].at[3, f()])
                if other is not None:
                    copy((Kind.W_Y, m, q), self.why, lambda m=m, f=mine: held[m].at[2, f()], lambda m=m, f=mine: held[m].at[2, f()])
                    copy((Kind.W_TURN, m, q), self.core, lambda m=m, f=other: held[m].at[2, f()], lambda m=m, f=other: held[m].at[3, f()])
        for slot, to in ((1, self.core), (2, self.ex), (3, self.diagonal)):
            copy((Kind.W_BIAS, slot), to, lambda: r.bi.at[0], lambda slot=slot: r.bi.at[slot])

        for m in range(2):
            for slot in (3, 1):
                received = r.rca if slot == 3 else r.rcd
                copy((Kind.F_CORE, m, slot), self.core, lambda m=m, s=slot: self.grad(m).at[s], lambda m=m, t=received: t.at[m])
        for u, (m, start, size, order) in enumerate(UNITS):
            grad, out = self.grad(m), r.fout.at[m]
            base = lambda f=start: f
            both, offset, levels, back = True, 0, [], []
            for level, axis in enumerate(order):
                mine, parts, peers = self.axes[axis]
                if axis == X:
                    both = False
                    keep = lambda f=base, s=size: span(f(), s)
                    gives = [keep]
                else:
                    size //= parts
                    keep, gives, base = self.cut(base, size, mine, peers)
                    back.append((axis, keep))
                landing = [[], []]
                for k, (to, _) in enumerate(peers):
                    for slot, kind, wanted in ((2, Kind.F_AWAY, both or axis == X), (0, Kind.F_OWN, axis != X)):
                        if wanted:
                            target = r.rf.at[u, offset : offset + size]
                            offset += size
                            landing[slot // 2].append(target)
                            copy((kind, u, level, k), to, lambda g=grad, s=slot, f=gives[k]: g.at[s, f()], lambda t=target: t)
                levels.append((axis, keep, landing))
            for step, (axis, keep) in enumerate(reversed(back)):
                for k, (to, _) in enumerate(self.axes[axis][2]):
                    copy((Kind.F_BACK, u, step, k), to, lambda o=out, f=keep: o.at[f()], lambda o=out, f=keep: o.at[f()])
            self.units.append((m, levels))

        for n in range(2 + PARTS):
            if n < 2:
                grad, received, out = r.gw.at[n], r.ra.at[n], r.aout.at[n]
            else:
                grad, received, out = r.gqk.at[n - 2], r.rq.at[n - 2], r.qout.at[n - 2]
            size = grad.shape[0]
            base = lambda: 0
            offset, levels = 0, []
            for level, axis in enumerate(CHUNKS[n]):
                mine, parts, peers = self.axes[axis]
                size //= parts
                keep, gives, base = self.cut(base, size, mine, peers)
                landing = []
                for k, (to, _) in enumerate(peers):
                    target = received.at[offset : offset + size]
                    offset += size
                    landing.append(target)
                    copy((Kind.A_OUT, n, level, k), to, lambda g=grad, f=gives[k]: g.at[f()], lambda t=target: t)
                    copy((Kind.A_BACK, n, level, k), to, lambda o=out, f=keep: o.at[f()], lambda o=out, f=keep: o.at[f()])
                levels.append((keep, landing))
            self.parts.append((grad, out, levels))

        for at, to in enumerate((self.core, self.ex, self.why, self.next, self.far)):
            copy((Kind.V_STEP, at), to, lambda at=at: r.vs.at[at], lambda at=at: r.vr.at[at])

    def enter(self):
        barrier = pltpu.get_barrier_semaphore()
        peers = [to for axis in (WIDE, BATCH) for to, _ in self.axes[axis][2]]
        for peer in peers:
            pl.semaphore_signal(barrier, inc=1, device_id=peer, device_id_type=pl.DeviceIdType.MESH)
        pl.semaphore_wait(barrier, len(peers))
        for slot in (1, 2, 3):
            self.start((Kind.W_BIAS, slot))
        for m in range(2):
            self.group(self.start, Kind.W_X, m)
        self.start((Kind.W_CORE, 0), (Kind.W_CORE, 1))

    def slices(self, m):
        y = self.y
        if m == 0:
            for q in range(4):
                yield (lambda q=q: self.span(y * 256 + q * 64, 64)), (lambda q=q: self.span((1 - y) * 256 + q * 64, 64))
        else:
            yield (lambda: self.span(y * 256, 128)), (lambda: self.span((1 - y) * 256, 128))
            for row in (128, 384):
                yield (lambda row=row: self.span(row, 128)), None

    def pass_x(self, m, q):
        self.got((Kind.W_X, m, q))
        if (Kind.W_Y, m, q) in self.table:
            self.start((Kind.W_Y, m, q))
        self.start((Kind.W_PASS, m, q))

    def pass_y(self, m, q):
        self.got((Kind.W_Y, m, q))
        self.start((Kind.W_TURN, m, q))

    def arrived_near(self, m):
        if m == 0:
            self.got((Kind.W_BIAS, 1), (Kind.W_BIAS, 2), (Kind.W_BIAS, 3))
        self.got((Kind.W_CORE, m))

    def arrived_far(self, m):
        self.group(self.got, Kind.W_PASS, m)
        self.group(self.got, Kind.W_TURN, m)

    def grad(self, m):
        return (self.r.gwo2, self.r.gwi)[m]

    def f_core(self, m, slot):
        self.start((Kind.F_CORE, m, slot))

    def f_begin(self, kind, m):
        for u, unit in enumerate(self.units):
            if unit[0] == m:
                self.group(self.start, kind, u, 0)

    def f_x(self, m):
        self.got((Kind.F_CORE, m, 3))
        grad = self.grad(m)
        grad[2] = grad[2] + self.r.rca[m]
        self.f_begin(Kind.F_AWAY, m)

    def f_near(self, m):
        self.got((Kind.F_CORE, m, 1))
        grad = self.grad(m)
        grad[0] = grad[0] + self.r.rcd[m]
        self.f_begin(Kind.F_OWN, m)

    def plus(self, total, landing):
        if len(landing) == 1:
            return total + landing[0][...]
        total = total.astype(f32)
        for part in landing:
            total += part[...].astype(f32)
        return total.astype(bf16)

    def f_step(self, u, level):
        m, levels = self.units[u]
        grad = self.grad(m)
        axis, keep, (landing_own, landing_away) = levels[level]
        s = keep()
        if landing_away:
            self.group(self.got, Kind.F_AWAY, u, level)
            if axis != X:
                grad[2, s] = self.plus(grad[2, s], landing_away)
        if landing_own:
            self.group(self.got, Kind.F_OWN, u, level)
        total = self.plus(grad[0, s], landing_away if axis == X else landing_own)
        if level == len(levels) - 1:
            self.r.fout[m, s] = total
            self.group(self.start, Kind.F_BACK, u, 0)
        else:
            grad[0, s] = total
            self.group(self.start, Kind.F_AWAY, u, level + 1)
            self.group(self.start, Kind.F_OWN, u, level + 1)

    def f_back(self, u, step):
        self.group(self.got, Kind.F_BACK, u, step)
        if not self.group(self.start, Kind.F_BACK, u, step + 1):
            self.r.put("f", u)

    def a_core(self, n):
        self.group(self.start, Kind.A_OUT, n, 0)

    def a_step(self, n, level):
        grad, out, levels = self.parts[n]
        self.group(self.got, Kind.A_OUT, n, level)
        keep, landing = levels[level]
        s = keep()
        total = self.plus(grad[s], landing)
        if level + 1 < len(levels):
            grad[s] = total
            self.group(self.start, Kind.A_OUT, n, level + 1)
        else:
            out[s] = total
            self.group(self.start, Kind.A_BACK, n, level)

    def a_back(self, n, level):
        self.group(self.got, Kind.A_BACK, n, level)
        if level:
            self.group(self.start, Kind.A_BACK, n, level - 1)
        else:
            self.r.put("a", n)

    def v_core(self):
        r = self.r
        x, c = self.x, self.c
        r.vs[0, 0:8] = r.gvec[...]
        r.vs[0, pl.ds(8 + x * 2 + c, 1)] = r.gbi[0]
        r.vs[0, pl.ds(8 + x * 2 + 1 - c, 1)] = r.gbi[1]
        r.vs[0, pl.ds(8 + (1 - x) * 2 + c, 1)] = r.gbi[2]
        r.vs[0, pl.ds(8 + (1 - x) * 2 + 1 - c, 1)] = r.gbi[3]
        self.start((Kind.V_STEP, 0))

    def v_next(self, at):
        r = self.r
        self.got((Kind.V_STEP, at))
        r.vs[at + 1] = r.vs[at] + r.vr[at]
        if at < 4:
            self.start((Kind.V_STEP, at + 1))
        else:
            r.vs[5, 12:13] = r.vs[5, pl.ds(8 + self.w, 1)]
            r.put("v", 0)

    def leave(self):
        for name in self.table:
            if name in self.used:
                self.build(name).wait_send()


def plain_kernel(names, *refs):
    r = Refs(names, refs)
    begin(r, r.x.shape[0])
    layer(r, Quiet())
    r.drain()


ANY = pl.BlockSpec(memory_space=pl.ANY)
IN_VMEM = pl.BlockSpec(memory_space=pltpu.VMEM)
IN_SMEM = pl.BlockSpec(memory_space=pltpu.SMEM)
COST = pl.CostEstimate(
    flops=25 * 10**9, bytes_accessed=30 << 20, transcendentals=12 << 20
)


def plain_layer(operands, count, vectors, wi, bi, wo2):
    tokens, width = operands["x_hbm"].shape
    hidden = wi.shape[0]
    shape = jax.ShapeDtypeStruct
    ins = {name: (value, ANY) for name, value in operands.items()}
    ins.update(count_ref=(count, IN_SMEM))
    ins.update({name: (value, IN_VMEM) for name, value in vectors.items()})
    ins.update(wi=(wi, IN_VMEM), bi=(bi, IN_VMEM), wo2=(wo2, IN_VMEM))
    outs = dict(
        lo_out=(shape((tokens, width), bf16), ANY),
        dual_out=(shape((tokens, width), f32), ANY),
        gx_out=(shape((tokens, width), f32), ANY),
        gw=(shape((2, width, width), bf16), IN_VMEM),
        gqk=(shape((PARTS, width, 2 * width // PARTS), bf16), IN_VMEM),
        gwi=(shape((hidden, width, HALF), bf16), IN_VMEM),
        gwo2=(shape((hidden, HALF, width), bf16), IN_VMEM),
        gvec=(shape((8, width), f32), IN_VMEM),
        gbi=(shape((hidden, 1, HALF), f32), IN_VMEM),
    )
    scratch = scratch_of(tokens, width, hidden)
    scratch["sems"] = pltpu.SemaphoreType.DMA((len(FETCHED) + 4,))
    names = list(ins) + list(outs) + list(scratch)
    return pl.pallas_call(
        functools.partial(plain_kernel, names),
        out_shape=[o[0] for o in outs.values()],
        in_specs=[i[1] for i in ins.values()],
        out_specs=[o[1] for o in outs.values()],
        scratch_shapes=list(scratch.values()),
        compiler_params=pltpu.CompilerParams(vmem_limit_bytes=62 << 20),
        cost_estimate=COST,
    )(*[i[0] for i in ins.values()])


def sort_out(layer_in, dual_in, long_count, w_query, w_key, w_value, w_output, gain_one, shift_one,
             w_in, bias_in, w_out, bias_out, gain_two, shift_two, cot_main, cot_dual):
    operands = dict(
        x_hbm=layer_in, wq_hbm=w_query, wk_hbm=w_key, wv_hbm=w_value, wo_hbm=w_output,
        dual_hbm=dual_in, cm_hbm=cot_main, cd_hbm=cot_dual,
    )
    vectors = dict(
        gain_one=gain_one, shift_one=shift_one, gain_two=gain_two, shift_two=shift_two, bias_out=bias_out
    )
    return operands, long_count, vectors, w_in, bias_in, w_out


def plain_body(*args):
    operands, count, vectors, w_in, bias_in, w_out = sort_out(*args)
    width = w_in.shape[0]
    w_in_all = lax.all_gather(w_in, "wide", axis=1, tiled=True)
    bias_all = lax.all_gather(bias_in, "wide", axis=0, tiled=True)
    w_out_all = lax.all_gather(w_out, "wide", axis=0, tiled=True)
    hidden = w_in_all.shape[1] // HALF
    wi = w_in_all.reshape(width, hidden, HALF).transpose(1, 0, 2)
    wo2 = w_out_all.reshape(hidden, HALF, width)
    bi = bias_all.astype(f32).reshape(hidden, 1, HALF)
    lo, dual, gx, gw, gqk, gwi, gwo2, gvec, gbi = plain_layer(operands, count, vectors, wi, bi, wo2)
    gwi = gwi.transpose(1, 0, 2).reshape(w_in_all.shape)
    gwo2 = gwo2.reshape(w_out_all.shape)
    gwi = lax.psum(lax.psum_scatter(gwi, "wide", scatter_dimension=1, tiled=True), "batch")
    gwo2 = lax.psum(lax.psum_scatter(gwo2, "wide", scatter_dimension=0, tiled=True), "batch")
    gbi = lax.psum_scatter(gbi.reshape(-1), "wide", scatter_dimension=0, tiled=True)
    gbi = lax.psum(gbi, "batch")
    gw, gqk, gvec = lax.psum((gw, gqk, gvec), ("batch", "wide"))
    gw, gqk = gw.astype(f32), gqk.astype(f32)
    part = width // PARTS
    gq = jnp.concatenate(list(gqk[:, :, :part]), axis=1)
    gk = jnp.concatenate(list(gqk[:, :, part:]), axis=1)
    return (lo, dual, gx, gq, gk, gw[1], gw[0], gvec[0], gvec[1], gwi.astype(f32), gbi,
            gwo2.astype(f32), gvec[2], gvec[3], gvec[4])


def steps():
    n = Net
    plan = {}
    plan[(At.ATTEND, 0)] = (
        (n.pass_x, 0, 0),
    )
    plan[(At.ATTEND, 3)] = (
        (n.pass_x, 0, 1),
    )
    plan[(At.ATTEND, 5)] = (
        (n.pass_x, 0, 2),
    )
    plan[(At.ATTEND, 7)] = (
        (n.pass_x, 0, 3),
    )
    plan[(At.ATTEND, 8)] = (
        (n.pass_y, 0, 0),
    )
    plan[(At.HIDDEN,)] = (
        (n.pass_y, 0, 1),
        (n.pass_x, 1, 0),
        (n.arrived_near, 0),
    )
    plan[(At.HALVES, 3)] = (
        (n.pass_y, 0, 2),
    )
    plan[(At.OTHERS,)] = (
        (n.pass_y, 0, 3),
        (n.pass_x, 1, 1),
        (n.pass_x, 1, 2),
        (n.arrived_far, 0),
    )
    plan[(At.HALVES2, 1)] = (
        (n.pass_y, 1, 0),
    )
    plan[(At.OUT, 3)] = (
        (n.f_core, 0, 3),
    )
    plan[(At.OUT, 1)] = (
        (n.f_core, 0, 1),
    )
    plan[(At.PRE, 2)] = (
        (n.f_x, 0),
    )
    plan[(At.PRE, 3)] = (
        (n.f_near, 0),
    )
    plan[(At.IN, 3)] = (
        (n.f_core, 1, 3),
    )
    plan[(At.IN, 1)] = (
        (n.f_core, 1, 1),
    )
    plan[(At.FIRST, 1)] = (
        (n.f_x, 1),
    )
    plan[(At.FIRST, 3)] = (
        (n.f_near, 1),
    )
    plan[(At.W_OUTPUT,)] = (
        (n.v_core,),
        (n.a_core, 0),
        (n.f_step, 0, 0),
        (n.f_step, 1, 0),
    )
    plan[(At.VALUES, 5)] = (
        (n.v_next, 0),
    )
    plan[(At.VALUES, 7)] = (
        (n.a_step, 0, 0),
    )
    plan[(At.W_VALUE,)] = (
        (n.a_core, 1),
    )
    plan[(At.SCORES, 1)] = (
        (n.f_step, 0, 1),
        (n.f_step, 1, 1),
    )
    plan[(At.SCORES, 2)] = (
        (n.a_step, 1, 0),
        (n.a_core, 2),
        (n.v_next, 1),
    )
    plan[(At.SCORES, 4)] = (
        (n.a_core, 3),
        (n.a_step, 0, 1),
        (n.f_step, 3, 0),
        (n.a_step, 2, 0),
        (n.f_step, 2, 0),
    )
    plan[(At.SCORES, 5)] = (
        (n.f_step, 0, 2),
    )
    plan[(At.SCORES, 6)] = (
        (n.a_core, 4),
        (n.a_step, 3, 0),
        (n.a_step, 1, 1),
    )
    plan[(At.SCORES, 7)] = (
        (n.f_step, 1, 2),
        (n.v_next, 2),
        (n.a_step, 2, 1),
        (n.a_step, 0, 2),
    )
    plan[(At.SCORES, 8)] = (
        (n.a_core, 5),
        (n.a_step, 4, 0),
        (n.f_step, 3, 1),
    )
    plan[(At.INPUT, 1)] = (
        (n.a_step, 1, 2),
        (n.f_step, 2, 1),
        (n.a_step, 3, 1),
        (n.f_step, 0, 3),
    )
    plan[(At.INPUT, 3)] = (
        (n.a_step, 5, 0),
        (n.a_step, 2, 2),
    )
    plan[(At.END,)] = (
        (n.v_next, 3),
        (n.a_step, 4, 1),
        (n.a_step, 0, 3),
        (n.f_back, 1, 0),
        (n.a_step, 3, 2),
        (n.f_step, 3, 2),
        (n.f_step, 2, 2),
        (n.a_step, 1, 3),
        (n.a_step, 5, 1),
        (n.f_back, 0, 0),
        (n.a_step, 2, 3),
        (n.a_step, 4, 2),
        (n.v_next, 4),
        (n.a_step, 1, 4),
        (n.f_step, 2, 3),
        (n.a_step, 0, 4),
        (n.a_step, 3, 3),
        (n.f_back, 1, 1),
        (n.a_step, 5, 2),
        (n.f_back, 0, 1),
        (n.f_step, 3, 3),
        (n.a_step, 2, 4),
        (n.a_back, 1, 4),
        (n.a_step, 3, 4),
        (n.f_back, 2, 0),
        (n.a_step, 4, 3),
        (n.a_back, 0, 4),
        (n.a_step, 5, 3),
        (n.f_back, 3, 0),
        (n.a_back, 2, 4),
        (n.f_back, 0, 2),
        (n.a_back, 3, 4),
        (n.a_back, 0, 3),
        (n.a_back, 1, 3),
        (n.f_back, 2, 1),
        (n.a_back, 2, 3),
        (n.a_back, 4, 3),
        (n.f_back, 3, 1),
        (n.a_back, 3, 3),
        (n.a_back, 5, 3),
        (n.a_back, 0, 2),
        (n.a_back, 1, 2),
        (n.a_back, 2, 2),
        (n.a_back, 4, 2),
        (n.a_back, 3, 2),
        (n.a_back, 5, 2),
        (n.f_back, 3, 2),
        (n.a_back, 0, 1),
        (n.f_back, 2, 2),
        (n.a_back, 1, 1),
        (n.a_back, 2, 1),
        (n.a_back, 5, 1),
        (n.a_back, 4, 1),
        (n.a_back, 3, 1),
        (n.a_back, 0, 0),
        (n.a_back, 1, 0),
        (n.a_back, 2, 0),
        (n.a_back, 5, 0),
        (n.a_back, 4, 0),
        (n.a_back, 3, 0),
    )
    plan[(At.BRANCH,)] = (
        (n.arrived_near, 1),
        (n.arrived_far, 1),
    )
    return plan


COPIES = 224


def tuned_kernel(names, *refs):
    r = Refs(names, refs)
    base = begin(r, r.x.shape[0])
    sems = r.sems
    for u, (m, start, size, _) in enumerate(UNITS):
        cut = slice(start, start + size)
        r.outs["f", u] = (r.fout.at[m, cut], r.f_out.at[m, cut], sems.at[base + u])
    for n in range(2 + PARTS):
        pair = (r.aout.at[n], r.a_out.at[n]) if n < 2 else (r.qout.at[n - 2], r.q_out.at[n - 2])
        r.outs["a", n] = (*pair, sems.at[base + len(UNITS) + n])
    r.outs["v", 0] = (r.vs.at[5], r.v_out, sems.at[base + len(UNITS) + 2 + PARTS])
    r.fetch("wi", r.wi_hbm, r.wi.at[0], sems.at[base + len(UNITS) + 3 + PARTS])
    r.fetch("wo2", r.wo2_hbm, r.wo2.at[0], sems.at[base + len(UNITS) + 4 + PARTS])
    r.bi[0] = jnp.broadcast_to(r.bias_in[...].astype(f32)[None], r.bi.shape[1:])
    net = Net(r, steps())
    net.enter()
    r.wait("wi", "wo2")
    layer(r, net)
    net.leave()
    r.drain()


def tuned_layer(operands, count, vectors, w_in, bias_in, w_out):
    tokens, width = operands["x_hbm"].shape
    hidden = 4
    part = 2 * width // PARTS
    shape = jax.ShapeDtypeStruct
    vmem = pltpu.VMEM
    ins = {name: (value, ANY) for name, value in operands.items()}
    ins.update(count_ref=(count, IN_SMEM))
    ins.update({name: (value, IN_VMEM) for name, value in vectors.items()})
    ins.update(wi_hbm=(w_in, ANY), wo2_hbm=(w_out, ANY), bias_in=(bias_in, IN_VMEM))
    outs = dict(
        lo_out=shape((tokens, width), bf16),
        dual_out=shape((tokens, width), f32),
        gx_out=shape((tokens, width), f32),
        f_out=shape((2, HALF, width), bf16),
        a_out=shape((2, width, width), bf16),
        q_out=shape((PARTS, width, part), bf16),
        v_out=shape((16, width), f32),
    )
    scratch = scratch_of(tokens, width, hidden)
    scratch.update(
        wi=vmem((hidden, width, HALF), bf16),
        wo2=vmem((hidden, HALF, width), bf16),
        bi=vmem((hidden, 8, HALF), f32),
        gw=vmem((2, width, width), bf16),
        gqk=vmem((PARTS, width, part), bf16),
        gwi=vmem((hidden, width, HALF), bf16),
        gwo2=vmem((hidden, HALF, width), bf16),
        gvec=vmem((8, width), f32),
        gbi=vmem((hidden, 1, HALF), f32),
        rca=vmem((2, HALF, width), bf16),
        rcd=vmem((2, HALF, width), bf16),
        rf=vmem((len(UNITS), max(unit[2] for unit in UNITS) * 15 // 8, width), bf16),
        fout=vmem((2, HALF, width), bf16),
        ra=vmem((2, width * 31 // 32, width), bf16),
        aout=vmem((2, width, width), bf16),
        rq=vmem((PARTS, width * 31 // 32, part), bf16),
        qout=vmem((PARTS, width, part), bf16),
        vs=vmem((6, 16, width), f32),
        vr=vmem((5, 16, width), f32),
        sems=pltpu.SemaphoreType.DMA((len(FETCHED) + 4 + len(UNITS) + 5 + PARTS,)),
        send_sem=pltpu.SemaphoreType.DMA((COPIES,)),
        recv_sem=pltpu.SemaphoreType.DMA((COPIES,)),
    )
    names = list(ins) + list(outs) + list(scratch)
    return pl.pallas_call(
        functools.partial(tuned_kernel, names),
        out_shape=list(outs.values()),
        in_specs=[i[1] for i in ins.values()],
        out_specs=[ANY] * len(outs),
        scratch_shapes=list(scratch.values()),
        compiler_params=pltpu.CompilerParams(
            vmem_limit_bytes=int(63.5 * 2**20), collective_id=0, has_side_effects=True
        ),
        cost_estimate=COST,
    )(*[i[0] for i in ins.values()])


def widen_kernel(lo, dual, gx, f, a, q, v, lo_out, dual_out, gx_out, gq, gk, gv, go, gwi, gwo,
                 gg1, gs1, gbi, gbo, gg2, gs2, f_low, a_low, q_low, lo_held, dual_held, gx_held, wide, sems):
    def copy(source, target, at):
        made = pltpu.make_async_copy(source, target, sems.at[at])
        made.start()
        return made

    low = [copy(*pair, at) for at, pair in enumerate(((f, f_low), (a, a_low), (q, q_low)))]
    moves = []
    for source, held, target in ((dual, dual_held, dual_out), (gx, gx_held, gx_out), (lo, lo_held, lo_out)):
        for at in range(source.shape[0] // BLOCK):
            rows = rows_of(at)
            moves.append((source.at[rows], held.at[rows], target.at[rows]))
    loads = [copy(source, held, 3 + at) for at, (source, held, _) in enumerate(moves)]
    stores = []

    def store(source, target):
        stores.append(copy(source, target, 3 + len(moves) + len(stores)))

    def widened(at, value, target):
        wide[at] = value.astype(f32)
        store(wide.at[at], target)

    for at, out in enumerate((gg1, gs1, gbo, gg2, gs2)):
        out[...] = v[at]
    gbi[...] = v[12]
    low[0].wait()
    widened(0, f_low[0], gwo)
    widened(1, f_low[1], gwi)
    low[1].wait()
    widened(2, a_low[0], go)
    widened(3, a_low[1], gv)
    low[2].wait()
    part = q.shape[2] // 2
    for at, target in ((4, gq), (5, gk)):
        cols = span_of(at - 4, part)
        for p in range(PARTS):
            wide[at, :, p * part : (p + 1) * part] = q_low[p, :, cols].astype(f32)
        store(wide.at[at], target)
    for load, (_, held, target) in zip(loads, moves):
        load.wait()
        store(held, target)
    for made in stores:
        made.wait()


def widen(lo, dual, gx, f, a, q, v):
    width = f.shape[2]
    shape = jax.ShapeDtypeStruct
    matrix = (shape((width, width), f32), ANY)
    vector = (shape((width,), f32), IN_VMEM)
    outs = [(shape(t.shape, t.dtype), ANY) for t in (lo, dual, gx)] + [matrix] * 6 + [vector] * 6
    return pl.pallas_call(
        widen_kernel,
        out_shape=[o[0] for o in outs],
        in_specs=[ANY] * 6 + [IN_VMEM],
        out_specs=[o[1] for o in outs],
        scratch_shapes=[
            pltpu.VMEM(f.shape, bf16),
            pltpu.VMEM(a.shape, bf16),
            pltpu.VMEM(q.shape, bf16),
            *[pltpu.VMEM(t.shape, t.dtype) for t in (lo, dual, gx)],
            pltpu.VMEM((6, width, width), f32),
            pltpu.SemaphoreType.DMA((9 + 6 * (lo.shape[0] // BLOCK),)),
        ],
        compiler_params=pltpu.CompilerParams(vmem_limit_bytes=int(63.5 * 2**20)),
        cost_estimate=pl.CostEstimate(flops=0, bytes_accessed=19 << 20, transcendentals=0),
    )(lo, dual, gx, f, a, q, v)


def tuned_body(*args):
    (lo, dual, gx, gq, gk, gv, go, gwi, gwo, gg1, gs1, gbi, gbo, gg2, gs2) = widen(*tuned_layer(*sort_out(*args)))
    return lo, dual, gx, gq, gk, gv, go, gg1, gs1, gwi, gbi, gwo, gbo, gg2, gs2


def solution(mesh):
    tokens = P(("batch", "wide"), None)
    fits = mesh.shape["batch"] == 8 and mesh.shape["wide"] == 4
    return jax.shard_map(
        tuned_body if fits else plain_body,
        mesh=mesh,
        in_specs=(tokens, tokens, P(("batch", "wide")), P(), P(), P(), P(), P(), P(), P(None, "wide"), P("wide"),
                  P("wide", None), P(), P(), P(), tokens, tokens),
        out_specs=(tokens, tokens, tokens, P(), P(), P(), P(), P(), P(), P(None, "wide"), P("wide"),
                   P("wide", None), P(), P(), P()),
        check_vma=False,
    )
```
